128 devices in a mesh: row: 8 (over y, z_lo), col: 16 (over z_hi, x, core).
Axes of the slice: x: 4, y: 4, z: 4 (z_hi: 2, z_lo: 2; z = z_hi * 2 + z_lo), core: 2. Of those that a mesh axis runs over, the one named last changes fastest.
Arguments:
- object_field: float32 [2, 4096, 8192], P(None, 'row', 'col'), may hold values from -6 to 6
- probe_field: float32 [2, 128, 128], replicated, may hold values from -1 to 1
- amplitudes: float32 [192, 128, 2048], P('row', None, 'col'), may hold values from 0 to 2
- positions: int32 [8, 16, 2, 24], P('row', 'col'), may hold values from -32 to 416
- counts: int32 [8, 16], P('row', 'col'), may hold values from 8 to 24, as said below
Outputs:
- estimate: float32 [2, 4096, 8192], P(None, 'row', 'col')
- correction: float32 [2, 4096, 8192], P(None, 'row', 'col')
The draws below stay inside these ranges and needn't reach their ends.
Inputs may be any that keep to these rules, and one draw needn't show every extreme that they name: `counts`: between 8 and 24 live slots per tile; some tile has exactly 24 and some exactly 8; slots at or beyond a tile's count carry data that is not used.
All inputs are finite; a program needn't handle non-finite values.
Results may differ from the reference program's by a relative error of at most 0.0001.
Values sent between devices are 32-bit elements; how exact they have to be, the bound alone decides.
A program may use at most 128 MiB of HBM per device.

```python
import jax
import jax.numpy as jnp
from jax import lax

TILE = 512
PROBE = 128
BORDER = 32
PMAX = 24
PMIN = 8
ITERS = 2
TILE_ROWS = 8
TILE_COLS = 16
HEIGHT = 4096
WIDTH = 8192


def draw_counts(key, part):
    key_first, key_second, key_full, key_light = jax.random.split(key, 4)
    device_total = TILE_ROWS * TILE_COLS
    spread = PMAX - PMIN
    first_draw = jax.random.randint(key_first, (device_total,), 0, spread + 1)
    second_draw = jax.random.randint(key_second, (device_total,), 0, spread + 1)
    counts_flat = PMIN + first_draw * second_draw // spread
    fullest = jax.random.randint(key_full, (), 0, device_total)
    lightest = (fullest + 1 + jax.random.randint(key_light, (), 0, device_total - 1)) % device_total
    counts_flat = counts_flat.at[fullest].set(PMAX).at[lightest].set(PMIN)
    return counts_flat.reshape(TILE_ROWS, TILE_COLS).astype(jnp.int32)


def touch_ends(array, key, least, high):
    longest = array.shape.index(max(array.shape))
    spots = []
    for shift in (0, 1):
        where = [jax.random.randint(jax.random.fold_in(key, axis), (), 0, length) for axis, length in enumerate(array.shape)]
        where[longest] = (where[longest] + shift) % array.shape[longest]
        spots.append(tuple(where))
    return array.at[spots[0]].set(least).at[spots[1]].set(high)


def level_of(key, shape, pieces, low, high):
    gain, own = 1.0, jax.random.fold_in(key, 6)
    for dim, shards_of in pieces:
        heights = jnp.exp(jax.random.uniform(jax.random.fold_in(own, dim), (shards_of,), jnp.float32, low / len(pieces), high / len(pieces)))
        gain = gain * jnp.repeat(heights, shape[dim] // shards_of).reshape([-1 if axis == dim else 1 for axis in range(len(shape))])
    return gain


def centred(own_key, extent, scale, bound, pieces=(), held_as=jnp.bfloat16):
    array = jax.random.normal(own_key, extent, jnp.float32) * scale
    if len(pieces) > 0:
        array = level_of(own_key, extent, pieces, -0.22, 0.18) * array
    return jnp.clip(array, min=-bound, max=bound).astype(held_as)


def setup_inputs(seed: int = 0) -> dict:
    splits = jax.random.split(jax.random.key(seed), 6)
    return {
        "object_field": centred(splits[0], (2, HEIGHT, WIDTH), 1.0, 6.0, ((1, 8), (2, 16)), jnp.float32),
        "probe_field": jnp.clip(jax.random.uniform(splits[1], (2, PROBE, PROBE), jnp.float32, -1.0, 1.0), -1.0, 1.0),
        "amplitudes": jnp.clip(2.0 * jax.random.uniform(splits[2], (TILE_ROWS * PMAX, PROBE, TILE_COLS * PROBE), jnp.float32) ** level_of(splits[2], (TILE_ROWS * PMAX, PROBE, TILE_COLS * PROBE), ((0, 8), (2, 16)), -0.2, 0.2), 0.0, 2.0),
        "positions": touch_ends(jax.random.randint(splits[3], (TILE_ROWS, TILE_COLS, 2, PMAX), -BORDER, TILE - PROBE + BORDER + 1), jax.random.fold_in(splits[3], 1), -BORDER, TILE - PROBE + BORDER).astype(jnp.int32),
        "counts": draw_counts(jax.random.fold_in(splits[5], 71), 0),
    }


smoothing = 0.5
step_gain = 0.5
highest = lax.Precision.HIGHEST

def dft_tables(length):
    counter = jnp.arange(length, dtype=jnp.int32)
    product = counter[:, None] * counter[None, :] % length
    angles = 2.0 * jnp.pi / length * product.astype(jnp.float32)
    factor = 1.0 / jnp.sqrt(jnp.float32(length))
    return (jnp.cos(angles) * factor, -jnp.sin(angles) * factor)

def transform(real_part, imag_part, table_real, table_imag):
    left_real = jnp.einsum('kp,spq->skq', table_real, real_part, precision=highest) - jnp.einsum('kp,spq->skq', table_imag, imag_part, precision=highest)
    left_imag = jnp.einsum('kp,spq->skq', table_real, imag_part, precision=highest) + jnp.einsum('kp,spq->skq', table_imag, real_part, precision=highest)
    right_real = jnp.einsum('spq,qk->spk', left_real, table_real, precision=highest) - jnp.einsum('spq,qk->spk', left_imag, table_imag, precision=highest)
    right_imag = jnp.einsum('spq,qk->spk', left_real, table_imag, precision=highest) + jnp.einsum('spq,qk->spk', left_imag, table_real, precision=highest)
    return (right_real, right_imag)

def probe_gradient(patch_real, patch_imag, probe_field, amplitude, table_real, table_imag):
    probe_real = probe_field[0]
    probe_imag = probe_field[1]
    exit_real = probe_real * patch_real - probe_imag * patch_imag
    exit_imag = probe_real * patch_imag + probe_imag * patch_real
    wave_real, wave_imag = transform(exit_real, exit_imag, table_real, table_imag)
    modulus = jnp.sqrt(wave_real * wave_real + wave_imag * wave_imag + smoothing)
    shrink = amplitude / modulus - 1.0
    back_real, back_imag = transform(wave_real * shrink, wave_imag * shrink, table_real, -table_imag)
    grad_real = probe_real * back_real + probe_imag * back_imag
    grad_imag = probe_real * back_imag - probe_imag * back_real
    return (grad_real, grad_imag)

def reference(object_field, probe_field, amplitudes, positions, counts):
    table_real, table_imag = dft_tables(PROBE)
    step_rate = step_gain / (jnp.max(probe_field[0] * probe_field[0] + probe_field[1] * probe_field[1]) + 1e-06)
    row_base = jnp.arange(TILE_ROWS, dtype=jnp.int32)[:, None, None] * TILE
    col_base = jnp.arange(TILE_COLS, dtype=jnp.int32)[None, :, None] * TILE
    row_start = (positions[:, :, 0, :] + row_base + BORDER).astype(jnp.int32)
    col_start = (positions[:, :, 1, :] + col_base + BORDER).astype(jnp.int32)
    slot_ids = jnp.arange(PMAX, dtype=jnp.int32)[None, None, :]
    live_mask = (slot_ids < counts[:, :, None]).astype(jnp.float32)
    measured = amplitudes.reshape(TILE_ROWS, PMAX, PROBE, TILE_COLS, PROBE).transpose(0, 3, 1, 2, 4)
    zero_index = jnp.zeros((), jnp.int32)
    correction = jnp.zeros_like(object_field)
    for iteration in range(ITERS):
        padded = jnp.pad(object_field + correction, ((0, 0), (BORDER, BORDER), (BORDER, BORDER)))

        def cut_patch(start_row, start_col):
            return lax.dynamic_slice(padded, (zero_index, start_row, start_col), (2, PROBE, PROBE))

        def row_block(gradient_sum, block_items):
            block_rows, block_cols, block_mask, block_measured = block_items
            block_rows = block_rows.reshape(-1)
            block_cols = block_cols.reshape(-1)
            block_mask = block_mask.reshape(-1, 1, 1)
            block_measured = block_measured.reshape(-1, PROBE, PROBE)
            patches = jax.vmap(cut_patch)(block_rows, block_cols)
            grad_real, grad_imag = probe_gradient(patches[:, 0], patches[:, 1], probe_field, block_measured, table_real, table_imag)
            gradient = jnp.stack([grad_real * block_mask, grad_imag * block_mask], axis=1)

            def accumulate(slot_index, running):
                corner = (zero_index, block_rows[slot_index], block_cols[slot_index])
                current = lax.dynamic_slice(running, corner, (2, PROBE, PROBE))
                return lax.dynamic_update_slice(running, current + gradient[slot_index], corner)
            return (lax.fori_loop(0, gradient.shape[0], accumulate, gradient_sum), None)
        gradient_sum, unused = lax.scan(row_block, jnp.zeros_like(padded), (row_start, col_start, live_mask, measured))
        correction = correction + step_rate * gradient_sum[:, BORDER:BORDER + HEIGHT, BORDER:BORDER + WIDTH]
    return (object_field + correction, correction)
```

```python
import functools

import jax
import jax.numpy as jnp
import ml_dtypes
import numpy as np
from jax import lax
from jax.experimental import pallas as pl
from jax.experimental.pallas import tpu as pltpu
from jax.sharding import PartitionSpec as P

BORDER = 32
PROBE = 128
TILE = 512
ROWS = TILE + 2 * BORDER
BLOCKS = 6
GROUP = 8
smoothing = 0.5
step_gain = 0.5
f32 = jnp.float32
bf16 = jnp.bfloat16
MESH = pl.DeviceIdType.MESH

DIRS = ((-1, 0), (1, 0), (0, -1), (0, 1), (-1, -1), (-1, 1), (1, -1), (1, 1))
OPP = (1, 0, 3, 2, 7, 6, 5, 4)


def tables():
    n = np.arange(PROBE)
    angle = 2.0 * np.pi / PROBE * (n[:, None] * n[None, :] % PROBE)
    real, imag = np.cos(angle) / np.sqrt(PROBE), -np.sin(angle) / np.sqrt(PROBE)
    whole = np.block([[real, -imag], [imag, real]]).astype(np.float32)

    def halves(matrix):
        high = matrix.astype(ml_dtypes.bfloat16)
        return high, (matrix - high.astype(np.float32)).astype(ml_dtypes.bfloat16)

    high, low = halves(whole)
    high_t, low_t = halves(whole.T.copy())
    return (
        np.concatenate([high, high, low], 1),
        np.concatenate([high_t, high_t, low_t], 0),
        np.concatenate([high_t, high_t, low_t], 1),
        np.concatenate([high, high, low], 0),
    )


def split(value):
    high = value.astype(bf16)
    return high, (value - high.astype(f32)).astype(bf16)


def dot(a, b):
    return jnp.dot(a, b, preferred_element_type=f32)


def left(table, pairs):
    parts = [split(jnp.concatenate([a, b], 0)) for a, b in pairs]
    high = jnp.concatenate([p[0] for p in parts], 1)
    low = jnp.concatenate([p[1] for p in parts], 1)
    out = dot(table[...], jnp.concatenate([high, low, high], 0))
    n = PROBE
    return [(out[:n, n * k : n * k + n], out[n:, n * k : n * k + n]) for k in range(len(pairs))]


def right(table, pairs):
    parts = [split(jnp.concatenate([a, b], 1)) for a, b in pairs]
    high = jnp.concatenate([p[0] for p in parts], 0)
    low = jnp.concatenate([p[1] for p in parts], 0)
    out = dot(jnp.concatenate([high, low, high], 1), table[...])
    n = PROBE
    return [(out[n * k : n * k + n, :n], out[n * k : n * k + n, n:]) for k in range(len(pairs))]


def lanes(rows=PROBE):
    return lax.broadcasted_iota(jnp.int32, (rows, 128), 1)


def cut(cur, row, col):
    block, lane = col >> 7, col & 127
    out = []
    for p in range(2):
        a = cur[p, block, pl.ds(row, PROBE), :]
        b = cur[p, block + 1, pl.ds(row, PROBE), :]
        out.append(pltpu.roll(jnp.where(lanes() >= lane, a, b), (128 - lane) & 127, 1))
    return out


def place(acc, grad, row, col):
    block, lane = col >> 7, col & 127
    for p in range(2):
        g = pltpu.roll(grad[p], lane, 1)
        acc[p, block, pl.ds(row, PROBE), :] += jnp.where(lanes() >= lane, g, 0.0)
        acc[p, block + 1, pl.ds(row, PROBE), :] += jnp.where(lanes() >= lane, 0.0, g)


def all_slots(count, pos, cur, acc, amps, probe, tabs):
    forward_left, forward_right, back_left, back_right = tabs
    pr, pi = probe[0], probe[1]

    def body(i, carry):
        slots = [i * GROUP + k for k in range(GROUP)]
        corners = [(pos[0, s] + BORDER, pos[1, s] + 128) for s in slots]
        pairs = []
        for row, col in corners:
            a, b = cut(cur, row, col)
            pairs.append((pr * a - pi * b, pr * b + pi * a))
        waves = left(forward_left, right(forward_right, pairs))
        shrunk = []
        for (a, b), s in zip(waves, slots):
            k = amps[s] * lax.rsqrt(a * a + b * b + smoothing) - 1.0
            k = k * jnp.where(s < count, 1.0, 0.0)
            shrunk.append((a * k, b * k))
        backs = right(back_right, left(back_left, shrunk))
        for (a, b), (row, col) in zip(backs, corners):
            place(acc, (pr * a + pi * b, pr * b - pi * a), row, col)
        return carry

    lax.fori_loop(0, lax.div(count + GROUP - 1, GROUP), body, 0)


def step_of(probe):
    return step_gain / (jnp.max(probe[0] * probe[0] + probe[1] * probe[1]) + 1e-06)


def neighbours():
    rows, cols = lax.axis_size("row"), lax.axis_size("col")
    row, col = lax.axis_index("row"), lax.axis_index("col")
    out = []
    for dr, dc in DIRS:
        there = None
        for cond in (
            [row > 0] if dr < 0 else [row < rows - 1] if dr > 0 else []
        ) + ([col > 0] if dc < 0 else [col < cols - 1] if dc > 0 else []):
            there = cond if there is None else jnp.logical_and(there, cond)
        out.append((there, (row + dr, col + dc)))
    return out


def greet(near):
    barrier = pltpu.get_barrier_semaphore()
    total = 0
    for there, where in near:
        @pl.when(there)
        def _():
            pl.semaphore_signal(barrier, inc=1, device_id=where, device_id_type=MESH)
        total = total + there.astype(jnp.int32)
    pl.semaphore_wait(barrier, total)


def remote(k, near, sources, targets, send, recv):
    return pltpu.make_async_remote_copy(
        src_ref=sources[k],
        dst_ref=targets[OPP[k]],
        send_sem=send.at[k],
        recv_sem=recv.at[OPP[k]],
        device_id=near[k][1],
        device_id_type=MESH,
    )


def start_all(near, sources, targets, send, recv, which=range(8)):
    for k in which:
        @pl.when(near[k][0])
        def _():
            remote(k, near, sources, targets, send, recv).start()


def finish_all(near, sources, targets, send, recv):
    for k in range(8):
        @pl.when(near[k][0])
        def _():
            remote(k, near, sources, targets, send, recv).wait_send()
            pltpu.make_async_remote_copy(
                src_ref=sources[k],
                dst_ref=targets[k],
                send_sem=send.at[k],
                recv_sem=recv.at[k],
                device_id=near[k][1],
                device_id_type=MESH,
            ).wait_recv()


def split_refs(v, c, d):
    return [v.at[0], v.at[1], c.at[0], c.at[1]] + [d.at[k] for k in range(4)]


def pack(pieces, start):
    lane = lanes()
    out = None
    for q, piece in enumerate(pieces):
        turned = pltpu.roll(piece, (32 * q - start) % 128, 1)
        out = turned if out is None else jnp.where(lane >= 32 * q, turned, out)
    return out


def unpack(value, start):
    return [pltpu.roll(value, (start - 32 * q) % 128, 1) if (start - 32 * q) % 128 else value for q in range(4)]


def halo_kernel(obj, v, c, d, edge, corner, packed, send, recv, load):
    near = neighbours()
    loads = [
        pltpu.make_async_copy(obj.at[:, :, pl.ds(384 * k, 128)], edge.at[k], load.at[k]) for k in range(2)
    ]
    for copy in loads:
        copy.start()
    greet(near)
    targets = split_refs(v, c, d)
    sources = [obj.at[:, pl.ds(0, 32), :], obj.at[:, pl.ds(TILE - 32, 32), :], packed.at[0], packed.at[1]] + [
        corner.at[k] for k in range(4)
    ]
    start_all(near, sources, targets, send, recv, (0, 1))
    for k in range(2):
        loads[k].wait()
        for p in range(2):
            packed[k, p] = pack([edge[k, p, 128 * q : 128 * q + 128, :] for q in range(4)], 96 * k)
            for up in range(2):
                corner[2 * up + k, p] = edge[k, p, (TILE - 32) * up : (TILE - 32) * up + 32, :]
        start_all(near, sources, targets, send, recv, (2 + k, 4 + k, 6 + k))
    finish_all(near, sources, targets, send, recv)


def swap_kernel(sv, sc, sd, v, c, d, send, recv):
    near = neighbours()
    greet(near)
    sources, targets = split_refs(sv, sc, sd), split_refs(v, c, d)
    start_all(near, sources, targets, send, recv)
    finish_all(near, sources, targets, send, recv)


def present(near, k, value):
    return jnp.where(near[k][0], value, 0.0)


def first_kernel(count, pos, obj, hv, hc, hd, amps_hbm, probe, t0, t1, t2, t3, cur, acc, sv, sc, sd, amps, sems):
    near = neighbours()
    copies = [
        pltpu.make_async_copy(
            obj.at[:, :, pl.ds(128 * j, 128)], cur.at[:, j + 1, pl.ds(BORDER, TILE), :], sems.at[j]
        )
        for j in range(4)
    ] + [pltpu.make_async_copy(amps_hbm, amps, sems.at[4])]
    for copy in copies:
        copy.start()
    acc[...] = jnp.zeros_like(acc)
    for k, base in ((0, 0), (1, BORDER + TILE)):
        for j in range(4):
            for p in range(2):
                cur[p, j + 1, base : base + 32, :] = present(near, k, hv[k, p, :, 128 * j : 128 * j + 128])
    for k, block in ((0, 0), (1, 5)):
        for p in range(2):
            for q, piece in enumerate(unpack(hc[k, p], 0 if k else 96)):
                cur[p, block, BORDER + 128 * q : BORDER + 128 * q + 128, :] = present(near, 2 + k, piece)
    for k in range(4):
        base, block = (BORDER + TILE) * (k // 2), 5 * (k % 2)
        for p in range(2):
            cur[p, block, base : base + 32, :] = present(near, 4 + k, hd[k, p])
    for copy in copies:
        copy.wait()
    all_slots(count[0, 0], pos, cur, acc, amps, probe, (t0, t1, t2, t3))
    edge = lanes(64) >= 96
    for p in range(2):
        for k in range(2):
            base = TILE * k
            for j in range(4):
                sv[k, p, j] = acc[p, j + 1, base : base + 64, :]
            sv[k, p, 4] = jnp.where(edge, acc[p, 0, base : base + 64, :], acc[p, 5, base : base + 64, :])
            for side in range(2):
                a, b = acc[p, 4 * side, base : base + 64, :], acc[p, 4 * side + 1, base : base + 64, :]
                sd[2 * k + side, p] = jnp.where(edge, a, b)
        for side in range(2):
            a, b = acc[p, 4 * side], acc[p, 4 * side + 1]
            strip = jnp.where(lanes(ROWS) >= 96, a, b)
            low, high = strip[: ROWS // 2], pltpu.roll(strip[ROWS // 2 :], 64, 1)
            lane = lanes(ROWS // 2)
            middle = jnp.logical_and(lane >= 32, lane < 96)
            sc[side, p] = jnp.where(middle, high, low)


def second_kernel(
    count, pos, cur_in, acc_in, rv, rc, rd, amps_hbm, probe, t0, t1, t2, t3, corr, inner, fv, fc, fd, cur, acc, amps, sems
):
    near = neighbours()
    load = pltpu.make_async_copy(amps_hbm, amps, sems.at[0])
    load.start()
    step = step_of(probe)
    acc[...] = acc_in[...]
    edge = lanes(64) >= 96
    half = ROWS // 2
    for p in range(2):
        for k in range(2):
            base = TILE * k
            for j in range(4):
                acc[p, j + 1, base : base + 64, :] += present(near, k, rv[k, p, j])
            for side in range(2):
                mine = edge if side == 0 else jnp.logical_not(edge)
                acc[p, 5 * side, base : base + 64, :] += jnp.where(mine, present(near, k, rv[k, p, 4]), 0.0)
                both = present(near, 4 + 2 * k + side, rd[2 * k + side, p])
                acc[p, 4 * side, base : base + 64, :] += jnp.where(edge, both, 0.0)
                acc[p, 4 * side + 1, base : base + 64, :] += jnp.where(edge, 0.0, both)
        for side in range(2):
            both = present(near, 2 + side, rc[side, p])
            for q, piece in enumerate((both, pltpu.roll(both, 64, 1))):
                lane = lanes(half)
                acc[p, 4 * side, half * q : half * q + half, :] += jnp.where(lane >= 96, piece, 0.0)
                acc[p, 4 * side + 1, half * q : half * q + half, :] += jnp.where(lane < 32, piece, 0.0)
    cur[...] = cur_in[...] + step * acc[...]
    for k, base in ((0, 0), (1, BORDER + TILE)):
        cur[:, :, base : base + 32, :] = present(near, k, cur[:, :, base : base + 32, :])
    for k, block in ((0, 0), (1, 5)):
        cur[:, block] = present(near, 2 + k, cur[:, block])
    corr[...] = step * acc[:, 1:5, BORDER : BORDER + TILE, :]
    acc[...] = jnp.zeros_like(acc)
    load.wait()
    all_slots(count[0, 0], pos, cur, acc, amps, probe, (t0, t1, t2, t3))
    for p in range(2):
        for k in range(2):
            base = (BORDER + TILE) * k
            for j in range(4):
                fv[k, p, j] = acc[p, j + 1, base : base + 32, :]
            for side in range(2):
                fd[2 * k + side, p] = acc[p, 5 * side, base : base + 32, :]
        for side in range(2):
            fc[side, p] = pack(
                [acc[p, 5 * side, BORDER + 128 * q : BORDER + 128 * q + 128, :] for q in range(4)], 0 if side else 96
            )
    inner[...] = acc[:, 1:5, BORDER : BORDER + TILE, :]


def last_kernel(obj, corr, inner_in, gv, gc, gd, probe, est_out, corr_out, est, total, inner, sems):
    near = neighbours()
    loads = [
        pltpu.make_async_copy(obj.at[:, :, pl.ds(128 * j, 128)], est.at[:, j], sems.at[j]) for j in range(4)
    ]
    for load in loads:
        load.start()
    step = step_of(probe)
    inner[...] = inner_in[...]
    for p in range(2):
        for k in range(2):
            base = (TILE - 32) * k
            for j in range(4):
                inner[p, j, base : base + 32, :] += present(near, k, gv[k, p, j])
            for side in range(2):
                lane = lanes(32)
                mine = lane < 32 if side == 0 else lane >= 96
                both = present(near, 4 + 2 * k + side, gd[2 * k + side, p])
                inner[p, 3 * side, base : base + 32, :] += jnp.where(mine, both, 0.0)
        for side in range(2):
            lane = lanes()
            mine = lane < 32 if side == 0 else lane >= 96
            for q, piece in enumerate(unpack(gc[side, p], 96 if side else 0)):
                inner[p, 3 * side, 128 * q : 128 * q + 128, :] += jnp.where(mine, present(near, 2 + side, piece), 0.0)
    total[...] = corr[...] + step * inner[...]
    stores = []
    for j in range(4):
        stores.append(
            pltpu.make_async_copy(total.at[:, j], corr_out.at[:, :, pl.ds(128 * j, 128)], sems.at[4 + j])
        )
        stores[-1].start()
    for j in range(4):
        loads[j].wait()
        est[:, j] = est[:, j] + total[:, j]
        stores.append(pltpu.make_async_copy(est.at[:, j], est_out.at[:, :, pl.ds(128 * j, 128)], sems.at[8 + j]))
        stores[-1].start()
    for store in stores:
        store.wait()


VM = pl.BlockSpec(memory_space=pltpu.VMEM)
SM = pl.BlockSpec(memory_space=pltpu.SMEM)
ANY = pl.BlockSpec(memory_space=pl.ANY)


def shape(*dims):
    return jax.ShapeDtypeStruct(dims, f32)


def params(limit_mib=40, **kw):
    return pltpu.CompilerParams(vmem_limit_bytes=limit_mib * 2**20, **kw)


def on_device(object_field, probe_field, amplitudes, positions, counts):
    pos = positions[0, 0]
    tabs = [jnp.asarray(t) for t in tables()]
    dma = pltpu.SemaphoreType.DMA
    halo = (shape(2, 2, 32, TILE), shape(2, 2, 128, 128), shape(4, 2, 32, 128))
    hv, hc, hd = pl.pallas_call(
        halo_kernel,
        out_shape=halo,
        in_specs=[ANY],
        out_specs=[VM] * 3,
        scratch_shapes=[
            pltpu.VMEM((2, 2, TILE, 128), f32),
            pltpu.VMEM((4, 2, 32, 128), f32),
            pltpu.VMEM((2, 2, 128, 128), f32),
            dma((8,)),
            dma((8,)),
            dma((2,)),
        ],
        compiler_params=params(collective_id=0, has_side_effects=True),
        name="halo",
    )(object_field)
    ext = (2, BLOCKS, ROWS, 128)
    strips = (shape(2, 2, 5, 64, 128), shape(2, 2, ROWS // 2, 128), shape(4, 2, 64, 128))
    cur, acc, *sent = pl.pallas_call(
        first_kernel,
        out_shape=(shape(*ext), shape(*ext)) + strips,
        in_specs=[SM, SM, ANY, VM, VM, VM, ANY] + [VM] * 5,
        out_specs=[VM] * 5,
        scratch_shapes=[pltpu.VMEM((24, 128, 128), f32), dma((5,))],
        compiler_params=params(),
        name="first",
    )(counts, pos, object_field, hv, hc, hd, amplitudes, probe_field, *tabs)
    got = pl.pallas_call(
        swap_kernel,
        out_shape=strips,
        in_specs=[VM] * 3,
        out_specs=[VM] * 3,
        scratch_shapes=[dma((8,)), dma((8,))],
        compiler_params=params(collective_id=1, has_side_effects=True),
        name="strips",
    )(*sent)
    folds = (shape(2, 2, 4, 32, 128), shape(2, 2, 128, 128), shape(4, 2, 32, 128))
    tile = (2, 4, TILE, 128)
    corr, inner, *sent = pl.pallas_call(
        second_kernel,
        out_shape=(shape(*tile), shape(*tile)) + folds,
        in_specs=[SM, SM, VM, VM, VM, VM, VM, ANY] + [VM] * 5,
        out_specs=[VM] * 5,
        scratch_shapes=[
            pltpu.VMEM(ext, f32),
            pltpu.VMEM(ext, f32),
            pltpu.VMEM((24, 128, 128), f32),
            dma((1,)),
        ],
        compiler_params=params(),
        name="second",
    )(counts, pos, cur, acc, *got, amplitudes, probe_field, *tabs)
    got = pl.pallas_call(
        swap_kernel,
        out_shape=folds,
        in_specs=[VM] * 3,
        out_specs=[VM] * 3,
        scratch_shapes=[dma((8,)), dma((8,))],
        compiler_params=params(collective_id=2, has_side_effects=True),
        name="folds",
    )(*sent)
    return pl.pallas_call(
        last_kernel,
        out_shape=(shape(2, TILE, TILE), shape(2, TILE, TILE)),
        in_specs=[ANY] + [VM] * 6,
        out_specs=[ANY] * 2,
        scratch_shapes=[pltpu.VMEM(tile, f32)] * 3 + [dma((12,))],
        compiler_params=params(),
        name="last",
    )(object_field, corr, inner, *got, probe_field)


def solution(mesh):
    placed = (
        P(None, "row", "col"),
        P(),
        P("row", None, "col"),
        P("row", "col", None, None),
        P("row", "col"),
    )
    return jax.shard_map(
        on_device,
        mesh=mesh,
        in_specs=placed,
        out_specs=(P(None, "row", "col"), P(None, "row", "col")),
        check_vma=False,
    )
```

```python
import functools

import jax
import jax.numpy as jnp
import ml_dtypes
import numpy as np
from jax import lax
from jax.experimental import pallas as pl
from jax.experimental.pallas import tpu as pltpu
from jax.sharding import PartitionSpec as P

BORDER = 32
PROBE = 128
TILE = 512
PMAX = 24
ROWS = TILE + 2 * BORDER
BLOCKS = 6
GROUP = 8
smoothing = 0.5
step_gain = 0.5
f32 = jnp.float32
bf16 = jnp.bfloat16
MESH = pl.DeviceIdType.MESH

DIRS = ((-1, 0), (1, 0), (0, -1), (0, 1), (-1, -1), (-1, 1), (1, -1), (1, 1))
OPP = (1, 0, 3, 2, 7, 6, 5, 4)


def tables():
    n = np.arange(PROBE)
    angle = 2.0 * np.pi / PROBE * (n[:, None] * n[None, :] % PROBE)
    real, imag = np.cos(angle) / np.sqrt(PROBE), -np.sin(angle) / np.sqrt(PROBE)
    whole = np.block([[real, -imag], [imag, real]]).astype(np.float32)

    def halves(matrix):
        high = matrix.astype(ml_dtypes.bfloat16)
        return high, (matrix - high.astype(np.float32)).astype(ml_dtypes.bfloat16)

    return np.stack(halves(whole)), np.stack(halves(whole.T.copy()))


def split(value):
    high = value.astype(bf16)
    return high, (value - high.astype(f32)).astype(bf16)


def dot(a, b):
    return jnp.dot(a, b, preferred_element_type=f32)


def left(table, pairs):
    parts = [split(jnp.concatenate([a, b], 0)) for a, b in pairs]
    high = jnp.concatenate([p[0] for p in parts], 1)
    low = jnp.concatenate([p[1] for p in parts], 1)
    wide = jnp.concatenate([table[0], table[0], table[1]], 1)
    out = dot(wide, jnp.concatenate([high, low, high], 0))
    n = PROBE
    return [(out[:n, n * k : n * k + n], out[n:, n * k : n * k + n]) for k in range(len(pairs))]


def right(table, pairs):
    parts = [split(jnp.concatenate([a, b], 1)) for a, b in pairs]
    high = jnp.concatenate([p[0] for p in parts], 0)
    low = jnp.concatenate([p[1] for p in parts], 0)
    tall = jnp.concatenate([table[0], table[0], table[1]], 0)
    out = dot(jnp.concatenate([high, low, high], 1), tall)
    n = PROBE
    return [(out[n * k : n * k + n, :n], out[n * k : n * k + n, n:]) for k in range(len(pairs))]


def lanes(rows=PROBE):
    return lax.broadcasted_iota(jnp.int32, (rows, 128), 1)


def cut(cur, row, col):
    block, lane = col >> 7, col & 127
    out = []
    for p in range(2):
        a = cur[p, block, pl.ds(row, PROBE), :]
        b = cur[p, block + 1, pl.ds(row, PROBE), :]
        out.append(pltpu.roll(jnp.where(lanes() >= lane, a, b), (128 - lane) & 127, 1))
    return out


def place(acc, grad, row, col):
    block, lane = col >> 7, col & 127
    for p in range(2):
        g = pltpu.roll(grad[p], lane, 1)
        acc[p, block, pl.ds(row, PROBE), :] += jnp.where(lanes() >= lane, g, 0.0)
        acc[p, block + 1, pl.ds(row, PROBE), :] += jnp.where(lanes() >= lane, 0.0, g)


def gradients(cur, amps, probe, tabs, pos, slots, scale=None):
    forward, backward = tabs
    pr, pi = probe[0], probe[1]
    pairs = []
    for s in slots:
        a, b = cut(cur, *corner_of(pos, s))
        pairs.append((pr * a - pi * b, pr * b + pi * a))
    waves = left(forward, right(backward, pairs))
    shrunk = []
    for k, ((a, b), s) in enumerate(zip(waves, slots)):
        gain = amps[s] * lax.rsqrt(a * a + b * b + smoothing) - 1.0
        if scale is not None:
            gain = gain * scale[k]
        shrunk.append((a * gain, b * gain))
    backs = right(forward, left(backward, shrunk))
    return [(pr * a + pi * b, pr * b - pi * a) for a, b in backs]


def corner_of(pos, s):
    return pos[0, s] + BORDER, pos[1, s] + 128


def inside(pos, s, low, high):
    r, c = pos[0, s], pos[1, s]
    return jnp.logical_and(
        jnp.logical_and(r >= low, r <= high), jnp.logical_and(c >= low, c <= high)
    )


def listed_slots(amount, todo, pos, cur, acc, amps, probe, tabs):
    def body(i, carry):
        at = [i * GROUP + k for k in range(GROUP)]
        slots = [jnp.where(j < amount, todo[j], 0) for j in at]
        scale = [jnp.where(j < amount, 1.0, 0.0) for j in at]
        grads = gradients(cur, amps, probe, tabs, pos, slots, scale)
        for grad, s in zip(grads, slots):
            place(acc, grad, *corner_of(pos, s))
        return carry

    lax.fori_loop(0, lax.div(amount + GROUP - 1, GROUP), body, 0)


def step_of(probe):
    return step_gain / (jnp.max(probe[0] * probe[0] + probe[1] * probe[1]) + 1e-06)


def neighbours():
    rows, cols = lax.axis_size("row"), lax.axis_size("col")
    row, col = lax.axis_index("row"), lax.axis_index("col")
    out = []
    for dr, dc in DIRS:
        there = None
        for cond in (
            [row > 0] if dr < 0 else [row < rows - 1] if dr > 0 else []
        ) + ([col > 0] if dc < 0 else [col < cols - 1] if dc > 0 else []):
            there = cond if there is None else jnp.logical_and(there, cond)
        out.append((there, (row + dr, col + dc)))
    return out


def greet(near):
    barrier = pltpu.get_barrier_semaphore()
    total = 0
    for there, where in near:
        @pl.when(there)
        def _():
            pl.semaphore_signal(barrier, inc=1, device_id=where, device_id_type=MESH)
        total = total + there.astype(jnp.int32)
    pl.semaphore_wait(barrier, total)


def remote(k, near, source, target, send, recv, n):
    return pltpu.make_async_remote_copy(
        src_ref=source,
        dst_ref=target,
        send_sem=send.at[n],
        recv_sem=recv.at[n],
        device_id=near[k][1],
        device_id_type=MESH,
    )


class Post:
    def __init__(self, near, send, recv):
        self.near, self.send, self.recv = near, send, recv
        self.count, self.waits = 0, []

    def pair(self, k, outs, intos):
        for i, way in enumerate((k, OPP[k])):
            n = self.count + i
            @pl.when(self.near[way][0])
            def _(i=i, way=way, n=n):
                remote(way, self.near, outs[i], intos[1 - i], self.send, self.recv, n).start()

        def wait(base=self.count):
            for i, way in enumerate((k, OPP[k])):
                @pl.when(self.near[way][0])
                def _(i=i, way=way):
                    remote(way, self.near, outs[i], intos[i], self.send, self.recv, base + i).wait_send()
                    remote(way, self.near, outs[i], intos[i], self.send, self.recv, base + 1 - i).wait_recv()

        self.count += 2
        return wait


def pack(pieces, start):
    lane = lanes(pieces[0].shape[0])
    out = None
    for q, piece in enumerate(pieces):
        turn = (32 * q - start) % 128
        turned = pltpu.roll(piece, turn, 1) if turn else piece
        out = turned if out is None else jnp.where(lane >= 32 * q, turned, out)
    return out


def unpack(value, start):
    turns = [(start - 32 * q) % 128 for q in range(4)]
    return [pltpu.roll(value, turn, 1) if turn else value for turn in turns]


def pack_two(value):
    half = value.shape[0] // 2
    lane = lanes(half)
    middle = jnp.logical_and(lane >= 32, lane < 96)
    return jnp.where(middle, pltpu.roll(value[half:], 64, 1), value[:half])


def unpack_two(value):
    return jnp.concatenate([value, pltpu.roll(value, 64, 1)], 0)


def seam(a, b):
    return jnp.where(lanes(a.shape[0]) >= 96, a, b)


def present(near, k, value):
    return jnp.where(near[k][0], value, 0.0)


EARLY = 16
LATE = 8


def halo_kernel(
    count, pos, obj, amps_hbm, probe, t0, t1, cur, early, order, amps, hv, hc, hd, sc, sd, follow, send, recv, sems
):
    near = neighbours()
    tile_at = [
        pltpu.make_async_copy(
            obj.at[:, :, pl.ds(128 * j, 128)], cur.at[:, j + 1, pl.ds(BORDER, TILE), :], sems.at[j]
        )
        for j in range(4)
    ]
    for j in (0, 3, 1, 2):
        tile_at[j].start()
    measured = pltpu.make_async_copy(amps_hbm, amps, sems.at[4])
    measured.start()
    greet(near)
    post = Post(near, send, recv)
    waits = [post.pair(0, [obj.at[:, pl.ds(0, 32), :], obj.at[:, pl.ds(TILE - 32, 32), :]], [hv.at[0], hv.at[1]])]
    for side in range(2):
        tile_at[3 * side].wait()
        block, start = 1 + 3 * side, 96 * side
        for p in range(2):
            sc[side, p] = pack(
                [cur[p, block, BORDER + 128 * q : BORDER + 128 * q + 128, :] for q in range(4)], start
            )
            for ud in range(2):
                base = BORDER + (TILE - 32) * ud
                sd[2 * ud + side, p] = pack(
                    [cur[p, block, base + 8 * q : base + 8 * q + 8, :] for q in range(4)], start
                )
    waits.append(post.pair(4, [sd.at[0], sd.at[3]], [hd.at[0], hd.at[3]]))
    waits.append(post.pair(5, [sd.at[1], sd.at[2]], [hd.at[1], hd.at[2]]))
    waits.append(post.pair(2, [sc.at[0], sc.at[1]], [hc.at[0], hc.at[1]]))
    coming = jnp.int32(PMAX)
    follow[PMAX] = coming
    for s in range(PMAX - 1, -1, -1):
        keep = jnp.logical_and(s < count[0, 0], inside(pos, s, 0, TILE - PROBE))
        coming = jnp.where(keep, s, coming)
        follow[s] = coming
    coming = follow[0]
    for k in range(EARLY):
        order[k] = coming
        coming = follow[jnp.minimum(coming + 1, PMAX)]
    zeros = jnp.zeros((2, BLOCKS, BORDER, 128), f32)
    cur[:, :, 0:BORDER, :] = zeros
    cur[:, :, BORDER + TILE :, :] = zeros
    cur[:, 0] = jnp.zeros((2, ROWS, 128), f32)
    cur[:, 5] = jnp.zeros((2, ROWS, 128), f32)
    tile_at[1].wait()
    tile_at[2].wait()
    measured.wait()

    def body(i, carry):
        slots = [jnp.minimum(order[i * GROUP + k], PMAX - 1) for k in range(GROUP)]
        for k, (a, b) in enumerate(gradients(cur, amps, probe, (t0, t1), pos, slots)):
            early[i * GROUP + k, 0] = a
            early[i * GROUP + k, 1] = b
        return carry

    lax.fori_loop(0, EARLY // GROUP, body, 0)
    for wait in waits:
        wait()
    for p in range(2):
        for k in range(2):
            base = (BORDER + TILE) * k
            for j in range(4):
                cur[p, j + 1, base : base + 32, :] = present(near, k, hv[k, p, :, 128 * j : 128 * j + 128])
            for side in range(2):
                for q, piece in enumerate(unpack(hd[2 * k + side, p], 96 - 96 * side)):
                    cur[p, 5 * side, base + 8 * q : base + 8 * q + 8, :] = present(near, 4 + 2 * k + side, piece)
        for side in range(2):
            for q, piece in enumerate(unpack(hc[side, p], 96 - 96 * side)):
                at = BORDER + 128 * q
                cur[p, 5 * side, at : at + 128, :] = present(near, 2 + side, piece)


def first_kernel(count, pos, order, cur, early, amps, probe, t0, t1, acc, after, todo):
    live = count[0, 0]
    acc[...] = jnp.zeros_like(acc)

    def sort(s, carry):
        amount, kept = carry
        keep = inside(pos, s, 0, TILE - PROBE)
        done = jnp.logical_and(keep, kept < EARLY)

        @pl.when(jnp.logical_not(done))
        def _():
            todo[amount] = s

        return amount + jnp.where(done, 0, 1), kept + jnp.where(keep, 1, 0)

    amount, kept = lax.fori_loop(0, live, sort, (jnp.int32(0), jnp.int32(0)))

    def put(k, carry):
        place(acc, (early[k, 0], early[k, 1]), *corner_of(pos, order[k]))
        return carry

    lax.fori_loop(0, jnp.minimum(kept, EARLY), put, 0)
    listed_slots(amount, todo, pos, cur, acc, amps, probe, (t0, t1))
    after[...] = cur[...] + step_of(probe) * acc[...]


def strip_kernel(pos, acc, cur, amps, probe, t0, t1, grads, rv, rs, rc, rm, sv, ss, sc, sm, send, recv):
    near = neighbours()
    for p in range(2):
        for side in range(2):
            for ud in range(2):
                rows = pl.ds(TILE * ud, 64)
                sc[side, ud, p] = pack_two(seam(acc[p, 4 * side, rows, :], acc[p, 4 * side + 1, rows, :]))
    greet(near)
    post = Post(near, send, recv)
    corners = post.pair(2, [sc.at[0], sc.at[1]], [rc.at[0], rc.at[1]])
    waits = [
        post.pair(
            0,
            [acc.at[:, pl.ds(2, 2), pl.ds(TILE * ud, 64), :] for ud in range(2)],
            [rv.at[ud, :, pl.ds(1, 2)] for ud in range(2)],
        )
    ]
    for p in range(2):
        for side in range(2):
            sm[side, p] = pack_two(seam(acc[p, 4 * side, 64:TILE, :], acc[p, 4 * side + 1, 64:TILE, :]))
    waits.append(post.pair(2, [sm.at[0], sm.at[1]], [rm.at[0], rm.at[1]]))

    def body(i, carry):
        slots = [i * GROUP + k for k in range(GROUP)]
        for s, (a, b) in zip(slots, gradients(cur, amps, probe, (t0, t1), pos, slots)):
            grads[s, 0] = a
            grads[s, 1] = b
        return carry

    lax.fori_loop(0, 1, body, 0)
    corners()
    lane = lanes(64)
    for p in range(2):
        for ud in range(2):
            rows = pl.ds(TILE * ud, 64)
            west = present(near, 2, unpack_two(rc[0, ud, p]))
            east = present(near, 3, unpack_two(rc[1, ud, p]))
            sv[ud, p, 0] = acc[p, 1, rows, :] + jnp.where(lane < 32, west, 0.0)
            sv[ud, p, 1] = acc[p, 4, rows, :] + jnp.where(lane >= 96, east, 0.0)
            ss[ud, p] = pack_two(seam(acc[p, 0, rows, :] + west, acc[p, 5, rows, :] + east))
    for n, block in ((0, 0), (1, 3)):
        waits.append(
            post.pair(0, [sv.at[ud, :, n] for ud in range(2)], [rv.at[ud, :, block] for ud in range(2)])
        )
    waits.append(post.pair(0, [ss.at[0], ss.at[1]], [rs.at[0], rs.at[1]]))
    lax.fori_loop(1, PMAX // GROUP, body, 0)
    for wait in waits:
        wait()


def second_kernel(
    count, pos, acc_in, cur_in, rv, rs, rc, rm, grads, amps, probe, t0, t1, acc, cur, late, todo
):
    near = neighbours()
    step = step_of(probe)
    live = count[0, 0]
    acc[...] = acc_in[...]
    cur[...] = cur_in[...]

    def add(p, block, rows, value):
        acc[p, block, rows, :] += value
        cur[p, block, rows, :] += step * value

    for p in range(2):
        for ud in range(2):
            rows = pl.ds(TILE * ud, 64)
            for j in range(4):
                add(p, j + 1, rows, present(near, ud, rv[ud, p, j]))
            sides = present(near, ud, unpack_two(rs[ud, p]))
            lane = lanes(64)
            add(p, 0, rows, jnp.where(lane >= 96, sides, 0.0))
            add(p, 5, rows, jnp.where(lane < 32, sides, 0.0))
        for side in range(2):
            for rows, piece in (
                (pl.ds(0, 64), rc[side, 0, p]),
                (pl.ds(64, TILE - 64), rm[side, p]),
                (pl.ds(TILE, 64), rc[side, 1, p]),
            ):
                piece = present(near, 2 + side, unpack_two(piece))
                lane = lanes(piece.shape[0])
                add(p, 4 * side, rows, jnp.where(lane >= 96, piece, 0.0))
                add(p, 4 * side + 1, rows, jnp.where(lane < 32, piece, 0.0))
    for k in range(2):
        rows = pl.ds((BORDER + TILE) * k, BORDER)
        cur[:, :, rows, :] = present(near, k, cur[:, :, rows, :])
        cur[:, 5 * k] = present(near, 2 + k, cur[:, 5 * k])
        acc[:, :, rows, :] = jnp.zeros((2, BLOCKS, BORDER, 128), f32)
        acc[:, 5 * k] = jnp.zeros((2, ROWS, 128), f32)
    for k in range(LATE):
        late[k] = PMAX

    def sort(s, carry):
        amount, held = carry
        done = inside(pos, s, BORDER, TILE - PROBE - BORDER)
        hold = jnp.logical_and(
            jnp.logical_and(inside(pos, s, 0, TILE - PROBE), held < LATE), jnp.logical_not(done)
        )

        @pl.when(done)
        def _():
            place(acc, (grads[s, 0], grads[s, 1]), *corner_of(pos, s))

        @pl.when(hold)
        def _():
            late[held] = s

        now = jnp.logical_not(jnp.logical_or(done, hold))

        @pl.when(now)
        def _():
            todo[amount] = s

        return amount + jnp.where(now, 1, 0), held + jnp.where(hold, 1, 0)

    amount, _ = lax.fori_loop(0, live, sort, (jnp.int32(0), jnp.int32(0)))
    listed_slots(amount, todo, pos, cur, acc, amps, probe, (t0, t1))


def fold_kernel(pos, late, acc, cur, amps, probe, t0, t1, grads, gv, gc, gd, sc, sd, send, recv):
    near = neighbours()
    for p in range(2):
        for side in range(2):
            start = 96 - 96 * side
            for ud in range(2):
                base = (BORDER + TILE) * ud
                sd[2 * ud + side, p] = pack(
                    [acc[p, 5 * side, base + 8 * q : base + 8 * q + 8, :] for q in range(4)], start
                )
    greet(near)
    post = Post(near, send, recv)
    waits = [
        post.pair(
            0,
            [acc.at[:, pl.ds(1, 4), pl.ds((BORDER + TILE) * ud, BORDER), :] for ud in range(2)],
            [gv.at[0], gv.at[1]],
        ),
        post.pair(4, [sd.at[0], sd.at[3]], [gd.at[0], gd.at[3]]),
        post.pair(5, [sd.at[1], sd.at[2]], [gd.at[1], gd.at[2]]),
    ]
    for p in range(2):
        for side in range(2):
            sc[side, p] = pack(
                [acc[p, 5 * side, BORDER + 128 * q : BORDER + 128 * q + 128, :] for q in range(4)], 96 - 96 * side
            )
    waits.append(post.pair(2, [sc.at[0], sc.at[1]], [gc.at[0], gc.at[1]]))

    def body(i, carry):
        slots = [jnp.minimum(late[i * GROUP + k], PMAX - 1) for k in range(GROUP)]
        for k, (a, b) in enumerate(gradients(cur, amps, probe, (t0, t1), pos, slots)):
            grads[i * GROUP + k, 0] = a
            grads[i * GROUP + k, 1] = b
        return carry

    lax.fori_loop(0, LATE // GROUP, body, 0)
    for wait in waits:
        wait()


def last_kernel(
    pos, late, obj, acc_in, gv, gc, gd, grads, probe, est_out, corr_out, est, acc, sems
):
    near = neighbours()
    loads = [
        pltpu.make_async_copy(obj.at[:, :, pl.ds(128 * j, 128)], est.at[:, j], sems.at[j]) for j in range(4)
    ]
    for load in loads:
        load.start()
    step = step_of(probe)
    acc[...] = acc_in[...]

    def put(k, carry):
        s = late[k]

        @pl.when(s < PMAX)
        def _():
            place(acc, (grads[k, 0], grads[k, 1]), *corner_of(pos, s))

        return carry

    lax.fori_loop(0, LATE, put, 0)
    for p in range(2):
        for side in range(2):
            block, start = 1 + 3 * side, 96 * side

            def mine(rows):
                return lanes(rows) >= 96 if side else lanes(rows) < 32

            for q, piece in enumerate(unpack(gc[side, p], start)):
                at = BORDER + 128 * q
                acc[p, block, at : at + 128, :] += jnp.where(mine(128), present(near, 2 + side, piece), 0.0)
            for ud in range(2):
                base = BORDER + (TILE - 32) * ud
                for q, piece in enumerate(unpack(gd[2 * ud + side, p], start)):
                    at = base + 8 * q
                    piece = present(near, 4 + 2 * ud + side, piece)
                    acc[p, block, at : at + 8, :] += jnp.where(mine(8), piece, 0.0)
        for ud in range(2):
            base = BORDER + (TILE - 32) * ud
            for j in range(4):
                acc[p, j + 1, base : base + 32, :] += present(near, ud, gv[ud, p, j])
    stores = []
    inner = pl.ds(BORDER, TILE)
    for j in range(4):
        out = pl.ds(128 * j, 128)
        acc[:, j + 1, inner, :] = step * acc[:, j + 1, inner, :]
        stores.append(pltpu.make_async_copy(acc.at[:, j + 1, inner, :], corr_out.at[:, :, out], sems.at[4 + j]))
        stores[-1].start()
        loads[j].wait()
        est[:, j] = est[:, j] + acc[:, j + 1, inner, :]
        stores.append(pltpu.make_async_copy(est.at[:, j], est_out.at[:, :, out], sems.at[8 + j]))
        stores[-1].start()
    for store in stores:
        store.wait()


VM = pl.BlockSpec(memory_space=pltpu.VMEM)
SM = pl.BlockSpec(memory_space=pltpu.SMEM)
HBM = pl.BlockSpec(memory_space=pltpu.HBM)


def shape(*dims, dtype=f32):
    return jax.ShapeDtypeStruct(dims, dtype)


def params(limit_mib=14, **kw):
    return pltpu.CompilerParams(vmem_limit_bytes=limit_mib * 2**20, **kw)


def remote_params(which):
    return params(collective_id=which, has_side_effects=True)


def on_device(object_field, probe_field, amplitudes, positions, counts):
    pos = positions[0, 0]
    tabs = [jnp.asarray(t) for t in tables()]
    dma = pltpu.SemaphoreType.DMA
    tile = (2, BLOCKS, ROWS, 128)
    window = (2, PROBE, PROBE)
    measured = shape(PMAX, PROBE, PROBE)
    far = functools.partial(pltpu.with_memory_space_constraint, memory_space=pltpu.HBM)
    cur, early, order, amps = pl.pallas_call(
        halo_kernel,
        out_shape=(shape(*tile), shape(EARLY, *window), shape(EARLY, dtype=jnp.int32), measured),
        in_specs=[SM, SM, HBM, HBM, VM, VM, VM],
        out_specs=[VM, VM, SM, VM],
        scratch_shapes=[
            pltpu.VMEM((2, 2, 32, TILE), f32),
            pltpu.VMEM((2, 2, 128, 128), f32),
            pltpu.VMEM((4, 2, 8, 128), f32),
            pltpu.VMEM((2, 2, 128, 128), f32),
            pltpu.VMEM((4, 2, 8, 128), f32),
            pltpu.SMEM((PMAX + 1,), jnp.int32),
            dma((8,)),
            dma((8,)),
            dma((5,)),
        ],
        compiler_params=remote_params(0),
        name="halo",
    )(counts, pos, far(object_field), far(amplitudes), probe_field, *tabs)
    shared = (amps, probe_field, *tabs)
    acc, after = pl.pallas_call(
        first_kernel,
        out_shape=(shape(*tile), shape(*tile)),
        in_specs=[SM, SM, SM] + [VM] * 6,
        out_specs=[VM] * 2,
        scratch_shapes=[pltpu.SMEM((PMAX,), jnp.int32)],
        compiler_params=params(),
        name="first",
    )(counts, pos, order, cur, early, *shared)
    strips = ((2, 2, 4, 64, 128), (2, 2, 32, 128), (2, 2, 2, 32, 128), (2, 2, 224, 128))
    grads, *got = pl.pallas_call(
        strip_kernel,
        out_shape=(shape(PMAX, *window),) + tuple(shape(*s) for s in strips),
        in_specs=[SM] + [VM] * 6,
        out_specs=[VM] * 5,
        scratch_shapes=[
            pltpu.VMEM((2, 2, 2, 64, 128), f32),
            pltpu.VMEM((2, 2, 32, 128), f32),
            pltpu.VMEM((2, 2, 2, 32, 128), f32),
            pltpu.VMEM((2, 2, 224, 128), f32),
            dma((12,)),
            dma((12,)),
        ],
        compiler_params=remote_params(1),
        name="strips",
    )(pos, acc, after, *shared)
    acc, cur, late = pl.pallas_call(
        second_kernel,
        out_shape=(shape(*tile), shape(*tile), shape(LATE, dtype=jnp.int32)),
        in_specs=[SM, SM] + [VM] * 11,
        out_specs=[VM, VM, SM],
        scratch_shapes=[pltpu.SMEM((PMAX,), jnp.int32)],
        compiler_params=params(),
        name="second",
    )(counts, pos, acc, after, *got, grads, *shared)
    folds = ((2, 2, 4, 32, 128), (2, 2, 128, 128), (4, 2, 8, 128))
    grads, *got = pl.pallas_call(
        fold_kernel,
        out_shape=(shape(LATE, *window),) + tuple(shape(*s) for s in folds),
        in_specs=[SM, SM] + [VM] * 6,
        out_specs=[VM] * 4,
        scratch_shapes=[
            pltpu.VMEM((2, 2, 128, 128), f32),
            pltpu.VMEM((4, 2, 8, 128), f32),
            dma((8,)),
            dma((8,)),
        ],
        compiler_params=remote_params(2),
        name="folds",
    )(pos, late, acc, cur, *shared)
    return pl.pallas_call(
        last_kernel,
        out_shape=(shape(2, TILE, TILE), shape(2, TILE, TILE)),
        in_specs=[SM, SM, HBM] + [VM] * 6,
        out_specs=[HBM] * 2,
        scratch_shapes=[pltpu.VMEM((2, 4, TILE, 128), f32), pltpu.VMEM(tile, f32), dma((12,))],
        compiler_params=params(),
        name="last",
    )(pos, late, far(object_field), acc, *got, grads, probe_field)


def solution(mesh):
    placed = (
        P(None, "row", "col"),
        P(),
        P("row", None, "col"),
        P("row", "col", None, None),
        P("row", "col"),
    )
    return jax.shard_map(
        on_device,
        mesh=mesh,
        in_specs=placed,
        out_specs=(P(None, "row", "col"), P(None, "row", "col")),
        check_vma=False,
    )
```

```python
import functools

import jax
import jax.numpy as jnp
import ml_dtypes
import numpy as np
from jax import lax
from jax.experimental import pallas as pl
from jax.experimental.pallas import tpu as pltpu
from jax.sharding import PartitionSpec as P

BORDER = 32
PROBE = 128
TILE = 512
PMAX = 24
ROWS = TILE + 2 * BORDER
BLOCKS = 6
GROUP = 8
smoothing = 0.5
step_gain = 0.5
f32 = jnp.float32
bf16 = jnp.bfloat16
MESH = pl.DeviceIdType.MESH

DIRS = ((-1, 0), (1, 0), (0, -1), (0, 1), (-1, -1), (-1, 1), (1, -1), (1, 1))
OPP = (1, 0, 3, 2, 7, 6, 5, 4)


def tables():
    n = np.arange(PROBE)
    angle = 2.0 * np.pi / PROBE * (n[:, None] * n[None, :] % PROBE)
    real, imag = np.cos(angle) / np.sqrt(PROBE), -np.sin(angle) / np.sqrt(PROBE)
    whole = np.block([[real, -imag], [imag, real]]).astype(np.float32)

    def halves(matrix):
        high = matrix.astype(ml_dtypes.bfloat16)
        return high, (matrix - high.astype(np.float32)).astype(ml_dtypes.bfloat16)

    return np.stack(halves(whole)), np.stack(halves(whole.T.copy()))


def split(value):
    high = value.astype(bf16)
    return high, (value - high.astype(f32)).astype(bf16)


def dot(a, b):
    return jnp.dot(a, b, preferred_element_type=f32)


def left(table, pairs):
    parts = [split(jnp.concatenate([a, b], 0)) for a, b in pairs]
    high = jnp.concatenate([p[0] for p in parts], 1)
    low = jnp.concatenate([p[1] for p in parts], 1)
    wide = jnp.concatenate([table[0], table[0], table[1]], 1)
    out = dot(wide, jnp.concatenate([high, low, high], 0))
    n = PROBE
    return [(out[:n, n * k : n * k + n], out[n:, n * k : n * k + n]) for k in range(len(pairs))]


def right(table, pairs):
    parts = [split(jnp.concatenate([a, b], 1)) for a, b in pairs]
    high = jnp.concatenate([p[0] for p in parts], 0)
    low = jnp.concatenate([p[1] for p in parts], 0)
    tall = jnp.concatenate([table[0], table[0], table[1]], 0)
    out = dot(jnp.concatenate([high, low, high], 1), tall)
    n = PROBE
    return [(out[n * k : n * k + n, :n], out[n * k : n * k + n, n:]) for k in range(len(pairs))]


def lanes(rows=PROBE):
    return lax.broadcasted_iota(jnp.int32, (rows, 128), 1)


def cut(cur, row, col):
    block, lane = col >> 7, col & 127
    out = []
    for p in range(2):
        a = cur[p, block, pl.ds(row, PROBE), :]
        b = cur[p, block + 1, pl.ds(row, PROBE), :]
        out.append(pltpu.roll(jnp.where(lanes() >= lane, a, b), (128 - lane) & 127, 1))
    return out


def place(acc, grad, row, col):
    block, lane = col >> 7, col & 127
    for p in range(2):
        g = pltpu.roll(grad[p], lane, 1)
        acc[p, block, pl.ds(row, PROBE), :] += jnp.where(lanes() >= lane, g, 0.0)
        acc[p, block + 1, pl.ds(row, PROBE), :] += jnp.where(lanes() >= lane, 0.0, g)


def gradients(cur, amps, probe, tabs, pos, slots, scale=None):
    forward, backward = tabs
    pr, pi = probe[0], probe[1]
    pairs = []
    for s in slots:
        a, b = cut(cur, *corner_of(pos, s))
        pairs.append((pr * a - pi * b, pr * b + pi * a))
    waves = left(forward, right(backward, pairs))
    shrunk = []
    for k, ((a, b), s) in enumerate(zip(waves, slots)):
        gain = amps[s] * lax.rsqrt(a * a + b * b + smoothing) - 1.0
        if scale is not None:
            gain = gain * scale[k]
        shrunk.append((a * gain, b * gain))
    backs = right(forward, left(backward, shrunk))
    return [(pr * a + pi * b, pr * b - pi * a) for a, b in backs]


def corner_of(pos, s):
    return pos[0, 0, 0, s] + BORDER, pos[0, 0, 1, s] + 128


def within(start, margin):
    return jnp.logical_and(start >= margin, start <= TILE - PROBE - margin)


def rows_within(pos, s, margin):
    return within(pos[0, 0, 0, s], margin)


def columns_within(pos, s, margin):
    return within(pos[0, 0, 1, s], margin)


def listed_slots(amount, todo, pos, cur, acc, amps, probe, tabs):
    def some(start, size):
        at = [start + k for k in range(size)]
        slots = [jnp.where(j < amount, todo[j], 0) for j in at]
        scale = [jnp.where(j < amount, 1.0, 0.0) for j in at]
        grads = gradients(cur, amps, probe, tabs, pos, slots, scale)
        for grad, s in zip(grads, slots):
            place(acc, grad, *corner_of(pos, s))

    def body(i, carry):
        some(i * GROUP, GROUP)
        return carry

    full = lax.div(amount + GROUP // 2 - 1, GROUP)
    lax.fori_loop(0, full, body, 0)

    @pl.when(amount > full * GROUP)
    def _():
        some(full * GROUP, GROUP // 2)


def step_of(probe):
    return step_gain / (jnp.max(probe[0] * probe[0] + probe[1] * probe[1]) + 1e-06)


def neighbours():
    rows, cols = lax.axis_size("row"), lax.axis_size("col")
    row, col = lax.axis_index("row"), lax.axis_index("col")
    out = []
    for dr, dc in DIRS:
        there = None
        for cond in (
            [row > 0] if dr < 0 else [row < rows - 1] if dr > 0 else []
        ) + ([col > 0] if dc < 0 else [col < cols - 1] if dc > 0 else []):
            there = cond if there is None else jnp.logical_and(there, cond)
        out.append((there, (row + dr, col + dc)))
    return out


def greet(near):
    barrier = pltpu.get_barrier_semaphore()
    for there, where in near:
        @pl.when(there)
        def _():
            pl.semaphore_signal(barrier, inc=1, device_id=where, device_id_type=MESH)


def greeted(near):
    total = 0
    for there, _ in near:
        total = total + there.astype(jnp.int32)
    pl.semaphore_wait(pltpu.get_barrier_semaphore(), total)


def remote(k, near, source, target, send, recv, n):
    return pltpu.make_async_remote_copy(
        src_ref=source,
        dst_ref=target,
        send_sem=send.at[n],
        recv_sem=recv.at[n],
        device_id=near[k][1],
        device_id_type=MESH,
    )


class Post:
    def __init__(self, near, send, recv):
        self.near, self.send, self.recv = near, send, recv
        self.count, self.waits = 0, []

    def pair(self, k, outs, intos):
        for i, way in enumerate((k, OPP[k])):
            n = self.count + i
            @pl.when(self.near[way][0])
            def _(i=i, way=way, n=n):
                remote(way, self.near, outs[i], intos[1 - i], self.send, self.recv, n).start()

        def wait(base=self.count):
            for i, way in enumerate((k, OPP[k])):
                @pl.when(self.near[way][0])
                def _(i=i, way=way):
                    remote(way, self.near, outs[i], intos[i], self.send, self.recv, base + i).wait_send()
                    remote(way, self.near, outs[i], intos[i], self.send, self.recv, base + 1 - i).wait_recv()

        self.count += 2
        return wait


def pack(pieces, start):
    lane = lanes(pieces[0].shape[0])
    out = None
    for q, piece in enumerate(pieces):
        turn = (32 * q - start) % 128
        turned = pltpu.roll(piece, turn, 1) if turn else piece
        out = turned if out is None else jnp.where(lane >= 32 * q, turned, out)
    return out


def unpack(value, start):
    turns = [(start - 32 * q) % 128 for q in range(4)]
    return [pltpu.roll(value, turn, 1) if turn else value for turn in turns]


def pack_two(value):
    half = value.shape[0] // 2
    lane = lanes(half)
    middle = jnp.logical_and(lane >= 32, lane < 96)
    return jnp.where(middle, pltpu.roll(value[half:], 64, 1), value[:half])


def unpack_two(value):
    return jnp.concatenate([value, pltpu.roll(value, 64, 1)], 0)


def seam(a, b):
    return jnp.where(lanes(a.shape[0]) >= 96, a, b)


def present(near, k, value):
    return jnp.where(near[k][0], value, 0.0)


LATE = 8


def keep_gradients(grads, cur, amps, probe, tabs, pos):
    def body(i, carry):
        slots = [i * GROUP + k for k in range(GROUP)]
        for s, (a, b) in zip(slots, gradients(cur, amps, probe, tabs, pos, slots)):
            grads[s, 0] = a
            grads[s, 1] = b
        return carry

    return body


def halo_kernel(
    pos, obj, amps_far, probe_far, t0_far, t1_far, cur, grads, amps, probe, t0, t1, hv, hc, hd, sc, sd, send, recv, sems
):
    near = neighbours()
    greet(near)
    tile_at = [
        pltpu.make_async_copy(
            obj.at[:, :, pl.ds(128 * j, 128)], cur.at[:, j + 1, pl.ds(BORDER, TILE), :], sems.at[j]
        )
        for j in range(4)
    ]
    others = [
        pltpu.make_async_copy(there, here, sems.at[4 + n])
        for n, (there, here) in enumerate(((probe_far, probe), (t0_far, t0), (t1_far, t1), (amps_far, amps)))
    ]
    for copy in [tile_at[j] for j in (0, 3, 1, 2)] + others:
        copy.start()
    zeros = jnp.zeros((2, BLOCKS, BORDER, 128), f32)
    cur[:, :, 0:BORDER, :] = zeros
    cur[:, :, BORDER + TILE :, :] = zeros
    cur[:, 0] = jnp.zeros((2, ROWS, 128), f32)
    cur[:, 5] = jnp.zeros((2, ROWS, 128), f32)
    greeted(near)
    post = Post(near, send, recv)
    waits = [post.pair(0, [obj.at[:, pl.ds(0, 32), :], obj.at[:, pl.ds(TILE - 32, 32), :]], [hv.at[0], hv.at[1]])]
    for side in range(2):
        tile_at[3 * side].wait()
        block, start = 1 + 3 * side, 96 * side
        for p in range(2):
            sc[side, p] = pack(
                [cur[p, block, BORDER + 128 * q : BORDER + 128 * q + 128, :] for q in range(4)], start
            )
            for ud in range(2):
                base = BORDER + (TILE - 32) * ud
                sd[2 * ud + side, p] = pack(
                    [cur[p, block, base + 8 * q : base + 8 * q + 8, :] for q in range(4)], start
                )
    sideways = post.pair(2, [sc.at[0], sc.at[1]], [hc.at[0], hc.at[1]])
    waits.append(post.pair(4, [sd.at[0], sd.at[3]], [hd.at[0], hd.at[3]]))
    waits.append(post.pair(5, [sd.at[1], sd.at[2]], [hd.at[1], hd.at[2]]))
    for copy in [tile_at[1], tile_at[2]] + others:
        copy.wait()
    body = keep_gradients(grads, cur, amps, probe, (t0, t1), pos)
    lax.fori_loop(0, 1, body, 0)
    sideways()
    for p in range(2):
        for side in range(2):
            for q, piece in enumerate(unpack(hc[side, p], 96 - 96 * side)):
                at = BORDER + 128 * q
                cur[p, 5 * side, at : at + 128, :] = present(near, 2 + side, piece)
    lax.fori_loop(1, PMAX // GROUP, body, 0)
    for wait in waits:
        wait()
    for p in range(2):
        for k in range(2):
            base = (BORDER + TILE) * k
            for j in range(4):
                cur[p, j + 1, base : base + 32, :] = present(near, k, hv[k, p, :, 128 * j : 128 * j + 128])
            for side in range(2):
                for q, piece in enumerate(unpack(hd[2 * k + side, p], 96 - 96 * side)):
                    cur[p, 5 * side, base + 8 * q : base + 8 * q + 8, :] = present(near, 4 + 2 * k + side, piece)


def first_kernel(count, pos, cur, grads, amps, probe, t0, t1, acc, after, todo):
    acc[...] = jnp.zeros_like(acc)

    def sort(s, amount):
        done = jnp.logical_and(
            rows_within(pos, s, 0), jnp.logical_or(s >= GROUP, columns_within(pos, s, 0))
        )

        @pl.when(done)
        def _():
            place(acc, (grads[s, 0], grads[s, 1]), *corner_of(pos, s))

        @pl.when(jnp.logical_not(done))
        def _():
            todo[amount] = s

        return amount + jnp.where(done, 0, 1)

    amount = lax.fori_loop(0, count[0, 0], sort, jnp.int32(0))
    listed_slots(amount, todo, pos, cur, acc, amps, probe, (t0, t1))
    after[...] = cur[...] + step_of(probe) * acc[...]


def side_sums(near, rc, rm, side, p):
    for rows, value in (
        (pl.ds(0, 64), rc[side, 0, p]),
        (pl.ds(64, TILE - 64), rm[side, p]),
        (pl.ds(TILE, 64), rc[side, 1, p]),
    ):
        yield rows, present(near, 2 + side, unpack_two(value))


def strip_kernel(
    pos, acc, cur_in, amps, probe, t0, t1, grads, cur, rv, rs, rc, rm, sv, ss, sc, sm, send, recv, sems
):
    near = neighbours()
    greet(near)
    same = pltpu.make_async_copy(cur_in, cur, sems.at[0])
    same.start()
    for p in range(2):
        for side in range(2):
            for ud in range(2):
                rows = pl.ds(TILE * ud, 64)
                sc[side, ud, p] = pack_two(seam(acc[p, 4 * side, rows, :], acc[p, 4 * side + 1, rows, :]))
    greeted(near)
    post = Post(near, send, recv)
    corners = post.pair(2, [sc.at[0], sc.at[1]], [rc.at[0], rc.at[1]])
    waits = [
        post.pair(
            0,
            [acc.at[:, pl.ds(2, 2), pl.ds(TILE * ud, 64), :] for ud in range(2)],
            [rv.at[ud, :, pl.ds(1, 2)] for ud in range(2)],
        )
    ]
    for p in range(2):
        for side in range(2):
            sm[side, p] = pack_two(seam(acc[p, 4 * side, 64:TILE, :], acc[p, 4 * side + 1, 64:TILE, :]))
    middle = post.pair(2, [sm.at[0], sm.at[1]], [rm.at[0], rm.at[1]])
    corners()
    lane = lanes(64)
    for p in range(2):
        for ud in range(2):
            rows = pl.ds(TILE * ud, 64)
            west = present(near, 2, unpack_two(rc[0, ud, p]))
            east = present(near, 3, unpack_two(rc[1, ud, p]))
            sv[ud, p, 0] = acc[p, 1, rows, :] + jnp.where(lane < 32, west, 0.0)
            sv[ud, p, 1] = acc[p, 4, rows, :] + jnp.where(lane >= 96, east, 0.0)
            ss[ud, p] = pack_two(seam(acc[p, 0, rows, :] + west, acc[p, 5, rows, :] + east))
    for n, block in ((0, 0), (1, 3)):
        waits.append(
            post.pair(0, [sv.at[ud, :, n] for ud in range(2)], [rv.at[ud, :, block] for ud in range(2)])
        )
    waits.append(post.pair(0, [ss.at[0], ss.at[1]], [rs.at[0], rs.at[1]]))
    same.wait()
    middle()
    step = step_of(probe)
    for p in range(2):
        for side in range(2):
            for rows, value in side_sums(near, rc, rm, side, p):
                lane = lanes(value.shape[0])
                cur[p, 4 * side, rows, :] += step * jnp.where(lane >= 96, value, 0.0)
                cur[p, 4 * side + 1, rows, :] += step * jnp.where(lane < 32, value, 0.0)
    for side in range(2):
        cur[:, 5 * side] = present(near, 2 + side, cur[:, 5 * side])
    lax.fori_loop(0, PMAX // GROUP, keep_gradients(grads, cur, amps, probe, (t0, t1), pos), 0)
    for wait in waits:
        wait()


def second_kernel(
    count, pos, acc_in, cur_in, rv, rs, rc, rm, grads, amps, probe, t0, t1, acc, cur, late, todo
):
    near = neighbours()
    step = step_of(probe)
    del acc_in, cur_in

    def add(p, block, rows, value):
        acc[p, block, rows, :] += value
        cur[p, block, rows, :] += step * value

    for p in range(2):
        for ud in range(2):
            rows = pl.ds(TILE * ud, 64)
            for j in range(4):
                add(p, j + 1, rows, present(near, ud, rv[ud, p, j]))
            sides = present(near, ud, unpack_two(rs[ud, p]))
            lane = lanes(64)
            add(p, 0, rows, jnp.where(lane >= 96, sides, 0.0))
            add(p, 5, rows, jnp.where(lane < 32, sides, 0.0))
        for side in range(2):
            block = 1 + 3 * side
            for rows, value in side_sums(near, rc, rm, side, p):
                lane = lanes(value.shape[0])
                acc[p, block, rows, :] += jnp.where(lane >= 96 if side else lane < 32, value, 0.0)
    for k in range(2):
        rows = pl.ds((BORDER + TILE) * k, BORDER)
        cur[:, :, rows, :] = present(near, k, cur[:, :, rows, :])
        for p in range(2):
            for r in range(2):
                at = pl.ds((BORDER + TILE) * r, BORDER)
                cur[p, 5 * k, at, :] = present(near, 2 + k, cur[p, 5 * k, at, :])
        acc[:, :, rows, :] = jnp.zeros((2, BLOCKS, BORDER, 128), f32)
        acc[:, 5 * k] = jnp.zeros((2, ROWS, 128), f32)
    for k in range(LATE):
        late[k] = PMAX

    def sort(s, carry):
        amount, held = carry
        done = rows_within(pos, s, BORDER)
        inner = jnp.logical_and(rows_within(pos, s, 0), columns_within(pos, s, 0))
        hold = jnp.logical_and(jnp.logical_and(inner, held < LATE), jnp.logical_not(done))

        @pl.when(done)
        def _():
            place(acc, (grads[s, 0], grads[s, 1]), *corner_of(pos, s))

        @pl.when(hold)
        def _():
            late[held] = s

        now = jnp.logical_not(jnp.logical_or(done, hold))

        @pl.when(now)
        def _():
            todo[amount] = s

        return amount + jnp.where(now, 1, 0), held + jnp.where(hold, 1, 0)

    amount, _ = lax.fori_loop(0, count[0, 0], sort, (jnp.int32(0), jnp.int32(0)))
    listed_slots(amount, todo, pos, cur, acc, amps, probe, (t0, t1))


def fold_kernel(pos, late, acc, cur, amps, probe, t0, t1, grads, gv, gc, gd, sc, sd, send, recv):
    near = neighbours()
    greet(near)
    for p in range(2):
        for side in range(2):
            start = 96 - 96 * side
            for ud in range(2):
                base = (BORDER + TILE) * ud
                sd[2 * ud + side, p] = pack(
                    [acc[p, 5 * side, base + 8 * q : base + 8 * q + 8, :] for q in range(4)], start
                )
    greeted(near)
    post = Post(near, send, recv)
    waits = [
        post.pair(
            0,
            [acc.at[:, pl.ds(1, 4), pl.ds((BORDER + TILE) * ud, BORDER), :] for ud in range(2)],
            [gv.at[0], gv.at[1]],
        ),
        post.pair(4, [sd.at[0], sd.at[3]], [gd.at[0], gd.at[3]]),
        post.pair(5, [sd.at[1], sd.at[2]], [gd.at[1], gd.at[2]]),
    ]
    for p in range(2):
        for side in range(2):
            sc[side, p] = pack(
                [acc[p, 5 * side, BORDER + 128 * q : BORDER + 128 * q + 128, :] for q in range(4)], 96 - 96 * side
            )
    waits.append(post.pair(2, [sc.at[0], sc.at[1]], [gc.at[0], gc.at[1]]))

    def body(i, carry):
        slots = [jnp.minimum(late[i * GROUP + k], PMAX - 1) for k in range(GROUP)]
        for k, (a, b) in enumerate(gradients(cur, amps, probe, (t0, t1), pos, slots)):
            grads[i * GROUP + k, 0] = a
            grads[i * GROUP + k, 1] = b
        return carry

    lax.fori_loop(0, LATE // GROUP, body, 0)
    for wait in waits:
        wait()


def last_kernel(pos, late, obj, acc_in, gv, gc, gd, grads, probe, est_out, corr_out, acc, est, sems):
    near = neighbours()
    del acc_in
    step = step_of(probe)

    def put(k, carry):
        s = late[k]

        @pl.when(s < PMAX)
        def _():
            place(acc, (grads[k, 0], grads[k, 1]), *corner_of(pos, s))

        return carry

    lax.fori_loop(0, LATE, put, 0)
    for p in range(2):
        for side in range(2):
            block, start = 1 + 3 * side, 96 * side

            def mine(rows):
                return lanes(rows) >= 96 if side else lanes(rows) < 32

            for q, piece in enumerate(unpack(gc[side, p], start)):
                at = BORDER + 128 * q
                acc[p, block, at : at + 128, :] += jnp.where(mine(128), present(near, 2 + side, piece), 0.0)
            for ud in range(2):
                base = BORDER + (TILE - 32) * ud
                for q, piece in enumerate(unpack(gd[2 * ud + side, p], start)):
                    at = base + 8 * q
                    piece = present(near, 4 + 2 * ud + side, piece)
                    acc[p, block, at : at + 8, :] += jnp.where(mine(8), piece, 0.0)
        for ud in range(2):
            base = BORDER + (TILE - 32) * ud
            for j in range(4):
                acc[p, j + 1, base : base + 32, :] += present(near, ud, gv[ud, p, j])
    stores = []
    inner = pl.ds(BORDER, TILE)
    for j in range(4):
        out = pl.ds(128 * j, 128)
        acc[:, j + 1, inner, :] = step * acc[:, j + 1, inner, :]
        stores.append(pltpu.make_async_copy(acc.at[:, j + 1, inner, :], corr_out.at[:, :, out], sems.at[j]))
        stores[-1].start()
        est[:, j] = obj[:, :, 128 * j : 128 * j + 128] + acc[:, j + 1, inner, :]
        stores.append(pltpu.make_async_copy(est.at[:, j], est_out.at[:, :, out], sems.at[4 + j]))
        stores[-1].start()
    for store in stores:
        store.wait()


VM = pl.BlockSpec(memory_space=pltpu.VMEM)
SM = pl.BlockSpec(memory_space=pltpu.SMEM)
HBM = pl.BlockSpec(memory_space=pltpu.HBM)


def shape(*dims, dtype=f32):
    return jax.ShapeDtypeStruct(dims, dtype)


def params(limit_mib=14, **kw):
    return pltpu.CompilerParams(vmem_limit_bytes=limit_mib * 2**20, **kw)


def remote_params(which):
    return params(collective_id=which, has_side_effects=True)


def on_device(object_field, probe_field, amplitudes, positions, counts):
    tabs = [jnp.asarray(t) for t in tables()]
    dma = pltpu.SemaphoreType.DMA
    tile = shape(2, BLOCKS, ROWS, 128)
    kept = shape(PMAX, 2, PROBE, PROBE)
    far = [
        pltpu.with_memory_space_constraint(x, pltpu.HBM)
        for x in (object_field, amplitudes, probe_field, *tabs)
    ]
    cur, grads, *shared = pl.pallas_call(
        halo_kernel,
        out_shape=[tile, kept] + [jax.ShapeDtypeStruct(x.shape, x.dtype) for x in (amplitudes, probe_field, *tabs)],
        in_specs=[SM] + [HBM] * 5,
        out_specs=[VM] * 6,
        scratch_shapes=[
            pltpu.VMEM((2, 2, 32, TILE), f32),
            pltpu.VMEM((2, 2, 128, 128), f32),
            pltpu.VMEM((4, 2, 8, 128), f32),
            pltpu.VMEM((2, 2, 128, 128), f32),
            pltpu.VMEM((4, 2, 8, 128), f32),
            dma((8,)),
            dma((8,)),
            dma((8,)),
        ],
        compiler_params=remote_params(0),
        name="halo",
    )(positions, *far)
    acc, after = pl.pallas_call(
        first_kernel,
        out_shape=(tile, tile),
        in_specs=[SM, SM] + [VM] * 6,
        out_specs=[VM] * 2,
        scratch_shapes=[pltpu.SMEM((PMAX,), jnp.int32)],
        compiler_params=params(),
        name="first",
    )(counts, positions, cur, grads, *shared)
    strips = ((2, 2, 4, 64, 128), (2, 2, 32, 128), (2, 2, 2, 32, 128), (2, 2, 224, 128))
    grads, cur, *got = pl.pallas_call(
        strip_kernel,
        out_shape=(kept, tile) + tuple(shape(*s) for s in strips),
        in_specs=[SM] + [VM] * 6,
        out_specs=[VM] * 6,
        scratch_shapes=[
            pltpu.VMEM((2, 2, 2, 64, 128), f32),
            pltpu.VMEM((2, 2, 32, 128), f32),
            pltpu.VMEM((2, 2, 2, 32, 128), f32),
            pltpu.VMEM((2, 2, 224, 128), f32),
            dma((12,)),
            dma((12,)),
            dma((1,)),
        ],
        compiler_params=remote_params(1),
        name="strips",
    )(positions, acc, after, *shared)
    acc, cur, late = pl.pallas_call(
        second_kernel,
        out_shape=(tile, tile, shape(LATE, dtype=jnp.int32)),
        in_specs=[SM, SM] + [VM] * 11,
        out_specs=[VM, VM, SM],
        scratch_shapes=[pltpu.SMEM((PMAX,), jnp.int32)],
        input_output_aliases={2: 0, 3: 1},
        compiler_params=params(),
        name="second",
    )(counts, positions, acc, cur, *got, grads, *shared)
    folds = ((2, 2, 4, 32, 128), (2, 2, 128, 128), (4, 2, 8, 128))
    grads, *got = pl.pallas_call(
        fold_kernel,
        out_shape=(shape(LATE, 2, PROBE, PROBE),) + tuple(shape(*s) for s in folds),
        in_specs=[SM, SM] + [VM] * 6,
        out_specs=[VM] * 4,
        scratch_shapes=[
            pltpu.VMEM((2, 2, 128, 128), f32),
            pltpu.VMEM((4, 2, 8, 128), f32),
            dma((8,)),
            dma((8,)),
        ],
        compiler_params=remote_params(2),
        name="folds",
    )(positions, late, acc, cur, *shared)
    return pl.pallas_call(
        last_kernel,
        out_shape=(shape(2, TILE, TILE), shape(2, TILE, TILE), tile),
        in_specs=[SM, SM] + [VM] * 7,
        out_specs=[HBM, HBM, VM],
        scratch_shapes=[pltpu.VMEM((2, 4, TILE, 128), f32), dma((8,))],
        input_output_aliases={3: 2},
        compiler_params=params(),
        name="last",
    )(positions, late, object_field, acc, *got, grads, shared[1])[:2]


def solution(mesh):
    placed = (
        P(None, "row", "col"),
        P(),
        P("row", None, "col"),
        P("row", "col", None, None),
        P("row", "col"),
    )
    return jax.shard_map(
        on_device,
        mesh=mesh,
        in_specs=placed,
        out_specs=(P(None, "row", "col"), P(None, "row", "col")),
        check_vma=False,
    )
```

```python
import functools

import jax
import jax.numpy as jnp
import ml_dtypes
import numpy as np
from jax import lax
from jax.experimental import pallas as pl
from jax.experimental.pallas import tpu as pltpu
from jax.sharding import PartitionSpec as P

BORDER = 32
PROBE = 128
TILE = 512
PMAX = 24
ROWS = TILE + 2 * BORDER
BLOCKS = 6
GROUP = 8
smoothing = 0.5
step_gain = 0.5
f32 = jnp.float32
bf16 = jnp.bfloat16
MESH = pl.DeviceIdType.MESH

DIRS = ((-1, 0), (1, 0), (0, -1), (0, 1), (-1, -1), (-1, 1), (1, -1), (1, 1))
OPP = (1, 0, 3, 2, 7, 6, 5, 4)


def tables():
    n = np.arange(PROBE)
    angle = 2.0 * np.pi / PROBE * (n[:, None] * n[None, :] % PROBE)
    real, imag = np.cos(angle) / np.sqrt(PROBE), -np.sin(angle) / np.sqrt(PROBE)
    whole = np.block([[real, -imag], [imag, real]]).astype(np.float32)

    def halves(matrix):
        high = matrix.astype(ml_dtypes.bfloat16)
        return high, (matrix - high.astype(np.float32)).astype(ml_dtypes.bfloat16)

    return np.stack(halves(whole)), np.stack(halves(whole.T.copy()))


def split(value):
    high = value.astype(bf16)
    return high, (value - high.astype(f32)).astype(bf16)


def dot(a, b):
    return jnp.dot(a, b, preferred_element_type=f32)


def left(table, pairs):
    parts = [split(jnp.concatenate([a, b], 0)) for a, b in pairs]
    high = jnp.concatenate([p[0] for p in parts], 1)
    low = jnp.concatenate([p[1] for p in parts], 1)
    wide = jnp.concatenate([table[0], table[0], table[1]], 1)
    out = dot(wide, jnp.concatenate([high, low, high], 0))
    n = PROBE
    return [(out[:n, n * k : n * k + n], out[n:, n * k : n * k + n]) for k in range(len(pairs))]


def right(table, pairs):
    parts = [split(jnp.concatenate([a, b], 1)) for a, b in pairs]
    high = jnp.concatenate([p[0] for p in parts], 0)
    low = jnp.concatenate([p[1] for p in parts], 0)
    tall = jnp.concatenate([table[0], table[0], table[1]], 0)
    out = dot(jnp.concatenate([high, low, high], 1), tall)
    n = PROBE
    return [(out[n * k : n * k + n, :n], out[n * k : n * k + n, n:]) for k in range(len(pairs))]


def lanes(rows=PROBE):
    return lax.broadcasted_iota(jnp.int32, (rows, 128), 1)


def cut(cur, row, col):
    block, lane = col >> 7, col & 127
    out = []
    for p in range(2):
        a = cur[p, block, pl.ds(row, PROBE), :]
        b = cur[p, block + 1, pl.ds(row, PROBE), :]
        out.append(pltpu.roll(jnp.where(lanes() >= lane, a, b), (128 - lane) & 127, 1))
    return out


def place(acc, grad, row, col):
    block, lane = col >> 7, col & 127
    for p in range(2):
        g = pltpu.roll(grad[p], lane, 1)
        acc[p, block, pl.ds(row, PROBE), :] += jnp.where(lanes() >= lane, g, 0.0)
        acc[p, block + 1, pl.ds(row, PROBE), :] += jnp.where(lanes() >= lane, 0.0, g)


def gradients(cur, amps, probe, tabs, pos, slots, scale=None):
    forward, backward = tabs
    pr, pi = probe[0], probe[1]
    pairs = []
    for s in slots:
        a, b = cut(cur, *corner_of(pos, s))
        pairs.append((pr * a - pi * b, pr * b + pi * a))
    waves = left(forward, right(backward, pairs))
    shrunk = []
    for k, ((a, b), s) in enumerate(zip(waves, slots)):
        gain = amps[s] * lax.rsqrt(a * a + b * b + smoothing) - 1.0
        if scale is not None:
            gain = gain * scale[k]
        shrunk.append((a * gain, b * gain))
    backs = right(forward, left(backward, shrunk))
    return [(pr * a + pi * b, pr * b - pi * a) for a, b in backs]


def corner_of(pos, s):
    return pos[0, 0, 0, s] + BORDER, pos[0, 0, 1, s] + 128


def within(start, margin):
    return jnp.logical_and(start >= margin, start <= TILE - PROBE - margin)


def rows_within(pos, s, margin):
    return within(pos[0, 0, 0, s], margin)


def columns_within(pos, s, margin):
    return within(pos[0, 0, 1, s], margin)


def listed_slots(amount, todo, pos, cur, acc, amps, probe, tabs):
    def some(start, size):
        at = [start + k for k in range(size)]
        slots = [jnp.where(j < amount, todo[j], 0) for j in at]
        scale = [jnp.where(j < amount, 1.0, 0.0) for j in at]
        grads = gradients(cur, amps, probe, tabs, pos, slots, scale)
        for grad, s in zip(grads, slots):
            place(acc, grad, *corner_of(pos, s))

    def body(i, carry):
        some(i * GROUP, GROUP)
        return carry

    full = lax.div(amount + GROUP // 2 - 1, GROUP)
    lax.fori_loop(0, full, body, 0)

    @pl.when(amount > full * GROUP)
    def _():
        some(full * GROUP, GROUP // 2)


def step_of(probe):
    return step_gain / (jnp.max(probe[0] * probe[0] + probe[1] * probe[1]) + 1e-06)


def neighbours():
    rows, cols = lax.axis_size("row"), lax.axis_size("col")
    row, col = lax.axis_index("row"), lax.axis_index("col")
    out = []
    for dr, dc in DIRS:
        there = None
        for cond in (
            [row > 0] if dr < 0 else [row < rows - 1] if dr > 0 else []
        ) + ([col > 0] if dc < 0 else [col < cols - 1] if dc > 0 else []):
            there = cond if there is None else jnp.logical_and(there, cond)
        out.append((there, (row + dr, col + dc)))
    return out


def crossing():
    cols, row, col = lax.axis_size("col"), lax.axis_index("row"), lax.axis_index("col")
    middle = (cols // 2 - 1, cols // 2)
    outer = (cols - 1, 0)
    in_middle = jnp.logical_or(col == middle[0], col == middle[1])
    in_outer = jnp.logical_or(col == outer[0], col == outer[1])
    return row, col, middle, outer, in_middle, in_outer


def greet(near):
    barrier = pltpu.get_barrier_semaphore()

    def hail(there, where):
        @pl.when(there)
        def _():
            pl.semaphore_signal(barrier, inc=1, device_id=where, device_id_type=MESH)

    for there, where in near:
        hail(there, where)
    row, _, middle, outer, in_middle, in_outer = crossing()
    for k in range(2):
        hail(in_middle, (row, outer[k]))
        hail(in_outer, (row, middle[k]))


def greeted(near):
    *_, in_middle, in_outer = crossing()
    total = 2 * jnp.logical_or(in_middle, in_outer).astype(jnp.int32)
    for there, _ in near:
        total = total + there.astype(jnp.int32)
    pl.semaphore_wait(pltpu.get_barrier_semaphore(), total)


def remote(k, near, source, target, send, recv, n):
    return pltpu.make_async_remote_copy(
        src_ref=source,
        dst_ref=target,
        send_sem=send.at[n],
        recv_sem=recv.at[n],
        device_id=near[k][1],
        device_id_type=MESH,
    )


class Post:
    def __init__(self, near, send, recv):
        self.near, self.send, self.recv = near, send, recv
        self.count, self.waits = 0, []

    def pair(self, k, outs, intos):
        for i, way in enumerate((k, OPP[k])):
            n = self.count + i
            @pl.when(self.near[way][0])
            def _(i=i, way=way, n=n):
                remote(way, self.near, outs[i], intos[1 - i], self.send, self.recv, n).start()

        def wait(base=self.count):
            for i, way in enumerate((k, OPP[k])):
                @pl.when(self.near[way][0])
                def _(i=i, way=way):
                    remote(way, self.near, outs[i], intos[i], self.send, self.recv, base + i).wait_send()
                    remote(way, self.near, outs[i], intos[i], self.send, self.recv, base + 1 - i).wait_recv()

        self.count += 2
        return wait

    def sideways(self, outs, intos, hop, hop_sem):
        row, col, middle, outer, *_ = crossing()
        n = self.count

        def copy(source, target, i, sem, where):
            return pltpu.make_async_remote_copy(
                src_ref=source,
                dst_ref=target,
                send_sem=self.send.at[n + i],
                recv_sem=sem,
                device_id=(row, where),
                device_id_type=MESH,
            )

        def direct(i):
            there, (_, where) = self.near[2 + i]
            cross = col == middle[1 - i]
            return jnp.logical_and(there, jnp.logical_not(cross)), cross, where

        for i in range(2):
            there, cross, where = direct(i)

            @pl.when(there)
            def _(i=i, where=where):
                copy(outs[i], intos[1 - i], i, self.recv.at[n + i], where).start()

            @pl.when(cross)
            def _(i=i):
                copy(outs[i], hop, i, hop_sem, outer[1 - i]).start()

        def forward():
            for i in range(2):
                @pl.when(col == outer[1 - i])
                def _(i=i):
                    copy(outs[i], hop, i, hop_sem, middle[i]).wait_recv()
                    copy(hop, intos[1 - i], i, self.recv.at[n + i], middle[i]).start()

        def wait():
            for i in range(2):
                there, cross, where = direct(i)

                @pl.when(jnp.logical_or(there, cross))
                def _(i=i, where=where):
                    copy(outs[i], intos[1 - i], i, self.recv.at[n + i], where).wait_send()

                @pl.when(col == outer[1 - i])
                def _(i=i):
                    copy(hop, intos[1 - i], i, self.recv.at[n + i], middle[i]).wait_send()

                @pl.when(self.near[2 + i][0])
                def _(i=i, where=where):
                    copy(outs[i], intos[i], 1 - i, self.recv.at[n + 1 - i], where).wait_recv()

        self.count += 2
        return forward, wait


def halves(ref, rows):
    return [[ref.at[side, :, pl.ds(rows * h, rows)] for side in range(2)] for h in range(2)]


def groups_before():
    *_, in_middle, _ = crossing()
    late = in_middle.astype(jnp.int32)
    return 1 + late, late


def pack(pieces, start):
    lane = lanes(pieces[0].shape[0])
    out = None
    for q, piece in enumerate(pieces):
        turn = (32 * q - start) % 128
        turned = pltpu.roll(piece, turn, 1) if turn else piece
        out = turned if out is None else jnp.where(lane >= 32 * q, turned, out)
    return out


def unpack(value, start):
    turns = [(start - 32 * q) % 128 for q in range(4)]
    return [pltpu.roll(value, turn, 1) if turn else value for turn in turns]


def pack_two(value):
    half = value.shape[0] // 2
    lane = lanes(half)
    middle = jnp.logical_and(lane >= 32, lane < 96)
    return jnp.where(middle, pltpu.roll(value[half:], 64, 1), value[:half])


def unpack_two(value):
    return jnp.concatenate([value, pltpu.roll(value, 64, 1)], 0)


def seam(a, b):
    return jnp.where(lanes(a.shape[0]) >= 96, a, b)


def present(near, k, value):
    return jnp.where(near[k][0], value, 0.0)


LATE = 8


def keep_gradients(grads, cur, amps, probe, tabs, pos):
    def body(i, carry):
        slots = [i * GROUP + k for k in range(GROUP)]
        for s, (a, b) in zip(slots, gradients(cur, amps, probe, tabs, pos, slots)):
            grads[s, 0] = a
            grads[s, 1] = b
        return carry

    return body


def halo_kernel(
    pos, obj, amps_far, probe_far, t0_far, t1_far, cur, acc, grads, amps, probe, t0, t1, hv, hc, hd, sc, sd, hop, send, recv, hop_sem, sems
):
    near = neighbours()
    greet(near)
    tile_at = [
        pltpu.make_async_copy(
            obj.at[:, :, pl.ds(128 * j, 128)], cur.at[:, j + 1, pl.ds(BORDER, TILE), :], sems.at[j]
        )
        for j in range(4)
    ]
    others = [
        pltpu.make_async_copy(there, here, sems.at[4 + n])
        for n, (there, here) in enumerate(((probe_far, probe), (t0_far, t0), (t1_far, t1), (amps_far, amps)))
    ]
    for copy in [tile_at[j] for j in (0, 3, 1, 2)] + others:
        copy.start()
    zeros = jnp.zeros((2, BLOCKS, BORDER, 128), f32)
    cur[:, :, 0:BORDER, :] = zeros
    cur[:, :, BORDER + TILE :, :] = zeros
    cur[:, 0] = jnp.zeros((2, ROWS, 128), f32)
    cur[:, 5] = jnp.zeros((2, ROWS, 128), f32)
    acc[...] = jnp.zeros_like(acc)
    greeted(near)
    post = Post(near, send, recv)
    waits = [post.pair(0, [obj.at[:, pl.ds(0, 32), :], obj.at[:, pl.ds(TILE - 32, 32), :]], [hv.at[0], hv.at[1]])]
    for side in range(2):
        tile_at[3 * side].wait()
        block, start = 1 + 3 * side, 96 * side
        for p in range(2):
            sc[side, p] = pack(
                [cur[p, block, BORDER + 128 * q : BORDER + 128 * q + 128, :] for q in range(4)], start
            )
            for ud in range(2):
                base = BORDER + (TILE - 32) * ud
                sd[2 * ud + side, p] = pack(
                    [cur[p, block, base + 8 * q : base + 8 * q + 8, :] for q in range(4)], start
                )
    outs, intos = halves(sc, 64), halves(hc, 64)
    forward, over = post.sideways(outs[1], intos[1], hop, hop_sem.at[0])
    straight = post.pair(2, outs[0], intos[0])
    waits.append(post.pair(4, [sd.at[0], sd.at[3]], [hd.at[0], hd.at[3]]))
    waits.append(post.pair(5, [sd.at[1], sd.at[2]], [hd.at[1], hd.at[2]]))
    for copy in [tile_at[1], tile_at[2]] + others:
        copy.wait()
    body = keep_gradients(grads, cur, amps, probe, (t0, t1), pos)
    before, _ = groups_before()
    lax.fori_loop(0, 1, body, 0)
    forward()
    lax.fori_loop(1, before, body, 0)
    straight()
    over()
    for p in range(2):
        for side in range(2):
            for q, piece in enumerate(unpack(hc[side, p], 96 - 96 * side)):
                at = BORDER + 128 * q
                cur[p, 5 * side, at : at + 128, :] = present(near, 2 + side, piece)
    lax.fori_loop(before, PMAX // GROUP, body, 0)
    for wait in waits:
        wait()
    for p in range(2):
        for k in range(2):
            base = (BORDER + TILE) * k
            for j in range(4):
                cur[p, j + 1, base : base + 32, :] = present(near, k, hv[k, p, :, 128 * j : 128 * j + 128])
            for side in range(2):
                for q, piece in enumerate(unpack(hd[2 * k + side, p], 96 - 96 * side)):
                    cur[p, 5 * side, base + 8 * q : base + 8 * q + 8, :] = present(near, 4 + 2 * k + side, piece)


def first_kernel(count, pos, acc_in, cur, grads, amps, probe, t0, t1, acc, todo):
    del acc_in
    early = GROUP * groups_before()[0]

    def sort(s, amount):
        done = jnp.logical_and(
            rows_within(pos, s, 0), jnp.logical_or(s >= early, columns_within(pos, s, 0))
        )

        @pl.when(done)
        def _():
            place(acc, (grads[s, 0], grads[s, 1]), *corner_of(pos, s))

        @pl.when(jnp.logical_not(done))
        def _():
            todo[amount] = s

        return amount + jnp.where(done, 0, 1)

    amount = lax.fori_loop(0, count[0, 0], sort, jnp.int32(0))
    listed_slots(amount, todo, pos, cur, acc, amps, probe, (t0, t1))


def side_sums(near, rc, rm, side, p):
    for rows, value in (
        (pl.ds(0, 64), rc[side, 0, p]),
        (pl.ds(64, TILE - 64), rm[side, p]),
        (pl.ds(TILE, 64), rc[side, 1, p]),
    ):
        yield rows, present(near, 2 + side, unpack_two(value))


def strip_kernel(
    pos, acc, cur_in, amps, probe, t0, t1, grads, cur, rv, rs, rc, rm, sv, ss, sc, sm, hop, send, recv, hop_sem
):
    near = neighbours()
    greet(near)
    for p in range(2):
        for side in range(2):
            for ud in range(2):
                rows = pl.ds(TILE * ud, 64)
                sc[side, ud, p] = pack_two(seam(acc[p, 4 * side, rows, :], acc[p, 4 * side + 1, rows, :]))
    greeted(near)
    post = Post(near, send, recv)
    corners = post.pair(2, [sc.at[0], sc.at[1]], [rc.at[0], rc.at[1]])
    waits = [
        post.pair(
            0,
            [acc.at[:, pl.ds(2, 2), pl.ds(TILE * ud, 64), :] for ud in range(2)],
            [rv.at[ud, :, pl.ds(1, 2)] for ud in range(2)],
        )
    ]
    for p in range(2):
        for side in range(2):
            sm[side, p] = pack_two(seam(acc[p, 4 * side, 64:TILE, :], acc[p, 4 * side + 1, 64:TILE, :]))
    outs, intos = halves(sm, 112), halves(rm, 112)
    forward, over = post.sideways(outs[1], intos[1], hop, hop_sem.at[0])
    straight = post.pair(2, outs[0], intos[0])
    step = step_of(probe)
    cur[...] = cur_in[...] + step * acc[...]
    corners()
    lane = lanes(64)
    for p in range(2):
        for ud in range(2):
            rows = pl.ds(TILE * ud, 64)
            west = present(near, 2, unpack_two(rc[0, ud, p]))
            east = present(near, 3, unpack_two(rc[1, ud, p]))
            sv[ud, p, 0] = acc[p, 1, rows, :] + jnp.where(lane < 32, west, 0.0)
            sv[ud, p, 1] = acc[p, 4, rows, :] + jnp.where(lane >= 96, east, 0.0)
            ss[ud, p] = pack_two(seam(acc[p, 0, rows, :] + west, acc[p, 5, rows, :] + east))
    for n, block in ((0, 0), (1, 3)):
        waits.append(
            post.pair(0, [sv.at[ud, :, n] for ud in range(2)], [rv.at[ud, :, block] for ud in range(2)])
        )
    waits.append(post.pair(0, [ss.at[0], ss.at[1]], [rs.at[0], rs.at[1]]))
    for side in range(2):
        cur[:, 5 * side] = present(near, 2 + side, cur[:, 5 * side])
    forward()
    body = keep_gradients(grads, cur, amps, probe, (t0, t1), pos)
    _, before = groups_before()
    lax.fori_loop(0, before, body, 0)
    straight()
    over()
    for p in range(2):
        for side in range(2):
            for rows, value in side_sums(near, rc, rm, side, p):
                lane = lanes(value.shape[0])
                for block, mine in ((4 * side, lane >= 96), (4 * side + 1, lane < 32)):
                    cur[p, block, rows, :] += step * jnp.where(mine, value, 0.0)
    lax.fori_loop(before, PMAX // GROUP, body, 0)
    for wait in waits:
        wait()


def second_kernel(
    count, pos, acc_in, cur_in, rv, rs, rc, rm, grads, amps, probe, t0, t1, acc, cur, late, todo
):
    near = neighbours()
    step = step_of(probe)
    del acc_in, cur_in
    early = GROUP * groups_before()[1]

    def add(p, block, rows, value):
        acc[p, block, rows, :] += value
        cur[p, block, rows, :] += step * value

    for p in range(2):
        for ud in range(2):
            rows = pl.ds(TILE * ud, 64)
            for j in range(4):
                add(p, j + 1, rows, present(near, ud, rv[ud, p, j]))
            sides = present(near, ud, unpack_two(rs[ud, p]))
            lane = lanes(64)
            add(p, 0, rows, jnp.where(lane >= 96, sides, 0.0))
            add(p, 5, rows, jnp.where(lane < 32, sides, 0.0))
        for side in range(2):
            block = 1 + 3 * side
            for rows, value in side_sums(near, rc, rm, side, p):
                lane = lanes(value.shape[0])
                acc[p, block, rows, :] += jnp.where(lane >= 96 if side else lane < 32, value, 0.0)
    for k in range(2):
        rows = pl.ds((BORDER + TILE) * k, BORDER)
        cur[:, :, rows, :] = present(near, k, cur[:, :, rows, :])
        for p in range(2):
            for r in range(2):
                at = pl.ds((BORDER + TILE) * r, BORDER)
                cur[p, 5 * k, at, :] = present(near, 2 + k, cur[p, 5 * k, at, :])
        acc[:, :, rows, :] = jnp.zeros((2, BLOCKS, BORDER, 128), f32)
        acc[:, 5 * k] = jnp.zeros((2, ROWS, 128), f32)
    for k in range(LATE):
        late[k] = PMAX

    def sort(s, carry):
        amount, held = carry
        done = jnp.logical_and(
            rows_within(pos, s, BORDER), jnp.logical_or(s >= early, columns_within(pos, s, BORDER))
        )
        inner = jnp.logical_and(rows_within(pos, s, 0), columns_within(pos, s, 0))
        hold = jnp.logical_and(jnp.logical_and(inner, held < LATE), jnp.logical_not(done))

        @pl.when(done)
        def _():
            place(acc, (grads[s, 0], grads[s, 1]), *corner_of(pos, s))

        @pl.when(hold)
        def _():
            late[held] = s

        now = jnp.logical_not(jnp.logical_or(done, hold))

        @pl.when(now)
        def _():
            todo[amount] = s

        return amount + jnp.where(now, 1, 0), held + jnp.where(hold, 1, 0)

    amount, _ = lax.fori_loop(0, count[0, 0], sort, (jnp.int32(0), jnp.int32(0)))
    listed_slots(amount, todo, pos, cur, acc, amps, probe, (t0, t1))


def fold_kernel(pos, late, acc, cur, amps, probe, t0, t1, grads, gv, gc, gd, sc, sd, hop, send, recv, hop_sem):
    near = neighbours()
    greet(near)
    for p in range(2):
        for side in range(2):
            start = 96 - 96 * side
            for ud in range(2):
                base = (BORDER + TILE) * ud
                sd[2 * ud + side, p] = pack(
                    [acc[p, 5 * side, base + 8 * q : base + 8 * q + 8, :] for q in range(4)], start
                )
    greeted(near)
    post = Post(near, send, recv)
    waits = [
        post.pair(
            0,
            [acc.at[:, pl.ds(1, 4), pl.ds((BORDER + TILE) * ud, BORDER), :] for ud in range(2)],
            [gv.at[0], gv.at[1]],
        ),
        post.pair(4, [sd.at[0], sd.at[3]], [gd.at[0], gd.at[3]]),
        post.pair(5, [sd.at[1], sd.at[2]], [gd.at[1], gd.at[2]]),
    ]
    for p in range(2):
        for side in range(2):
            sc[side, p] = pack(
                [acc[p, 5 * side, BORDER + 128 * q : BORDER + 128 * q + 128, :] for q in range(4)], 96 - 96 * side
            )
    outs, intos = halves(sc, 64), halves(gc, 64)
    forward, over = post.sideways(outs[1], intos[1], hop, hop_sem.at[0])
    waits.append(post.pair(2, outs[0], intos[0]))
    waits.append(over)

    def body(i, carry):
        slots = [jnp.minimum(late[i * GROUP + k], PMAX - 1) for k in range(GROUP)]
        for k, (a, b) in enumerate(gradients(cur, amps, probe, (t0, t1), pos, slots)):
            grads[i * GROUP + k, 0] = a
            grads[i * GROUP + k, 1] = b
        return carry

    lax.fori_loop(0, LATE // GROUP, body, 0)
    forward()
    for wait in waits:
        wait()


def last_kernel(pos, late, obj, acc_in, gv, gc, gd, grads, probe, est_out, corr_out, acc, est, sems):
    near = neighbours()
    del acc_in
    step = step_of(probe)

    def put(k, carry):
        s = late[k]

        @pl.when(s < PMAX)
        def _():
            place(acc, (grads[k, 0], grads[k, 1]), *corner_of(pos, s))

        return carry

    lax.fori_loop(0, LATE, put, 0)
    for p in range(2):
        for side in range(2):
            block, start = 1 + 3 * side, 96 * side

            def mine(rows):
                return lanes(rows) >= 96 if side else lanes(rows) < 32

            for q, piece in enumerate(unpack(gc[side, p], start)):
                at = BORDER + 128 * q
                acc[p, block, at : at + 128, :] += jnp.where(mine(128), present(near, 2 + side, piece), 0.0)
            for ud in range(2):
                base = BORDER + (TILE - 32) * ud
                for q, piece in enumerate(unpack(gd[2 * ud + side, p], start)):
                    at = base + 8 * q
                    piece = present(near, 4 + 2 * ud + side, piece)
                    acc[p, block, at : at + 8, :] += jnp.where(mine(8), piece, 0.0)
        for ud in range(2):
            base = BORDER + (TILE - 32) * ud
            for j in range(4):
                acc[p, j + 1, base : base + 32, :] += present(near, ud, gv[ud, p, j])
    stores = []
    inner = pl.ds(BORDER, TILE)
    for j in range(4):
        out = pl.ds(128 * j, 128)
        acc[:, j + 1, inner, :] = step * acc[:, j + 1, inner, :]
        stores.append(pltpu.make_async_copy(acc.at[:, j + 1, inner, :], corr_out.at[:, :, out], sems.at[j]))
        stores[-1].start()
        est[:, j] = obj[:, :, 128 * j : 128 * j + 128] + acc[:, j + 1, inner, :]
        stores.append(pltpu.make_async_copy(est.at[:, j], est_out.at[:, :, out], sems.at[4 + j]))
        stores[-1].start()
    for store in stores:
        store.wait()


VM = pl.BlockSpec(memory_space=pltpu.VMEM)
SM = pl.BlockSpec(memory_space=pltpu.SMEM)
HBM = pl.BlockSpec(memory_space=pltpu.HBM)


def shape(*dims, dtype=f32):
    return jax.ShapeDtypeStruct(dims, dtype)


def params(limit_mib=14, **kw):
    return pltpu.CompilerParams(vmem_limit_bytes=limit_mib * 2**20, **kw)


def remote_params(which):
    return params(collective_id=which, has_side_effects=True)


def on_device(object_field, probe_field, amplitudes, positions, counts):
    tabs = [jnp.asarray(t) for t in tables()]
    dma = pltpu.SemaphoreType.DMA
    tile = shape(2, BLOCKS, ROWS, 128)
    kept = shape(PMAX, 2, PROBE, PROBE)
    far = [
        pltpu.with_memory_space_constraint(x, pltpu.HBM)
        for x in (object_field, amplitudes, probe_field, *tabs)
    ]
    cur, acc, grads, *shared = pl.pallas_call(
        halo_kernel,
        out_shape=[tile, tile, kept] + [jax.ShapeDtypeStruct(x.shape, x.dtype) for x in (amplitudes, probe_field, *tabs)],
        in_specs=[SM] + [HBM] * 5,
        out_specs=[VM] * 7,
        scratch_shapes=[
            pltpu.VMEM((2, 2, 32, TILE), f32),
            pltpu.VMEM((2, 2, 128, 128), f32),
            pltpu.VMEM((4, 2, 8, 128), f32),
            pltpu.VMEM((2, 2, 128, 128), f32),
            pltpu.VMEM((4, 2, 8, 128), f32),
            pltpu.VMEM((2, 64, 128), f32),
            dma((10,)),
            dma((10,)),
            dma((1,)),
            dma((8,)),
        ],
        compiler_params=remote_params(0),
        name="halo",
    )(positions, *far)
    acc = pl.pallas_call(
        first_kernel,
        out_shape=tile,
        in_specs=[SM, SM] + [VM] * 7,
        out_specs=VM,
        scratch_shapes=[pltpu.SMEM((PMAX,), jnp.int32)],
        input_output_aliases={2: 0},
        compiler_params=params(),
        name="first",
    )(counts, positions, acc, cur, grads, *shared)
    strips = ((2, 2, 4, 64, 128), (2, 2, 32, 128), (2, 2, 2, 32, 128), (2, 2, 224, 128))
    grads, cur, *got = pl.pallas_call(
        strip_kernel,
        out_shape=(kept, tile) + tuple(shape(*s) for s in strips),
        in_specs=[SM] + [VM] * 6,
        out_specs=[VM] * 6,
        scratch_shapes=[
            pltpu.VMEM((2, 2, 2, 64, 128), f32),
            pltpu.VMEM((2, 2, 32, 128), f32),
            pltpu.VMEM((2, 2, 2, 32, 128), f32),
            pltpu.VMEM((2, 2, 224, 128), f32),
            pltpu.VMEM((2, 112, 128), f32),
            dma((14,)),
            dma((14,)),
            dma((1,)),
        ],
        compiler_params=remote_params(1),
        name="strips",
    )(positions, acc, cur, *shared)
    acc, cur, late = pl.pallas_call(
        second_kernel,
        out_shape=(tile, tile, shape(LATE, dtype=jnp.int32)),
        in_specs=[SM, SM] + [VM] * 11,
        out_specs=[VM, VM, SM],
        scratch_shapes=[pltpu.SMEM((PMAX,), jnp.int32)],
        input_output_aliases={2: 0, 3: 1},
        compiler_params=params(),
        name="second",
    )(counts, positions, acc, cur, *got, grads, *shared)
    folds = ((2, 2, 4, 32, 128), (2, 2, 128, 128), (4, 2, 8, 128))
    grads, *got = pl.pallas_call(
        fold_kernel,
        out_shape=(shape(LATE, 2, PROBE, PROBE),) + tuple(shape(*s) for s in folds),
        in_specs=[SM, SM] + [VM] * 6,
        out_specs=[VM] * 4,
        scratch_shapes=[
            pltpu.VMEM((2, 2, 128, 128), f32),
            pltpu.VMEM((4, 2, 8, 128), f32),
            pltpu.VMEM((2, 64, 128), f32),
            dma((10,)),
            dma((10,)),
            dma((1,)),
        ],
        compiler_params=remote_params(2),
        name="folds",
    )(positions, late, acc, cur, *shared)
    return pl.pallas_call(
        last_kernel,
        out_shape=(shape(2, TILE, TILE), shape(2, TILE, TILE), tile),
        in_specs=[SM, SM] + [VM] * 7,
        out_specs=[HBM, HBM, VM],
        scratch_shapes=[pltpu.VMEM((2, 4, TILE, 128), f32), dma((8,))],
        input_output_aliases={3: 2},
        compiler_params=params(),
        name="last",
    )(positions, late, object_field, acc, *got, grads, shared[1])[:2]


def solution(mesh):
    placed = (
        P(None, "row", "col"),
        P(),
        P("row", None, "col"),
        P("row", "col", None, None),
        P("row", "col"),
    )
    return jax.shard_map(
        on_device,
        mesh=mesh,
        in_specs=placed,
        out_specs=(P(None, "row", "col"), P(None, "row", "col")),
        check_vma=False,
    )
```

```python
import functools

import jax
import jax.numpy as jnp
import ml_dtypes
import numpy as np
from jax import lax
from jax.experimental import pallas as pl
from jax.experimental.pallas import tpu as pltpu
from jax.sharding import PartitionSpec as P

BORDER = 32
PROBE = 128
TILE = 512
PMAX = 24
ROWS = TILE + 2 * BORDER
BLOCKS = 6
GROUP = 8
smoothing = 0.5
step_gain = 0.5
f32 = jnp.float32
bf16 = jnp.bfloat16
MESH = pl.DeviceIdType.MESH

DIRS = ((-1, 0), (1, 0), (0, -1), (0, 1), (-1, -1), (-1, 1), (1, -1), (1, 1))
OPP = (1, 0, 3, 2, 7, 6, 5, 4)


def tables():
    n = np.arange(PROBE)
    angle = 2.0 * np.pi / PROBE * (n[:, None] * n[None, :] % PROBE)
    real, imag = np.cos(angle) / np.sqrt(PROBE), -np.sin(angle) / np.sqrt(PROBE)
    whole = np.block([[real, -imag], [imag, real]]).astype(np.float32)

    def halves(matrix):
        high = matrix.astype(ml_dtypes.bfloat16)
        return high, (matrix - high.astype(np.float32)).astype(ml_dtypes.bfloat16)

    return np.stack(halves(whole)), np.stack(halves(whole.T.copy()))


def split(value):
    high = value.astype(bf16)
    return high, (value - high.astype(f32)).astype(bf16)


def dot(a, b):
    return jnp.dot(a, b, preferred_element_type=f32)


def left(table, pairs):
    parts = [split(jnp.concatenate([a, b], 0)) for a, b in pairs]
    high = jnp.concatenate([p[0] for p in parts], 1)
    low = jnp.concatenate([p[1] for p in parts], 1)
    wide = jnp.concatenate([table[0], table[0], table[1]], 1)
    out = dot(wide, jnp.concatenate([high, low, high], 0))
    n = PROBE
    return [(out[:n, n * k : n * k + n], out[n:, n * k : n * k + n]) for k in range(len(pairs))]


def right(table, pairs):
    parts = [split(jnp.concatenate([a, b], 1)) for a, b in pairs]
    high = jnp.concatenate([p[0] for p in parts], 0)
    low = jnp.concatenate([p[1] for p in parts], 0)
    tall = jnp.concatenate([table[0], table[0], table[1]], 0)
    out = dot(jnp.concatenate([high, low, high], 1), tall)
    n = PROBE
    return [(out[n * k : n * k + n, :n], out[n * k : n * k + n, n:]) for k in range(len(pairs))]


def lanes(rows=PROBE):
    return lax.broadcasted_iota(jnp.int32, (rows, 128), 1)


def cut(cur, row, col):
    block, lane = col >> 7, col & 127
    out = []
    for p in range(2):
        a = cur[p, block, pl.ds(row, PROBE), :]
        b = cur[p, block + 1, pl.ds(row, PROBE), :]
        out.append(pltpu.roll(jnp.where(lanes() >= lane, a, b), (128 - lane) & 127, 1))
    return out


def place(acc, grad, row, col):
    block, lane = col >> 7, col & 127
    for p in range(2):
        g = pltpu.roll(grad[p], lane, 1)
        acc[p, block, pl.ds(row, PROBE), :] += jnp.where(lanes() >= lane, g, 0.0)
        acc[p, block + 1, pl.ds(row, PROBE), :] += jnp.where(lanes() >= lane, 0.0, g)


def gradients(cur, amps, probe, tabs, pos, slots, scale=None):
    forward, backward = tabs
    pr, pi = probe[0], probe[1]
    pairs = []
    for s in slots:
        a, b = cut(cur, *corner_of(pos, s))
        pairs.append((pr * a - pi * b, pr * b + pi * a))
    waves = left(forward, right(backward, pairs))
    shrunk = []
    for k, ((a, b), s) in enumerate(zip(waves, slots)):
        gain = amps[s] * lax.rsqrt(a * a + b * b + smoothing) - 1.0
        if scale is not None:
            gain = gain * scale[k]
        shrunk.append((a * gain, b * gain))
    backs = right(forward, left(backward, shrunk))
    return [(pr * a + pi * b, pr * b - pi * a) for a, b in backs]


def corner_of(pos, s):
    return pos[0, 0, 0, s] + BORDER, pos[0, 0, 1, s] + 128


def within(start, margin):
    return jnp.logical_and(start >= margin, start <= TILE - PROBE - margin)


def rows_within(pos, s, margin):
    return within(pos[0, 0, 0, s], margin)


def columns_within(pos, s, margin):
    return within(pos[0, 0, 1, s], margin)


def listed_slots(amount, todo, pos, cur, acc, amps, probe, tabs):
    def some(start, size):
        at = [start + k for k in range(size)]
        slots = [jnp.where(j < amount, todo[j], 0) for j in at]
        scale = [jnp.where(j < amount, 1.0, 0.0) for j in at]
        grads = gradients(cur, amps, probe, tabs, pos, slots, scale)
        for grad, s in zip(grads, slots):
            place(acc, grad, *corner_of(pos, s))

    def body(i, carry):
        some(i * GROUP, GROUP)
        return carry

    full = lax.div(amount + GROUP // 2 - 1, GROUP)
    lax.fori_loop(0, full, body, 0)

    @pl.when(amount > full * GROUP)
    def _():
        some(full * GROUP, GROUP // 2)


def step_of(probe):
    return step_gain / (jnp.max(probe[0] * probe[0] + probe[1] * probe[1]) + 1e-06)


def neighbours():
    rows, cols = lax.axis_size("row"), lax.axis_size("col")
    row, col = lax.axis_index("row"), lax.axis_index("col")
    out = []
    for dr, dc in DIRS:
        there = None
        for cond in (
            [row > 0] if dr < 0 else [row < rows - 1] if dr > 0 else []
        ) + ([col > 0] if dc < 0 else [col < cols - 1] if dc > 0 else []):
            there = cond if there is None else jnp.logical_and(there, cond)
        out.append((there, (row + dr, col + dc)))
    return out


def greet(near):
    barrier = pltpu.get_barrier_semaphore()
    for there, where in near:
        @pl.when(there)
        def _():
            pl.semaphore_signal(barrier, inc=1, device_id=where, device_id_type=MESH)


def greeted(near):
    total = 0
    for there, _ in near:
        total = total + there.astype(jnp.int32)
    pl.semaphore_wait(pltpu.get_barrier_semaphore(), total)


def remote(k, near, source, target, send, recv, n):
    return pltpu.make_async_remote_copy(
        src_ref=source,
        dst_ref=target,
        send_sem=send.at[n],
        recv_sem=recv.at[n],
        device_id=near[k][1],
        device_id_type=MESH,
    )


class Post:
    def __init__(self, near, send, recv):
        self.near, self.send, self.recv = near, send, recv
        self.count, self.waits = 0, []

    def pair(self, k, outs, intos):
        for i, way in enumerate((k, OPP[k])):
            n = self.count + i
            @pl.when(self.near[way][0])
            def _(i=i, way=way, n=n):
                remote(way, self.near, outs[i], intos[1 - i], self.send, self.recv, n).start()

        def wait(base=self.count):
            for i, way in enumerate((k, OPP[k])):
                @pl.when(self.near[way][0])
                def _(i=i, way=way):
                    remote(way, self.near, outs[i], intos[i], self.send, self.recv, base + i).wait_send()
                    remote(way, self.near, outs[i], intos[i], self.send, self.recv, base + 1 - i).wait_recv()

        self.count += 2
        return wait


def groups_before():
    cols, col = lax.axis_size("col"), lax.axis_index("col")
    late = jnp.logical_or(col == cols // 2 - 1, col == cols // 2).astype(jnp.int32)
    return 1 + late, late


def pack(pieces, start):
    lane = lanes(pieces[0].shape[0])
    out = None
    for q, piece in enumerate(pieces):
        turn = (32 * q - start) % 128
        turned = pltpu.roll(piece, turn, 1) if turn else piece
        out = turned if out is None else jnp.where(lane >= 32 * q, turned, out)
    return out


def unpack(value, start):
    turns = [(start - 32 * q) % 128 for q in range(4)]
    return [pltpu.roll(value, turn, 1) if turn else value for turn in turns]


def pack_two(value):
    half = value.shape[0] // 2
    lane = lanes(half)
    middle = jnp.logical_and(lane >= 32, lane < 96)
    return jnp.where(middle, pltpu.roll(value[half:], 64, 1), value[:half])


def unpack_two(value):
    return jnp.concatenate([value, pltpu.roll(value, 64, 1)], 0)


def seam(a, b):
    return jnp.where(lanes(a.shape[0]) >= 96, a, b)


def present(near, k, value):
    return jnp.where(near[k][0], value, 0.0)


LATE = 8


def keep_gradients(grads, cur, amps, probe, tabs, pos):
    def body(i, carry):
        slots = [i * GROUP + k for k in range(GROUP)]
        for s, (a, b) in zip(slots, gradients(cur, amps, probe, tabs, pos, slots)):
            grads[s, 0] = a
            grads[s, 1] = b
        return carry

    return body


def halo_kernel(
    pos, obj, amps_far, probe_far, t0_far, t1_far, cur, acc, grads, amps, probe, t0, t1, hv, hc, hd, sc, sd, send, recv, sems
):
    near = neighbours()
    greet(near)
    tile_at = [
        pltpu.make_async_copy(
            obj.at[:, :, pl.ds(128 * j, 128)], cur.at[:, j + 1, pl.ds(BORDER, TILE), :], sems.at[j]
        )
        for j in range(4)
    ]
    others = [
        pltpu.make_async_copy(there, here, sems.at[4 + n])
        for n, (there, here) in enumerate(((probe_far, probe), (t0_far, t0), (t1_far, t1), (amps_far, amps)))
    ]
    for copy in [tile_at[j] for j in (0, 3, 1, 2)] + others:
        copy.start()
    zeros = jnp.zeros((2, BLOCKS, BORDER, 128), f32)
    cur[:, :, 0:BORDER, :] = zeros
    cur[:, :, BORDER + TILE :, :] = zeros
    cur[:, 0] = jnp.zeros((2, ROWS, 128), f32)
    cur[:, 5] = jnp.zeros((2, ROWS, 128), f32)
    acc[...] = jnp.zeros_like(acc)
    for side in range(2):
        tile_at[3 * side].wait()
        block, start = 1 + 3 * side, 96 * side
        for p in range(2):
            sc[side, p] = pack(
                [cur[p, block, BORDER + 128 * q : BORDER + 128 * q + 128, :] for q in range(4)], start
            )
            for ud in range(2):
                base = BORDER + (TILE - 32) * ud
                sd[2 * ud + side, p] = pack(
                    [cur[p, block, base + 8 * q : base + 8 * q + 8, :] for q in range(4)], start
                )
    greeted(near)
    post = Post(near, send, recv)
    sideways = post.pair(2, [sc.at[0], sc.at[1]], [hc.at[0], hc.at[1]])
    waits = [post.pair(0, [obj.at[:, pl.ds(0, 32), :], obj.at[:, pl.ds(TILE - 32, 32), :]], [hv.at[0], hv.at[1]])]
    waits.append(post.pair(4, [sd.at[0], sd.at[3]], [hd.at[0], hd.at[3]]))
    waits.append(post.pair(5, [sd.at[1], sd.at[2]], [hd.at[1], hd.at[2]]))
    for copy in [tile_at[1], tile_at[2]] + others:
        copy.wait()
    body = keep_gradients(grads, cur, amps, probe, (t0, t1), pos)
    before, _ = groups_before()
    lax.fori_loop(0, before, body, 0)
    sideways()
    for p in range(2):
        for side in range(2):
            for q, piece in enumerate(unpack(hc[side, p], 96 - 96 * side)):
                at = BORDER + 128 * q
                cur[p, 5 * side, at : at + 128, :] = present(near, 2 + side, piece)
    lax.fori_loop(before, PMAX // GROUP, body, 0)
    for wait in waits:
        wait()
    for p in range(2):
        for k in range(2):
            base = (BORDER + TILE) * k
            for j in range(4):
                cur[p, j + 1, base : base + 32, :] = present(near, k, hv[k, p, :, 128 * j : 128 * j + 128])
            for side in range(2):
                for q, piece in enumerate(unpack(hd[2 * k + side, p], 96 - 96 * side)):
                    cur[p, 5 * side, base + 8 * q : base + 8 * q + 8, :] = present(near, 4 + 2 * k + side, piece)


def first_kernel(count, pos, acc_in, cur, grads, amps, probe, t0, t1, acc, todo):
    del acc_in
    early = GROUP * groups_before()[0]

    def sort(s, amount):
        done = jnp.logical_and(
            rows_within(pos, s, 0), jnp.logical_or(s >= early, columns_within(pos, s, 0))
        )

        @pl.when(done)
        def _():
            place(acc, (grads[s, 0], grads[s, 1]), *corner_of(pos, s))

        @pl.when(jnp.logical_not(done))
        def _():
            todo[amount] = s

        return amount + jnp.where(done, 0, 1)

    amount = lax.fori_loop(0, count[0, 0], sort, jnp.int32(0))
    listed_slots(amount, todo, pos, cur, acc, amps, probe, (t0, t1))


def side_sums(near, rc, rm, side, p):
    for rows, value in (
        (pl.ds(0, 64), rc[side, 0, p]),
        (pl.ds(64, TILE - 64), rm[side, p]),
        (pl.ds(TILE, 64), rc[side, 1, p]),
    ):
        yield rows, present(near, 2 + side, unpack_two(value))


def strip_kernel(
    pos, acc, cur_in, amps, probe, t0, t1, grads, cur, rv, rs, rc, rm, sv, ss, sc, sm, send, recv
):
    near = neighbours()
    greet(near)
    for p in range(2):
        for side in range(2):
            for ud in range(2):
                rows = pl.ds(TILE * ud, 64)
                sc[side, ud, p] = pack_two(seam(acc[p, 4 * side, rows, :], acc[p, 4 * side + 1, rows, :]))
    greeted(near)
    post = Post(near, send, recv)
    corners = post.pair(2, [sc.at[0], sc.at[1]], [rc.at[0], rc.at[1]])
    for p in range(2):
        for side in range(2):
            sm[side, p] = pack_two(seam(acc[p, 4 * side, 64:TILE, :], acc[p, 4 * side + 1, 64:TILE, :]))
    middle = post.pair(2, [sm.at[0], sm.at[1]], [rm.at[0], rm.at[1]])
    waits = [
        post.pair(
            0,
            [acc.at[:, pl.ds(2, 2), pl.ds(TILE * ud, 64), :] for ud in range(2)],
            [rv.at[ud, :, pl.ds(1, 2)] for ud in range(2)],
        )
    ]
    step = step_of(probe)
    cur[...] = cur_in[...] + step * acc[...]
    corners()
    lane = lanes(64)
    for p in range(2):
        for ud in range(2):
            rows = pl.ds(TILE * ud, 64)
            west = present(near, 2, unpack_two(rc[0, ud, p]))
            east = present(near, 3, unpack_two(rc[1, ud, p]))
            sv[ud, p, 0] = acc[p, 1, rows, :] + jnp.where(lane < 32, west, 0.0)
            sv[ud, p, 1] = acc[p, 4, rows, :] + jnp.where(lane >= 96, east, 0.0)
            ss[ud, p] = pack_two(seam(acc[p, 0, rows, :] + west, acc[p, 5, rows, :] + east))
    for n, block in ((0, 0), (1, 3)):
        waits.append(
            post.pair(0, [sv.at[ud, :, n] for ud in range(2)], [rv.at[ud, :, block] for ud in range(2)])
        )
    waits.append(post.pair(0, [ss.at[0], ss.at[1]], [rs.at[0], rs.at[1]]))
    for side in range(2):
        cur[:, 5 * side] = present(near, 2 + side, cur[:, 5 * side])
    body = keep_gradients(grads, cur, amps, probe, (t0, t1), pos)
    _, before = groups_before()
    lax.fori_loop(0, before, body, 0)
    middle()
    for p in range(2):
        for side in range(2):
            for rows, value in side_sums(near, rc, rm, side, p):
                lane = lanes(value.shape[0])
                for block, mine in ((4 * side, lane >= 96), (4 * side + 1, lane < 32)):
                    cur[p, block, rows, :] += step * jnp.where(mine, value, 0.0)
    lax.fori_loop(before, PMAX // GROUP, body, 0)
    for wait in waits:
        wait()


def second_kernel(
    count, pos, acc_in, cur_in, rv, rs, rc, rm, grads, amps, probe, t0, t1, acc, cur, late, todo
):
    near = neighbours()
    step = step_of(probe)
    del acc_in, cur_in
    early = GROUP * groups_before()[1]

    def add(p, block, rows, value):
        acc[p, block, rows, :] += value
        cur[p, block, rows, :] += step * value

    for p in range(2):
        for ud in range(2):
            rows = pl.ds(TILE * ud, 64)
            for j in range(4):
                add(p, j + 1, rows, present(near, ud, rv[ud, p, j]))
            sides = present(near, ud, unpack_two(rs[ud, p]))
            lane = lanes(64)
            add(p, 0, rows, jnp.where(lane >= 96, sides, 0.0))
            add(p, 5, rows, jnp.where(lane < 32, sides, 0.0))
        for side in range(2):
            block = 1 + 3 * side
            for rows, value in side_sums(near, rc, rm, side, p):
                lane = lanes(value.shape[0])
                acc[p, block, rows, :] += jnp.where(lane >= 96 if side else lane < 32, value, 0.0)
    for k in range(2):
        rows = pl.ds((BORDER + TILE) * k, BORDER)
        cur[:, :, rows, :] = present(near, k, cur[:, :, rows, :])
        for p in range(2):
            for r in range(2):
                at = pl.ds((BORDER + TILE) * r, BORDER)
                cur[p, 5 * k, at, :] = present(near, 2 + k, cur[p, 5 * k, at, :])
        acc[:, :, rows, :] = jnp.zeros((2, BLOCKS, BORDER, 128), f32)
        acc[:, 5 * k] = jnp.zeros((2, ROWS, 128), f32)
    for k in range(LATE):
        late[k] = PMAX

    def sort(s, carry):
        amount, held = carry
        done = jnp.logical_and(
            rows_within(pos, s, BORDER), jnp.logical_or(s >= early, columns_within(pos, s, BORDER))
        )
        inner = jnp.logical_and(rows_within(pos, s, 0), columns_within(pos, s, 0))
        hold = jnp.logical_and(jnp.logical_and(inner, held < LATE), jnp.logical_not(done))

        @pl.when(done)
        def _():
            place(acc, (grads[s, 0], grads[s, 1]), *corner_of(pos, s))

        @pl.when(hold)
        def _():
            late[held] = s

        now = jnp.logical_not(jnp.logical_or(done, hold))

        @pl.when(now)
        def _():
            todo[amount] = s

        return amount + jnp.where(now, 1, 0), held + jnp.where(hold, 1, 0)

    amount, _ = lax.fori_loop(0, count[0, 0], sort, (jnp.int32(0), jnp.int32(0)))
    listed_slots(amount, todo, pos, cur, acc, amps, probe, (t0, t1))


def fold_kernel(pos, late, acc, cur, amps, probe, t0, t1, grads, gv, gc, gd, sc, sd, send, recv):
    near = neighbours()
    greet(near)
    for p in range(2):
        for side in range(2):
            start = 96 - 96 * side
            for ud in range(2):
                base = (BORDER + TILE) * ud
                sd[2 * ud + side, p] = pack(
                    [acc[p, 5 * side, base + 8 * q : base + 8 * q + 8, :] for q in range(4)], start
                )
    for p in range(2):
        for side in range(2):
            sc[side, p] = pack(
                [acc[p, 5 * side, BORDER + 128 * q : BORDER + 128 * q + 128, :] for q in range(4)], 96 - 96 * side
            )
    greeted(near)
    post = Post(near, send, recv)
    waits = [post.pair(2, [sc.at[0], sc.at[1]], [gc.at[0], gc.at[1]])]
    waits.append(
        post.pair(
            0,
            [acc.at[:, pl.ds(1, 4), pl.ds((BORDER + TILE) * ud, BORDER), :] for ud in range(2)],
            [gv.at[0], gv.at[1]],
        )
    )
    waits.append(post.pair(4, [sd.at[0], sd.at[3]], [gd.at[0], gd.at[3]]))
    waits.append(post.pair(5, [sd.at[1], sd.at[2]], [gd.at[1], gd.at[2]]))

    def body(i, carry):
        slots = [jnp.minimum(late[i * GROUP + k], PMAX - 1) for k in range(GROUP)]
        for k, (a, b) in enumerate(gradients(cur, amps, probe, (t0, t1), pos, slots)):
            grads[i * GROUP + k, 0] = a
            grads[i * GROUP + k, 1] = b
        return carry

    lax.fori_loop(0, LATE // GROUP, body, 0)
    for wait in waits:
        wait()


def last_kernel(pos, late, obj, acc_in, gv, gc, gd, grads, probe, est_out, corr_out, acc, est, sems):
    near = neighbours()
    del acc_in
    step = step_of(probe)

    def put(k, carry):
        s = late[k]

        @pl.when(s < PMAX)
        def _():
            place(acc, (grads[k, 0], grads[k, 1]), *corner_of(pos, s))

        return carry

    lax.fori_loop(0, LATE, put, 0)
    for p in range(2):
        for side in range(2):
            block, start = 1 + 3 * side, 96 * side

            def mine(rows):
                return lanes(rows) >= 96 if side else lanes(rows) < 32

            for q, piece in enumerate(unpack(gc[side, p], start)):
                at = BORDER + 128 * q
                acc[p, block, at : at + 128, :] += jnp.where(mine(128), present(near, 2 + side, piece), 0.0)
            for ud in range(2):
                base = BORDER + (TILE - 32) * ud
                for q, piece in enumerate(unpack(gd[2 * ud + side, p], start)):
                    at = base + 8 * q
                    piece = present(near, 4 + 2 * ud + side, piece)
                    acc[p, block, at : at + 8, :] += jnp.where(mine(8), piece, 0.0)
        for ud in range(2):
            base = BORDER + (TILE - 32) * ud
            for j in range(4):
                acc[p, j + 1, base : base + 32, :] += present(near, ud, gv[ud, p, j])
    stores = []
    inner = pl.ds(BORDER, TILE)
    for j in range(4):
        out = pl.ds(128 * j, 128)
        acc[:, j + 1, inner, :] = step * acc[:, j + 1, inner, :]
        stores.append(pltpu.make_async_copy(acc.at[:, j + 1, inner, :], corr_out.at[:, :, out], sems.at[j]))
        stores[-1].start()
        est[:, j] = obj[:, :, 128 * j : 128 * j + 128] + acc[:, j + 1, inner, :]
        stores.append(pltpu.make_async_copy(est.at[:, j], est_out.at[:, :, out], sems.at[4 + j]))
        stores[-1].start()
    for store in stores:
        store.wait()


VM = pl.BlockSpec(memory_space=pltpu.VMEM)
SM = pl.BlockSpec(memory_space=pltpu.SMEM)
HBM = pl.BlockSpec(memory_space=pltpu.HBM)


def shape(*dims, dtype=f32):
    return jax.ShapeDtypeStruct(dims, dtype)


def params(limit_mib=14, **kw):
    return pltpu.CompilerParams(vmem_limit_bytes=limit_mib * 2**20, **kw)


def remote_params(which):
    return params(collective_id=which, has_side_effects=True)


def on_device(object_field, probe_field, amplitudes, positions, counts):
    tabs = [jnp.asarray(t) for t in tables()]
    dma = pltpu.SemaphoreType.DMA
    tile = shape(2, BLOCKS, ROWS, 128)
    kept = shape(PMAX, 2, PROBE, PROBE)
    far = [
        pltpu.with_memory_space_constraint(x, pltpu.HBM)
        for x in (object_field, amplitudes, probe_field, *tabs)
    ]
    cur, acc, grads, *shared = pl.pallas_call(
        halo_kernel,
        out_shape=[tile, tile, kept] + [jax.ShapeDtypeStruct(x.shape, x.dtype) for x in (amplitudes, probe_field, *tabs)],
        in_specs=[SM] + [HBM] * 5,
        out_specs=[VM] * 7,
        scratch_shapes=[
            pltpu.VMEM((2, 2, 32, TILE), f32),
            pltpu.VMEM((2, 2, 128, 128), f32),
            pltpu.VMEM((4, 2, 8, 128), f32),
            pltpu.VMEM((2, 2, 128, 128), f32),
            pltpu.VMEM((4, 2, 8, 128), f32),
            dma((8,)),
            dma((8,)),
            dma((8,)),
        ],
        compiler_params=remote_params(0),
        name="halo",
    )(positions, *far)
    acc = pl.pallas_call(
        first_kernel,
        out_shape=tile,
        in_specs=[SM, SM] + [VM] * 7,
        out_specs=VM,
        scratch_shapes=[pltpu.SMEM((PMAX,), jnp.int32)],
        input_output_aliases={2: 0},
        compiler_params=params(),
        name="first",
    )(counts, positions, acc, cur, grads, *shared)
    strips = ((2, 2, 4, 64, 128), (2, 2, 32, 128), (2, 2, 2, 32, 128), (2, 2, 224, 128))
    grads, cur, *got = pl.pallas_call(
        strip_kernel,
        out_shape=(kept, tile) + tuple(shape(*s) for s in strips),
        in_specs=[SM] + [VM] * 6,
        out_specs=[VM] * 6,
        scratch_shapes=[
            pltpu.VMEM((2, 2, 2, 64, 128), f32),
            pltpu.VMEM((2, 2, 32, 128), f32),
            pltpu.VMEM((2, 2, 2, 32, 128), f32),
            pltpu.VMEM((2, 2, 224, 128), f32),
            dma((12,)),
            dma((12,)),
        ],
        compiler_params=remote_params(1),
        name="strips",
    )(positions, acc, cur, *shared)
    acc, cur, late = pl.pallas_call(
        second_kernel,
        out_shape=(tile, tile, shape(LATE, dtype=jnp.int32)),
        in_specs=[SM, SM] + [VM] * 11,
        out_specs=[VM, VM, SM],
        scratch_shapes=[pltpu.SMEM((PMAX,), jnp.int32)],
        input_output_aliases={2: 0, 3: 1},
        compiler_params=params(),
        name="second",
    )(counts, positions, acc, cur, *got, grads, *shared)
    folds = ((2, 2, 4, 32, 128), (2, 2, 128, 128), (4, 2, 8, 128))
    grads, *got = pl.pallas_call(
        fold_kernel,
        out_shape=(shape(LATE, 2, PROBE, PROBE),) + tuple(shape(*s) for s in folds),
        in_specs=[SM, SM] + [VM] * 6,
        out_specs=[VM] * 4,
        scratch_shapes=[
            pltpu.VMEM((2, 2, 128, 128), f32),
            pltpu.VMEM((4, 2, 8, 128), f32),
            dma((8,)),
            dma((8,)),
        ],
        compiler_params=remote_params(2),
        name="folds",
    )(positions, late, acc, cur, *shared)
    return pl.pallas_call(
        last_kernel,
        out_shape=(shape(2, TILE, TILE), shape(2, TILE, TILE), tile),
        in_specs=[SM, SM] + [VM] * 7,
        out_specs=[HBM, HBM, VM],
        scratch_shapes=[pltpu.VMEM((2, 4, TILE, 128), f32), dma((8,))],
        input_output_aliases={3: 2},
        compiler_params=params(),
        name="last",
    )(positions, late, object_field, acc, *got, grads, shared[1])[:2]


def solution(mesh):
    placed = (
        P(None, "row", "col"),
        P(),
        P("row", None, "col"),
        P("row", "col", None, None),
        P("row", "col"),
    )
    return jax.shard_map(
        on_device,
        mesh=mesh,
        in_specs=placed,
        out_specs=(P(None, "row", "col"), P(None, "row", "col")),
        check_vma=False,
    )
```

```python
import functools

import jax
import jax.numpy as jnp
import ml_dtypes
import numpy as np
from jax import lax
from jax.experimental import pallas as pl
from jax.experimental.pallas import tpu as pltpu
from jax.sharding import PartitionSpec as P

BORDER = 32
PROBE = 128
TILE = 512
PMAX = 24
ROWS = TILE + 2 * BORDER
BLOCKS = 6
GROUP = 8
smoothing = 0.5
step_gain = 0.5
f32 = jnp.float32
bf16 = jnp.bfloat16
MESH = pl.DeviceIdType.MESH

DIRS = ((-1, 0), (1, 0), (0, -1), (0, 1), (-1, -1), (-1, 1), (1, -1), (1, 1))
OPP = (1, 0, 3, 2, 7, 6, 5, 4)


def tables():
    n = np.arange(PROBE)
    angle = 2.0 * np.pi / PROBE * (n[:, None] * n[None, :] % PROBE)
    real, imag = np.cos(angle) / np.sqrt(PROBE), -np.sin(angle) / np.sqrt(PROBE)
    whole = np.block([[real, -imag], [imag, real]]).astype(np.float32)

    def halves(matrix):
        high = matrix.astype(ml_dtypes.bfloat16)
        return high, (matrix - high.astype(np.float32)).astype(ml_dtypes.bfloat16)

    return np.stack(halves(whole)), np.stack(halves(whole.T.copy()))


def split(value):
    high = value.astype(bf16)
    return high, (value - high.astype(f32)).astype(bf16)


def dot(a, b):
    return jnp.dot(a, b, preferred_element_type=f32)


def left(table, pairs):
    parts = [split(jnp.concatenate([a, b], 0)) for a, b in pairs]
    high = jnp.concatenate([p[0] for p in parts], 1)
    low = jnp.concatenate([p[1] for p in parts], 1)
    wide = jnp.concatenate([table[0], table[0], table[1]], 1)
    out = dot(wide, jnp.concatenate([high, low, high], 0))
    n = PROBE
    return [(out[:n, n * k : n * k + n], out[n:, n * k : n * k + n]) for k in range(len(pairs))]


def right(table, pairs):
    parts = [split(jnp.concatenate([a, b], 1)) for a, b in pairs]
    high = jnp.concatenate([p[0] for p in parts], 0)
    low = jnp.concatenate([p[1] for p in parts], 0)
    tall = jnp.concatenate([table[0], table[0], table[1]], 0)
    out = dot(jnp.concatenate([high, low, high], 1), tall)
    n = PROBE
    return [(out[n * k : n * k + n, :n], out[n * k : n * k + n, n:]) for k in range(len(pairs))]


def lanes(rows=PROBE):
    return lax.broadcasted_iota(jnp.int32, (rows, 128), 1)


def cut(cur, row, col):
    block, lane = col >> 7, col & 127
    out = []
    for p in range(2):
        a = cur[p, block, pl.ds(row, PROBE), :]
        b = cur[p, block + 1, pl.ds(row, PROBE), :]
        out.append(pltpu.roll(jnp.where(lanes() >= lane, a, b), (128 - lane) & 127, 1))
    return out


def turned(grad, pos, s):
    lane = corner_of(pos, s)[1] & 127
    return [pltpu.roll(g, lane, 1) for g in grad]


def place(acc, grad, pos, s):
    row, col = corner_of(pos, s)
    block, lane = col >> 7, col & 127
    rows = pl.ds(row, PROBE)
    first = lanes() >= lane
    for p in range(2):
        a, b = acc[p, block, rows, :], acc[p, block + 1, rows, :]
        acc[p, block, rows, :] = a + jnp.where(first, grad[p], 0.0)
        acc[p, block + 1, rows, :] = b + jnp.where(first, 0.0, grad[p])


def gradients(cur, amps, probe, tabs, pos, slots, scale=None):
    forward, backward = tabs
    pr, pi = probe[0], probe[1]
    pairs = []
    for s in slots:
        a, b = cut(cur, *corner_of(pos, s))
        pairs.append((pr * a - pi * b, pr * b + pi * a))
    waves = left(forward, right(backward, pairs))
    shrunk = []
    for k, ((a, b), s) in enumerate(zip(waves, slots)):
        gain = amps[s] * lax.rsqrt(a * a + b * b + smoothing) - 1.0
        if scale is not None:
            gain = gain * scale[k]
        shrunk.append((a * gain, b * gain))
    backs = right(forward, left(backward, shrunk))
    return [(pr * a + pi * b, pr * b - pi * a) for a, b in backs]


def corner_of(pos, s):
    return pos[0, 0, 0, s] + BORDER, pos[0, 0, 1, s] + 128


def within(start, margin):
    return jnp.logical_and(start >= margin, start <= TILE - PROBE - margin)


def rows_within(pos, s, margin):
    return within(pos[0, 0, 0, s], margin)


def columns_within(pos, s, margin):
    return within(pos[0, 0, 1, s], margin)


def listed_slots(amount, todo, pos, cur, acc, amps, probe, tabs):
    def some(start, size):
        at = [start + k for k in range(size)]
        slots = [jnp.where(j < amount, todo[j], 0) for j in at]
        scale = [jnp.where(j < amount, 1.0, 0.0) for j in at]
        grads = gradients(cur, amps, probe, tabs, pos, slots, scale)
        grads = [turned(grad, pos, s) for grad, s in zip(grads, slots)]
        for grad, s in zip(grads, slots):
            place(acc, grad, pos, s)

    def body(i, carry):
        some(i * GROUP, GROUP)
        return carry

    full = lax.div(amount + GROUP // 2 - 1, GROUP)
    lax.fori_loop(0, full, body, 0)

    @pl.when(amount > full * GROUP)
    def _():
        some(full * GROUP, GROUP // 2)


def step_of(probe):
    return step_gain / (jnp.max(probe[0] * probe[0] + probe[1] * probe[1]) + 1e-06)


def neighbours():
    rows, cols = lax.axis_size("row"), lax.axis_size("col")
    row, col = lax.axis_index("row"), lax.axis_index("col")
    out = []
    for dr, dc in DIRS:
        there = None
        for cond in (
            [row > 0] if dr < 0 else [row < rows - 1] if dr > 0 else []
        ) + ([col > 0] if dc < 0 else [col < cols - 1] if dc > 0 else []):
            there = cond if there is None else jnp.logical_and(there, cond)
        out.append((there, (row + dr, col + dc)))
    return out


def greet(near):
    barrier = pltpu.get_barrier_semaphore()
    for there, where in near:
        @pl.when(there)
        def _():
            pl.semaphore_signal(barrier, inc=1, device_id=where, device_id_type=MESH)


def greeted(near):
    total = 0
    for there, _ in near:
        total = total + there.astype(jnp.int32)
    pl.semaphore_wait(pltpu.get_barrier_semaphore(), total)


def remote(k, near, source, target, send, recv, n):
    return pltpu.make_async_remote_copy(
        src_ref=source,
        dst_ref=target,
        send_sem=send.at[n],
        recv_sem=recv.at[n],
        device_id=near[k][1],
        device_id_type=MESH,
    )


class Post:
    def __init__(self, near, send, recv):
        self.near, self.send, self.recv = near, send, recv
        self.count, self.waits = 0, []

    def pair(self, k, outs, intos):
        for i, way in enumerate((k, OPP[k])):
            n = self.count + i
            @pl.when(self.near[way][0])
            def _(i=i, way=way, n=n):
                remote(way, self.near, outs[i], intos[1 - i], self.send, self.recv, n).start()

        def wait(base=self.count):
            for i, way in enumerate((k, OPP[k])):
                @pl.when(self.near[way][0])
                def _(i=i, way=way):
                    remote(way, self.near, outs[i], intos[i], self.send, self.recv, base + i).wait_send()
                    remote(way, self.near, outs[i], intos[i], self.send, self.recv, base + 1 - i).wait_recv()

        self.count += 2
        return wait


def groups_before():
    cols, col = lax.axis_size("col"), lax.axis_index("col")
    late = jnp.logical_or(col == cols // 2 - 1, col == cols // 2).astype(jnp.int32)
    return 1 + late, late


def pack(pieces, start):
    lane = lanes(pieces[0].shape[0])
    out = None
    for q, piece in enumerate(pieces):
        turn = (32 * q - start) % 128
        turned = pltpu.roll(piece, turn, 1) if turn else piece
        out = turned if out is None else jnp.where(lane >= 32 * q, turned, out)
    return out


def unpack(value, start):
    turns = [(start - 32 * q) % 128 for q in range(4)]
    return [pltpu.roll(value, turn, 1) if turn else value for turn in turns]


def pack_two(value):
    half = value.shape[0] // 2
    lane = lanes(half)
    middle = jnp.logical_and(lane >= 32, lane < 96)
    return jnp.where(middle, pltpu.roll(value[half:], 64, 1), value[:half])


def unpack_two(value):
    return jnp.concatenate([value, pltpu.roll(value, 64, 1)], 0)


def seam(a, b):
    return jnp.where(lanes(a.shape[0]) >= 96, a, b)


def present(near, k, value):
    return jnp.where(near[k][0], value, 0.0)


LATE = 8


def keep_gradients(grads, cur, amps, probe, tabs, pos):
    def body(i, carry):
        slots = [i * GROUP + k for k in range(GROUP)]
        for s, grad in zip(slots, gradients(cur, amps, probe, tabs, pos, slots)):
            grads[s, 0], grads[s, 1] = turned(grad, pos, s)
        return carry

    return body


def halo_kernel(
    pos_far, obj, amps_far, probe_far, t0_far, t1_far, cur, acc, grads, amps, probe, t0, t1, hv, hc, hd, sc, sd, pos, send, recv, sems
):
    near = neighbours()
    greet(near)
    tile_at = [
        pltpu.make_async_copy(
            obj.at[:, :, pl.ds(128 * j, 128)], cur.at[:, j + 1, pl.ds(BORDER, TILE), :], sems.at[j]
        )
        for j in range(4)
    ]
    others = [
        pltpu.make_async_copy(there, here, sems.at[4 + n])
        for n, (there, here) in enumerate(
            ((probe_far, probe), (t0_far, t0), (t1_far, t1), (amps_far, amps), (pos_far, pos))
        )
    ]
    for copy in [tile_at[j] for j in (0, 3, 1, 2)] + others:
        copy.start()
    zeros = jnp.zeros((2, BLOCKS, BORDER, 128), f32)
    cur[:, :, 0:BORDER, :] = zeros
    cur[:, :, BORDER + TILE :, :] = zeros
    cur[:, 0] = jnp.zeros((2, ROWS, 128), f32)
    cur[:, 5] = jnp.zeros((2, ROWS, 128), f32)
    acc[...] = jnp.zeros_like(acc)
    for side in range(2):
        tile_at[3 * side].wait()
        block, start = 1 + 3 * side, 96 * side
        for p in range(2):
            sc[side, p] = pack(
                [cur[p, block, BORDER + 128 * q : BORDER + 128 * q + 128, :] for q in range(4)], start
            )
            for ud in range(2):
                base = BORDER + (TILE - 32) * ud
                sd[2 * ud + side, p] = pack(
                    [cur[p, block, base + 8 * q : base + 8 * q + 8, :] for q in range(4)], start
                )
    greeted(near)
    post = Post(near, send, recv)
    sideways = post.pair(2, [sc.at[0], sc.at[1]], [hc.at[0], hc.at[1]])
    waits = [post.pair(0, [obj.at[:, pl.ds(0, 32), :], obj.at[:, pl.ds(TILE - 32, 32), :]], [hv.at[0], hv.at[1]])]
    waits.append(post.pair(4, [sd.at[0], sd.at[3]], [hd.at[0], hd.at[3]]))
    waits.append(post.pair(5, [sd.at[1], sd.at[2]], [hd.at[1], hd.at[2]]))
    for copy in [tile_at[1], tile_at[2]] + others:
        copy.wait()
    body = keep_gradients(grads, cur, amps, probe, (t0, t1), pos)
    before, _ = groups_before()
    lax.fori_loop(0, before, body, 0)
    sideways()
    for p in range(2):
        for side in range(2):
            for q, piece in enumerate(unpack(hc[side, p], 96 - 96 * side)):
                at = BORDER + 128 * q
                cur[p, 5 * side, at : at + 128, :] = present(near, 2 + side, piece)
    lax.fori_loop(before, PMAX // GROUP, body, 0)
    for wait in waits:
        wait()
    for p in range(2):
        for k in range(2):
            base = (BORDER + TILE) * k
            for j in range(4):
                cur[p, j + 1, base : base + 32, :] = present(near, k, hv[k, p, :, 128 * j : 128 * j + 128])
            for side in range(2):
                for q, piece in enumerate(unpack(hd[2 * k + side, p], 96 - 96 * side)):
                    cur[p, 5 * side, base + 8 * q : base + 8 * q + 8, :] = present(near, 4 + 2 * k + side, piece)


def first_kernel(count, pos, acc_in, cur, grads, amps, probe, t0, t1, acc, todo):
    del acc_in
    early = GROUP * groups_before()[0]

    def sort(s, amount):
        done = jnp.logical_and(
            rows_within(pos, s, 0), jnp.logical_or(s >= early, columns_within(pos, s, 0))
        )

        @pl.when(done)
        def _():
            place(acc, (grads[s, 0], grads[s, 1]), pos, s)

        @pl.when(jnp.logical_not(done))
        def _():
            todo[amount] = s

        return amount + jnp.where(done, 0, 1)

    amount = lax.fori_loop(0, count[0, 0], sort, jnp.int32(0))
    listed_slots(amount, todo, pos, cur, acc, amps, probe, (t0, t1))


def side_sums(near, rc, rm, side, p):
    for rows, value in (
        (pl.ds(0, 64), rc[side, 0, p]),
        (pl.ds(64, TILE - 64), rm[side, p]),
        (pl.ds(TILE, 64), rc[side, 1, p]),
    ):
        yield rows, present(near, 2 + side, unpack_two(value))


def strip_kernel(
    pos, acc, cur_in, amps, probe, t0, t1, grads, cur, sums, rv, rs, rc, rm, sv, ss, sc, sm, send, recv
):
    near = neighbours()
    greet(near)
    for p in range(2):
        for side in range(2):
            for ud in range(2):
                rows = pl.ds(TILE * ud, 64)
                sc[side, ud, p] = pack_two(seam(acc[p, 4 * side, rows, :], acc[p, 4 * side + 1, rows, :]))
    greeted(near)
    post = Post(near, send, recv)
    corners = post.pair(2, [sc.at[0], sc.at[1]], [rc.at[0], rc.at[1]])
    for p in range(2):
        for side in range(2):
            sm[side, p] = pack_two(seam(acc[p, 4 * side, 64:TILE, :], acc[p, 4 * side + 1, 64:TILE, :]))
    middle = post.pair(2, [sm.at[0], sm.at[1]], [rm.at[0], rm.at[1]])
    waits = [
        post.pair(
            0,
            [acc.at[:, pl.ds(2, 2), pl.ds(TILE * ud, 64), :] for ud in range(2)],
            [rv.at[ud, :, pl.ds(1, 2)] for ud in range(2)],
        )
    ]
    step = step_of(probe)
    cur[...] = cur_in[...] + step * acc[...]
    corners()
    lane = lanes(64)
    for p in range(2):
        for ud in range(2):
            rows = pl.ds(TILE * ud, 64)
            west = present(near, 2, unpack_two(rc[0, ud, p]))
            east = present(near, 3, unpack_two(rc[1, ud, p]))
            sv[ud, p, 0] = acc[p, 1, rows, :] + jnp.where(lane < 32, west, 0.0)
            sv[ud, p, 1] = acc[p, 4, rows, :] + jnp.where(lane >= 96, east, 0.0)
            ss[ud, p] = pack_two(seam(acc[p, 0, rows, :] + west, acc[p, 5, rows, :] + east))
    for n, block in ((0, 0), (1, 3)):
        waits.append(
            post.pair(0, [sv.at[ud, :, n] for ud in range(2)], [rv.at[ud, :, block] for ud in range(2)])
        )
    waits.append(post.pair(0, [ss.at[0], ss.at[1]], [rs.at[0], rs.at[1]]))
    for k in range(2):
        outside = pl.ds((BORDER + TILE) * k, BORDER)
        cur[:, :, outside, :] = present(near, k, cur[:, :, outside, :])
        cur[:, 5 * k] = present(near, 2 + k, cur[:, 5 * k])
    body = keep_gradients(grads, cur, amps, probe, (t0, t1), pos)
    _, before = groups_before()
    lax.fori_loop(0, before, body, 0)
    middle()
    for p in range(2):
        for side in range(2):
            for rows, value in side_sums(near, rc, rm, side, p):
                lane = lanes(value.shape[0])
                for block, mine in ((4 * side, lane >= 96), (4 * side + 1, lane < 32)):
                    cur[p, block, rows, :] += step * jnp.where(mine, value, 0.0)
        for k in range(2):
            outside = pl.ds((BORDER + TILE) * k, BORDER)
            for block in (1, 4):
                cur[p, block, outside, :] = present(near, k, cur[p, block, outside, :])
                cur[p, 5 * (block // 4), outside, :] = present(near, k, cur[p, 5 * (block // 4), outside, :])
    lax.fori_loop(before, PMAX // GROUP, body, 0)
    sums[:, 1:5] = acc[:, 1:5]
    for p in range(2):
        for side in range(2):
            for rows, value in side_sums(near, rc, rm, side, p):
                lane = lanes(value.shape[0])
                sums[p, 1 + 3 * side, rows, :] += jnp.where(lane >= 96 if side else lane < 32, value, 0.0)
    for k in range(2):
        sums[:, 1:5, pl.ds((BORDER + TILE) * k, BORDER), :] = jnp.zeros((2, 4, BORDER, 128), f32)
        sums[:, 5 * k] = jnp.zeros((2, ROWS, 128), f32)
    for wait in waits:
        wait()


def second_kernel(
    count, pos, acc_in, cur_in, rv, rs, grads, amps, probe, t0, t1, acc, cur, late, todo
):
    near = neighbours()
    step = step_of(probe)
    del acc_in, cur_in
    early = GROUP * groups_before()[1]
    lane = lanes(64)
    for p in range(2):
        for ud in range(2):
            rows = pl.ds(TILE * ud, 64)
            inner, at = pl.ds(BORDER + (TILE - 32) * ud, 32), slice(32 - 32 * ud, 64 - 32 * ud)
            for j in range(4):
                value = present(near, ud, rv[ud, p, j])
                cur[p, j + 1, rows, :] += step * value
                acc[p, j + 1, inner, :] += value[at]
            value = step * present(near, ud, unpack_two(rs[ud, p]))
            for side, mine in ((0, lane >= 96), (1, lane < 32)):
                mine = jnp.logical_and(mine, near[2 + side][0])
                cur[p, 5 * side, rows, :] += jnp.where(mine, value, 0.0)
    for k in range(LATE):
        late[k] = PMAX

    def sort(s, carry):
        amount, held = carry
        done = jnp.logical_and(
            rows_within(pos, s, BORDER), jnp.logical_or(s >= early, columns_within(pos, s, BORDER))
        )
        inner = jnp.logical_and(rows_within(pos, s, 0), columns_within(pos, s, 0))
        hold = jnp.logical_and(jnp.logical_and(inner, held < LATE), jnp.logical_not(done))

        @pl.when(done)
        def _():
            place(acc, (grads[s, 0], grads[s, 1]), pos, s)

        @pl.when(hold)
        def _():
            late[held] = s

        now = jnp.logical_not(jnp.logical_or(done, hold))

        @pl.when(now)
        def _():
            todo[amount] = s

        return amount + jnp.where(now, 1, 0), held + jnp.where(hold, 1, 0)

    amount, _ = lax.fori_loop(0, count[0, 0], sort, (jnp.int32(0), jnp.int32(0)))
    listed_slots(amount, todo, pos, cur, acc, amps, probe, (t0, t1))


def fold_kernel(pos, late, acc, cur, amps, probe, t0, t1, grads, gv, gc, gd, sc, sd, send, recv):
    near = neighbours()
    greet(near)
    for p in range(2):
        for side in range(2):
            start = 96 - 96 * side
            for ud in range(2):
                base = (BORDER + TILE) * ud
                sd[2 * ud + side, p] = pack(
                    [acc[p, 5 * side, base + 8 * q : base + 8 * q + 8, :] for q in range(4)], start
                )
    for p in range(2):
        for side in range(2):
            sc[side, p] = pack(
                [acc[p, 5 * side, BORDER + 128 * q : BORDER + 128 * q + 128, :] for q in range(4)], 96 - 96 * side
            )
    greeted(near)
    post = Post(near, send, recv)
    waits = [post.pair(2, [sc.at[0], sc.at[1]], [gc.at[0], gc.at[1]])]
    waits.append(
        post.pair(
            0,
            [acc.at[:, pl.ds(1, 4), pl.ds((BORDER + TILE) * ud, BORDER), :] for ud in range(2)],
            [gv.at[0], gv.at[1]],
        )
    )
    waits.append(post.pair(4, [sd.at[0], sd.at[3]], [gd.at[0], gd.at[3]]))
    waits.append(post.pair(5, [sd.at[1], sd.at[2]], [gd.at[1], gd.at[2]]))

    def body(i, carry):
        slots = [jnp.minimum(late[i * GROUP + k], PMAX - 1) for k in range(GROUP)]
        for k, grad in enumerate(gradients(cur, amps, probe, (t0, t1), pos, slots)):
            grads[i * GROUP + k, 0], grads[i * GROUP + k, 1] = turned(grad, pos, slots[k])
        return carry

    lax.fori_loop(0, LATE // GROUP, body, 0)
    for wait in waits:
        wait()


def last_kernel(pos, late, obj, acc_in, gv, gc, gd, grads, probe, est_out, corr_out, acc, est, sems):
    near = neighbours()
    del acc_in
    step = step_of(probe)

    def put(k, carry):
        s = late[k]

        @pl.when(s < PMAX)
        def _():
            place(acc, (grads[k, 0], grads[k, 1]), pos, s)

        return carry

    lax.fori_loop(0, LATE, put, 0)
    inner = pl.ds(BORDER, TILE)
    stores = []

    def leave(j):
        out = pl.ds(128 * j, 128)
        acc[:, j + 1, inner, :] = step * acc[:, j + 1, inner, :]
        stores.append(pltpu.make_async_copy(acc.at[:, j + 1, inner, :], corr_out.at[:, :, out], sems.at[j]))
        stores[-1].start()
        est[:, j] = obj[:, :, 128 * j : 128 * j + 128] + acc[:, j + 1, inner, :]
        stores.append(pltpu.make_async_copy(est.at[:, j], est_out.at[:, :, out], sems.at[4 + j]))
        stores[-1].start()

    for j in (1, 2, 0, 3):
        for p in range(2):
            for ud in range(2):
                base = BORDER + (TILE - 32) * ud
                acc[p, j + 1, base : base + 32, :] += present(near, ud, gv[ud, p, j])
        if j in (0, 3):
            side, block, start = j // 3, j + 1, 32 * j

            def mine(rows):
                return lanes(rows) >= 96 if side else lanes(rows) < 32

            for p in range(2):
                for q, piece in enumerate(unpack(gc[side, p], start)):
                    at = BORDER + 128 * q
                    acc[p, block, at : at + 128, :] += jnp.where(mine(128), present(near, 2 + side, piece), 0.0)
                for ud in range(2):
                    base = BORDER + (TILE - 32) * ud
                    for q, piece in enumerate(unpack(gd[2 * ud + side, p], start)):
                        at = base + 8 * q
                        piece = present(near, 4 + 2 * ud + side, piece)
                        acc[p, block, at : at + 8, :] += jnp.where(mine(8), piece, 0.0)
        leave(j)
    for store in stores:
        store.wait()


VM = pl.BlockSpec(memory_space=pltpu.VMEM)
SM = pl.BlockSpec(memory_space=pltpu.SMEM)
HBM = pl.BlockSpec(memory_space=pltpu.HBM)


def shape(*dims, dtype=f32):
    return jax.ShapeDtypeStruct(dims, dtype)


def params(limit_mib=14, **kw):
    return pltpu.CompilerParams(vmem_limit_bytes=limit_mib * 2**20, **kw)


def remote_params(which):
    return params(collective_id=which, has_side_effects=True)


def on_device(object_field, probe_field, amplitudes, positions, counts):
    tabs = [jnp.asarray(t) for t in tables()]
    dma = pltpu.SemaphoreType.DMA
    tile = shape(2, BLOCKS, ROWS, 128)
    kept = shape(PMAX, 2, PROBE, PROBE)
    far = [
        pltpu.with_memory_space_constraint(x, pltpu.HBM)
        for x in (positions, object_field, amplitudes, probe_field, *tabs)
    ]
    cur, acc, grads, *shared = pl.pallas_call(
        halo_kernel,
        out_shape=[tile, tile, kept] + [jax.ShapeDtypeStruct(x.shape, x.dtype) for x in (amplitudes, probe_field, *tabs)],
        in_specs=[HBM] * 6,
        out_specs=[VM] * 7,
        scratch_shapes=[
            pltpu.VMEM((2, 2, 32, TILE), f32),
            pltpu.VMEM((2, 2, 128, 128), f32),
            pltpu.VMEM((4, 2, 8, 128), f32),
            pltpu.VMEM((2, 2, 128, 128), f32),
            pltpu.VMEM((4, 2, 8, 128), f32),
            pltpu.SMEM((1, 1, 2, PMAX), jnp.int32),
            dma((8,)),
            dma((8,)),
            dma((9,)),
        ],
        compiler_params=remote_params(0),
        name="halo",
    )(*far)
    acc = pl.pallas_call(
        first_kernel,
        out_shape=tile,
        in_specs=[SM, SM] + [VM] * 7,
        out_specs=VM,
        scratch_shapes=[pltpu.SMEM((PMAX,), jnp.int32)],
        input_output_aliases={2: 0},
        compiler_params=params(),
        name="first",
    )(counts, positions, acc, cur, grads, *shared)
    strips = ((2, 2, 4, 64, 128), (2, 2, 32, 128), (2, 2, 2, 32, 128), (2, 2, 224, 128))
    grads, cur, sums, rv, rs, *_ = pl.pallas_call(
        strip_kernel,
        out_shape=(kept, tile, tile) + tuple(shape(*s) for s in strips),
        in_specs=[SM] + [VM] * 6,
        out_specs=[VM] * 7,
        scratch_shapes=[
            pltpu.VMEM((2, 2, 2, 64, 128), f32),
            pltpu.VMEM((2, 2, 32, 128), f32),
            pltpu.VMEM((2, 2, 2, 32, 128), f32),
            pltpu.VMEM((2, 2, 224, 128), f32),
            dma((12,)),
            dma((12,)),
        ],
        compiler_params=remote_params(1),
        name="strips",
    )(positions, acc, cur, *shared)
    acc, cur, late = pl.pallas_call(
        second_kernel,
        out_shape=(tile, tile, shape(LATE, dtype=jnp.int32)),
        in_specs=[SM, SM] + [VM] * 9,
        out_specs=[VM, VM, SM],
        scratch_shapes=[pltpu.SMEM((PMAX,), jnp.int32)],
        input_output_aliases={2: 0, 3: 1},
        compiler_params=params(),
        name="second",
    )(counts, positions, sums, cur, rv, rs, grads, *shared)
    folds = ((2, 2, 4, 32, 128), (2, 2, 128, 128), (4, 2, 8, 128))
    grads, *got = pl.pallas_call(
        fold_kernel,
        out_shape=(shape(LATE, 2, PROBE, PROBE),) + tuple(shape(*s) for s in folds),
        in_specs=[SM, SM] + [VM] * 6,
        out_specs=[VM] * 4,
        scratch_shapes=[
            pltpu.VMEM((2, 2, 128, 128), f32),
            pltpu.VMEM((4, 2, 8, 128), f32),
            dma((8,)),
            dma((8,)),
        ],
        compiler_params=remote_params(2),
        name="folds",
    )(positions, late, acc, cur, *shared)
    return pl.pallas_call(
        last_kernel,
        out_shape=(shape(2, TILE, TILE), shape(2, TILE, TILE), tile),
        in_specs=[SM, SM] + [VM] * 7,
        out_specs=[HBM, HBM, VM],
        scratch_shapes=[pltpu.VMEM((2, 4, TILE, 128), f32), dma((8,))],
        input_output_aliases={3: 2},
        compiler_params=params(),
        name="last",
    )(positions, late, object_field, acc, *got, grads, shared[1])[:2]


def solution(mesh):
    placed = (
        P(None, "row", "col"),
        P(),
        P("row", None, "col"),
        P("row", "col", None, None),
        P("row", "col"),
    )
    return jax.shard_map(
        on_device,
        mesh=mesh,
        in_specs=placed,
        out_specs=(P(None, "row", "col"), P(None, "row", "col")),
        check_vma=False,
    )
```

```python
import functools

import jax
import jax.numpy as jnp
import ml_dtypes
import numpy as np
from jax import lax
from jax.experimental import pallas as pl
from jax.experimental.pallas import tpu as pltpu
from jax.sharding import PartitionSpec as P

BORDER = 32
PROBE = 128
TILE = 512
PMAX = 24
ROWS = TILE + 2 * BORDER
BLOCKS = 6
GROUP = 8
smoothing = 0.5
step_gain = 0.5
f32 = jnp.float32
bf16 = jnp.bfloat16
MESH = pl.DeviceIdType.MESH

DIRS = ((-1, 0), (1, 0), (0, -1), (0, 1))
OPP = (1, 0, 3, 2)


def tables():
    n = np.arange(PROBE)
    angle = 2.0 * np.pi / PROBE * (n[:, None] * n[None, :] % PROBE)
    real, imag = np.cos(angle) / np.sqrt(PROBE), -np.sin(angle) / np.sqrt(PROBE)
    whole = np.block([[real, -imag], [imag, real]]).astype(np.float32)

    def halves(matrix):
        high = matrix.astype(ml_dtypes.bfloat16)
        return high, (matrix - high.astype(np.float32)).astype(ml_dtypes.bfloat16)

    return np.stack(halves(whole)), np.stack(halves(whole.T.copy()))


def split(value):
    high = value.astype(bf16)
    return high, (value - high.astype(f32)).astype(bf16)


def dot(a, b):
    return jnp.dot(a, b, preferred_element_type=f32)


def left(table, pairs):
    parts = [split(jnp.concatenate([a, b], 0)) for a, b in pairs]
    high = jnp.concatenate([p[0] for p in parts], 1)
    low = jnp.concatenate([p[1] for p in parts], 1)
    wide = jnp.concatenate([table[0], table[0], table[1]], 1)
    out = dot(wide, jnp.concatenate([high, low, high], 0))
    n = PROBE
    return [(out[:n, n * k : n * k + n], out[n:, n * k : n * k + n]) for k in range(len(pairs))]


def right(table, pairs):
    parts = [split(jnp.concatenate([a, b], 1)) for a, b in pairs]
    high = jnp.concatenate([p[0] for p in parts], 0)
    low = jnp.concatenate([p[1] for p in parts], 0)
    tall = jnp.concatenate([table[0], table[0], table[1]], 0)
    out = dot(jnp.concatenate([high, low, high], 1), tall)
    n = PROBE
    return [(out[n * k : n * k + n, :n], out[n * k : n * k + n, n:]) for k in range(len(pairs))]


def lanes(rows=PROBE):
    return lax.broadcasted_iota(jnp.int32, (rows, 128), 1)


def cut(cur, row, col):
    block, lane = col >> 7, col & 127
    out = []
    for p in range(2):
        a = cur[p, block, pl.ds(row, PROBE), :]
        b = cur[p, block + 1, pl.ds(row, PROBE), :]
        out.append(pltpu.roll(jnp.where(lanes() >= lane, a, b), (128 - lane) & 127, 1))
    return out


def turned(grad, pos, s):
    lane = corner_of(pos, s)[1] & 127
    return [pltpu.roll(g, lane, 1) for g in grad]


def place(acc, grad, pos, s):
    row, col = corner_of(pos, s)
    block, lane = col >> 7, col & 127
    rows = pl.ds(row, PROBE)
    first = lanes() >= lane
    for p in range(2):
        a, b = acc[p, block, rows, :], acc[p, block + 1, rows, :]
        acc[p, block, rows, :] = a + jnp.where(first, grad[p], 0.0)
        acc[p, block + 1, rows, :] = b + jnp.where(first, 0.0, grad[p])


def gradients(cur, amps, probe, tabs, pos, slots, scale=None):
    forward, backward = tabs
    pr, pi = probe[0], probe[1]
    pairs = []
    for s in slots:
        a, b = cut(cur, *corner_of(pos, s))
        pairs.append((pr * a - pi * b, pr * b + pi * a))
    waves = left(forward, right(backward, pairs))
    shrunk = []
    for k, ((a, b), s) in enumerate(zip(waves, slots)):
        gain = amps[s] * lax.rsqrt(a * a + b * b + smoothing) - 1.0
        if scale is not None:
            gain = gain * scale[k]
        shrunk.append((a * gain, b * gain))
    backs = right(forward, left(backward, shrunk))
    return [(pr * a + pi * b, pr * b - pi * a) for a, b in backs]


def corner_of(pos, s):
    return pos[0, 0, 0, s] + BORDER, pos[0, 0, 1, s] + 128


def within(start, margin):
    return jnp.logical_and(start >= margin, start <= TILE - PROBE - margin)


def rows_within(pos, s, margin):
    return within(pos[0, 0, 0, s], margin)


def columns_within(pos, s, margin):
    return within(pos[0, 0, 1, s], margin)


def listed_slots(amount, todo, pos, cur, acc, amps, probe, tabs):
    def some(start, size):
        at = [start + k for k in range(size)]
        slots = [jnp.where(j < amount, todo[j], 0) for j in at]
        scale = [jnp.where(j < amount, 1.0, 0.0) for j in at]
        grads = gradients(cur, amps, probe, tabs, pos, slots, scale)
        grads = [turned(grad, pos, s) for grad, s in zip(grads, slots)]
        for grad, s in zip(grads, slots):
            place(acc, grad, pos, s)

    def body(i, carry):
        some(i * GROUP, GROUP)
        return carry

    full = lax.div(amount + GROUP // 2 - 1, GROUP)
    lax.fori_loop(0, full, body, 0)

    @pl.when(amount > full * GROUP)
    def _():
        some(full * GROUP, GROUP // 2)


def step_of(probe):
    return step_gain / (jnp.max(probe[0] * probe[0] + probe[1] * probe[1]) + 1e-06)


def neighbours():
    rows, cols = lax.axis_size("row"), lax.axis_size("col")
    row, col = lax.axis_index("row"), lax.axis_index("col")
    out = []
    for dr, dc in DIRS:
        there = None
        for cond in (
            [row > 0] if dr < 0 else [row < rows - 1] if dr > 0 else []
        ) + ([col > 0] if dc < 0 else [col < cols - 1] if dc > 0 else []):
            there = cond if there is None else jnp.logical_and(there, cond)
        out.append((there, (row + dr, col + dc)))
    return out


def greet(near):
    barrier = pltpu.get_barrier_semaphore()
    for there, where in near:
        @pl.when(there)
        def _():
            pl.semaphore_signal(barrier, inc=1, device_id=where, device_id_type=MESH)


def greeted(near):
    total = 0
    for there, _ in near:
        total = total + there.astype(jnp.int32)
    pl.semaphore_wait(pltpu.get_barrier_semaphore(), total)


def remote(k, near, source, target, send, recv, n):
    return pltpu.make_async_remote_copy(
        src_ref=source,
        dst_ref=target,
        send_sem=send.at[n],
        recv_sem=recv.at[n],
        device_id=near[k][1],
        device_id_type=MESH,
    )


class Post:
    def __init__(self, near, send, recv):
        self.near, self.send, self.recv = near, send, recv
        self.count, self.waits = 0, []

    def pair(self, k, outs, intos):
        for i, way in enumerate((k, OPP[k])):
            n = self.count + i
            @pl.when(self.near[way][0])
            def _(i=i, way=way, n=n):
                remote(way, self.near, outs[i], intos[1 - i], self.send, self.recv, n).start()

        def wait(base=self.count):
            for i, way in enumerate((k, OPP[k])):
                @pl.when(self.near[way][0])
                def _(i=i, way=way):
                    remote(way, self.near, outs[i], intos[i], self.send, self.recv, base + i).wait_send()
                    remote(way, self.near, outs[i], intos[i], self.send, self.recv, base + 1 - i).wait_recv()

        self.count += 2
        return wait


def groups_before():
    cols, col = lax.axis_size("col"), lax.axis_index("col")
    late = jnp.logical_or(col == cols // 2 - 1, col == cols // 2).astype(jnp.int32)
    return 1 + late, late


def pack(pieces, start):
    lane = lanes(pieces[0].shape[0])
    out = None
    for q, piece in enumerate(pieces):
        turn = (32 * q - start) % 128
        turned = pltpu.roll(piece, turn, 1) if turn else piece
        out = turned if out is None else jnp.where(lane >= 32 * q, turned, out)
    return out


def unpack(value, start):
    turns = [(start - 32 * q) % 128 for q in range(4)]
    return [pltpu.roll(value, turn, 1) if turn else value for turn in turns]


def pack_two(value):
    half = value.shape[0] // 2
    lane = lanes(half)
    middle = jnp.logical_and(lane >= 32, lane < 96)
    return jnp.where(middle, pltpu.roll(value[half:], 64, 1), value[:half])


def unpack_two(value):
    return jnp.concatenate([value, pltpu.roll(value, 64, 1)], 0)


def seam(a, b):
    return jnp.where(lanes(a.shape[0]) >= 96, a, b)


def present(near, k, value):
    return jnp.where(near[k][0], value, 0.0)


LATE = 8


def keep_gradients(grads, cur, amps, probe, tabs, pos):
    def body(i, carry):
        slots = [i * GROUP + k for k in range(GROUP)]
        for s, grad in zip(slots, gradients(cur, amps, probe, tabs, pos, slots)):
            grads[s, 0], grads[s, 1] = turned(grad, pos, s)
        return carry

    return body


def halo_kernel(
    pos_far, obj, amps_far, probe_far, t0_far, t1_far, cur, acc, grads, amps, probe, t0, t1, hv, hc, hd, sc, sd, pos, send, recv, sems
):
    near = neighbours()
    greet(near)
    tile_at = [
        pltpu.make_async_copy(
            obj.at[:, :, pl.ds(128 * j, 128)], cur.at[:, j + 1, pl.ds(BORDER, TILE), :], sems.at[j]
        )
        for j in range(4)
    ]
    others = [
        pltpu.make_async_copy(there, here, sems.at[4 + n])
        for n, (there, here) in enumerate(
            ((probe_far, probe), (t0_far, t0), (t1_far, t1), (amps_far, amps), (pos_far, pos))
        )
    ]
    for copy in [tile_at[j] for j in (0, 3, 1, 2)] + others:
        copy.start()
    zeros = jnp.zeros((2, BLOCKS, BORDER, 128), f32)
    cur[:, :, 0:BORDER, :] = zeros
    cur[:, :, BORDER + TILE :, :] = zeros
    cur[:, 0] = jnp.zeros((2, ROWS, 128), f32)
    cur[:, 5] = jnp.zeros((2, ROWS, 128), f32)
    acc[...] = jnp.zeros_like(acc)
    for side in range(2):
        tile_at[3 * side].wait()
        block, start = 1 + 3 * side, 96 * side
        for p in range(2):
            sc[side, p] = pack(
                [cur[p, block, BORDER + 128 * q : BORDER + 128 * q + 128, :] for q in range(4)], start
            )
    greeted(near)
    post = Post(near, send, recv)
    sideways = post.pair(2, [sc.at[0], sc.at[1]], [hc.at[0], hc.at[1]])
    waits = [post.pair(0, [obj.at[:, pl.ds(0, 32), :], obj.at[:, pl.ds(TILE - 32, 32), :]], [hv.at[0], hv.at[1]])]
    for copy in [tile_at[1], tile_at[2]] + others:
        copy.wait()
    body = keep_gradients(grads, cur, amps, probe, (t0, t1), pos)
    before, _ = groups_before()
    lax.fori_loop(0, before, body, 0)
    sideways()
    for p in range(2):
        for side in range(2):
            for q, piece in enumerate(unpack(hc[side, p], 96 - 96 * side)):
                at = BORDER + 128 * q
                cur[p, 5 * side, at : at + 128, :] = present(near, 2 + side, piece)
        for ud in range(2):
            rows = pl.ds(BORDER + (TILE - BORDER) * ud, BORDER)
            sd[ud, p] = pack_two(seam(cur[p, 0, rows, :], cur[p, 5, rows, :]))
    waits.append(post.pair(0, [sd.at[0], sd.at[1]], [hd.at[0], hd.at[1]]))
    lax.fori_loop(before, PMAX // GROUP, body, 0)
    for wait in waits:
        wait()
    for p in range(2):
        for k in range(2):
            base = (BORDER + TILE) * k
            for j in range(4):
                cur[p, j + 1, base : base + 32, :] = present(near, k, hv[k, p, :, 128 * j : 128 * j + 128])
            beside = present(near, k, unpack_two(hd[k, p]))
            for side in range(2):
                cur[p, 5 * side, base : base + 32, :] = beside


def first_kernel(count, pos, acc_in, cur, grads, amps, probe, t0, t1, acc, todo):
    del acc_in
    early = GROUP * groups_before()[0]

    def sort(s, amount):
        done = jnp.logical_and(
            rows_within(pos, s, 0), jnp.logical_or(s >= early, columns_within(pos, s, 0))
        )

        @pl.when(done)
        def _():
            place(acc, (grads[s, 0], grads[s, 1]), pos, s)

        @pl.when(jnp.logical_not(done))
        def _():
            todo[amount] = s

        return amount + jnp.where(done, 0, 1)

    amount = lax.fori_loop(0, count[0, 0], sort, jnp.int32(0))
    listed_slots(amount, todo, pos, cur, acc, amps, probe, (t0, t1))


def side_sums(near, rc, rm, side, p):
    for rows, value in (
        (pl.ds(0, 64), rc[side, 0, p]),
        (pl.ds(64, TILE - 64), rm[side, p]),
        (pl.ds(TILE, 64), rc[side, 1, p]),
    ):
        yield rows, present(near, 2 + side, unpack_two(value))


def strip_kernel(
    pos, acc, cur_in, amps, probe, t0, t1, grads, cur, sums, rv, rs, rc, rm, sv, ss, sc, sm, send, recv
):
    near = neighbours()
    greet(near)
    for p in range(2):
        for side in range(2):
            for ud in range(2):
                rows = pl.ds(TILE * ud, 64)
                sc[side, ud, p] = pack_two(seam(acc[p, 4 * side, rows, :], acc[p, 4 * side + 1, rows, :]))
    greeted(near)
    post = Post(near, send, recv)
    corners = post.pair(2, [sc.at[0], sc.at[1]], [rc.at[0], rc.at[1]])
    for p in range(2):
        for side in range(2):
            sm[side, p] = pack_two(seam(acc[p, 4 * side, 64:TILE, :], acc[p, 4 * side + 1, 64:TILE, :]))
    middle = post.pair(2, [sm.at[0], sm.at[1]], [rm.at[0], rm.at[1]])
    waits = [
        post.pair(
            0,
            [acc.at[:, pl.ds(2, 2), pl.ds(TILE * ud, 64), :] for ud in range(2)],
            [rv.at[ud, :, pl.ds(1, 2)] for ud in range(2)],
        )
    ]
    step = step_of(probe)
    cur[...] = cur_in[...] + step * acc[...]
    corners()
    lane = lanes(64)
    for p in range(2):
        for ud in range(2):
            rows = pl.ds(TILE * ud, 64)
            west = present(near, 2, unpack_two(rc[0, ud, p]))
            east = present(near, 3, unpack_two(rc[1, ud, p]))
            sv[ud, p, 0] = acc[p, 1, rows, :] + jnp.where(lane < 32, west, 0.0)
            sv[ud, p, 1] = acc[p, 4, rows, :] + jnp.where(lane >= 96, east, 0.0)
            ss[ud, p] = pack_two(seam(acc[p, 0, rows, :] + west, acc[p, 5, rows, :] + east))
    for n, block in ((0, 0), (1, 3)):
        waits.append(
            post.pair(0, [sv.at[ud, :, n] for ud in range(2)], [rv.at[ud, :, block] for ud in range(2)])
        )
    waits.append(post.pair(0, [ss.at[0], ss.at[1]], [rs.at[0], rs.at[1]]))
    for k in range(2):
        outside = pl.ds((BORDER + TILE) * k, BORDER)
        cur[:, :, outside, :] = present(near, k, cur[:, :, outside, :])
        cur[:, 5 * k] = present(near, 2 + k, cur[:, 5 * k])
    body = keep_gradients(grads, cur, amps, probe, (t0, t1), pos)
    _, before = groups_before()
    lax.fori_loop(0, before, body, 0)
    middle()
    for p in range(2):
        for side in range(2):
            for rows, value in side_sums(near, rc, rm, side, p):
                lane = lanes(value.shape[0])
                for block, mine in ((4 * side, lane >= 96), (4 * side + 1, lane < 32)):
                    cur[p, block, rows, :] += step * jnp.where(mine, value, 0.0)
        for k in range(2):
            outside = pl.ds((BORDER + TILE) * k, BORDER)
            for block in (1, 4):
                cur[p, block, outside, :] = present(near, k, cur[p, block, outside, :])
                cur[p, 5 * (block // 4), outside, :] = present(near, k, cur[p, 5 * (block // 4), outside, :])
    lax.fori_loop(before, PMAX // GROUP, body, 0)
    sums[:, 1:5] = acc[:, 1:5]
    for p in range(2):
        for side in range(2):
            for rows, value in side_sums(near, rc, rm, side, p):
                lane = lanes(value.shape[0])
                sums[p, 1 + 3 * side, rows, :] += jnp.where(lane >= 96 if side else lane < 32, value, 0.0)
    for k in range(2):
        sums[:, 1:5, pl.ds((BORDER + TILE) * k, BORDER), :] = jnp.zeros((2, 4, BORDER, 128), f32)
        sums[:, 5 * k] = jnp.zeros((2, ROWS, 128), f32)
    for wait in waits:
        wait()


def second_kernel(
    count, pos, acc_in, cur_in, rv, rs, grads, amps, probe, t0, t1, acc, cur, late, todo
):
    near = neighbours()
    step = step_of(probe)
    del acc_in, cur_in
    early = GROUP * groups_before()[1]
    lane = lanes(64)
    for p in range(2):
        for ud in range(2):
            rows = pl.ds(TILE * ud, 64)
            inner, at = pl.ds(BORDER + (TILE - 32) * ud, 32), slice(32 - 32 * ud, 64 - 32 * ud)
            for j in range(4):
                value = present(near, ud, rv[ud, p, j])
                cur[p, j + 1, rows, :] += step * value
                acc[p, j + 1, inner, :] += value[at]
            value = step * present(near, ud, unpack_two(rs[ud, p]))
            for side, mine in ((0, lane >= 96), (1, lane < 32)):
                mine = jnp.logical_and(mine, near[2 + side][0])
                cur[p, 5 * side, rows, :] += jnp.where(mine, value, 0.0)
    for k in range(LATE):
        late[k] = PMAX

    def sort(s, carry):
        amount, held = carry
        done = jnp.logical_and(
            rows_within(pos, s, BORDER), jnp.logical_or(s >= early, columns_within(pos, s, BORDER))
        )
        inner = jnp.logical_and(rows_within(pos, s, 0), columns_within(pos, s, 0))
        hold = jnp.logical_and(jnp.logical_and(inner, held < LATE), jnp.logical_not(done))

        @pl.when(done)
        def _():
            place(acc, (grads[s, 0], grads[s, 1]), pos, s)

        @pl.when(hold)
        def _():
            late[held] = s

        now = jnp.logical_not(jnp.logical_or(done, hold))

        @pl.when(now)
        def _():
            todo[amount] = s

        return amount + jnp.where(now, 1, 0), held + jnp.where(hold, 1, 0)

    amount, _ = lax.fori_loop(0, count[0, 0], sort, (jnp.int32(0), jnp.int32(0)))
    listed_slots(amount, todo, pos, cur, acc, amps, probe, (t0, t1))


def fold_kernel(pos, late, acc, cur, amps, probe, t0, t1, grads, gv, gc, gd, sc, sd, sv, send, recv):
    near = neighbours()
    greet(near)
    for p in range(2):
        for side in range(2):
            for ud in range(2):
                base = (BORDER + TILE) * ud
                sd[side, ud, p] = pack(
                    [acc[p, 5 * side, base + 8 * q : base + 8 * q + 8, :] for q in range(4)], 96 - 96 * side
                )
    greeted(near)
    post = Post(near, send, recv)
    corners = post.pair(2, [sd.at[0], sd.at[1]], [gd.at[0], gd.at[1]])
    waits = [
        post.pair(
            0,
            [acc.at[:, pl.ds(2, 2), pl.ds((BORDER + TILE) * ud, BORDER), :] for ud in range(2)],
            [gv.at[ud, :, pl.ds(1, 2)] for ud in range(2)],
        )
    ]
    for p in range(2):
        for side in range(2):
            sc[side, p] = pack(
                [acc[p, 5 * side, BORDER + 128 * q : BORDER + 128 * q + 128, :] for q in range(4)], 96 - 96 * side
            )
    waits.append(post.pair(2, [sc.at[0], sc.at[1]], [gc.at[0], gc.at[1]]))
    corners()
    lane = lanes(BORDER)
    for p in range(2):
        for ud in range(2):
            rows = pl.ds((BORDER + TILE) * ud, BORDER)
            for side in range(2):
                beside = present(near, 2 + side, jnp.concatenate(unpack(gd[side, ud, p], 96 * side), 0))
                mine = lane >= 96 if side else lane < 32
                sv[ud, p, side] = acc[p, 1 + 3 * side, rows, :] + jnp.where(mine, beside, 0.0)
    for side in range(2):
        waits.append(
            post.pair(0, [sv.at[ud, :, side] for ud in range(2)], [gv.at[ud, :, 3 * side] for ud in range(2)])
        )

    def body(i, carry):
        slots = [jnp.minimum(late[i * GROUP + k], PMAX - 1) for k in range(GROUP)]
        for k, grad in enumerate(gradients(cur, amps, probe, (t0, t1), pos, slots)):
            grads[i * GROUP + k, 0], grads[i * GROUP + k, 1] = turned(grad, pos, slots[k])
        return carry

    lax.fori_loop(0, LATE // GROUP, body, 0)
    for wait in waits:
        wait()


def last_kernel(pos, late, obj, acc_in, gv, gc, grads, probe, est_out, corr_out, acc, est, sems):
    near = neighbours()
    del acc_in
    step = step_of(probe)

    def put(k, carry):
        s = late[k]

        @pl.when(s < PMAX)
        def _():
            place(acc, (grads[k, 0], grads[k, 1]), pos, s)

        return carry

    lax.fori_loop(0, LATE, put, 0)
    inner = pl.ds(BORDER, TILE)
    stores = []

    def leave(j):
        out = pl.ds(128 * j, 128)
        acc[:, j + 1, inner, :] = step * acc[:, j + 1, inner, :]
        stores.append(pltpu.make_async_copy(acc.at[:, j + 1, inner, :], corr_out.at[:, :, out], sems.at[j]))
        stores[-1].start()
        est[:, j] = obj[:, :, 128 * j : 128 * j + 128] + acc[:, j + 1, inner, :]
        stores.append(pltpu.make_async_copy(est.at[:, j], est_out.at[:, :, out], sems.at[4 + j]))
        stores[-1].start()

    for j in (1, 2, 0, 3):
        for p in range(2):
            for ud in range(2):
                base = BORDER + (TILE - 32) * ud
                acc[p, j + 1, base : base + 32, :] += present(near, ud, gv[ud, p, j])
        if j in (0, 3):
            side, block, start = j // 3, j + 1, 32 * j

            def mine(rows):
                return lanes(rows) >= 96 if side else lanes(rows) < 32

            for p in range(2):
                for q, piece in enumerate(unpack(gc[side, p], start)):
                    at = BORDER + 128 * q
                    acc[p, block, at : at + 128, :] += jnp.where(mine(128), present(near, 2 + side, piece), 0.0)
        leave(j)
    for store in stores:
        store.wait()


VM = pl.BlockSpec(memory_space=pltpu.VMEM)
SM = pl.BlockSpec(memory_space=pltpu.SMEM)
HBM = pl.BlockSpec(memory_space=pltpu.HBM)


def shape(*dims, dtype=f32):
    return jax.ShapeDtypeStruct(dims, dtype)


def params(limit_mib=14, **kw):
    return pltpu.CompilerParams(vmem_limit_bytes=limit_mib * 2**20, **kw)


def remote_params(which):
    return params(collective_id=which, has_side_effects=True)


def on_device(object_field, probe_field, amplitudes, positions, counts):
    tabs = [jnp.asarray(t) for t in tables()]
    dma = pltpu.SemaphoreType.DMA
    tile = shape(2, BLOCKS, ROWS, 128)
    kept = shape(PMAX, 2, PROBE, PROBE)
    far = [
        pltpu.with_memory_space_constraint(x, pltpu.HBM)
        for x in (positions, object_field, amplitudes, probe_field, *tabs)
    ]
    cur, acc, grads, *shared = pl.pallas_call(
        halo_kernel,
        out_shape=[tile, tile, kept]
        + [jax.ShapeDtypeStruct(x.shape, x.dtype) for x in (amplitudes, probe_field, *tabs)],
        in_specs=[HBM] * 6,
        out_specs=[VM] * 7,
        scratch_shapes=[
            pltpu.VMEM((2, 2, 32, TILE), f32),
            pltpu.VMEM((2, 2, 128, 128), f32),
            pltpu.VMEM((2, 2, 16, 128), f32),
            pltpu.VMEM((2, 2, 128, 128), f32),
            pltpu.VMEM((2, 2, 16, 128), f32),
            pltpu.SMEM((1, 1, 2, PMAX), jnp.int32),
            dma((8,)),
            dma((8,)),
            dma((9,)),
        ],
        compiler_params=remote_params(0),
        name="halo",
    )(*far)
    acc = pl.pallas_call(
        first_kernel,
        out_shape=tile,
        in_specs=[SM, SM] + [VM] * 7,
        out_specs=VM,
        scratch_shapes=[pltpu.SMEM((PMAX,), jnp.int32)],
        input_output_aliases={2: 0},
        compiler_params=params(),
        name="first",
    )(counts, positions, acc, cur, grads, *shared)
    strips = ((2, 2, 4, 64, 128), (2, 2, 32, 128), (2, 2, 2, 32, 128), (2, 2, 224, 128))
    grads, cur, sums, rv, rs, *_ = pl.pallas_call(
        strip_kernel,
        out_shape=(kept, tile, tile) + tuple(shape(*s) for s in strips),
        in_specs=[SM] + [VM] * 6,
        out_specs=[VM] * 7,
        scratch_shapes=[
            pltpu.VMEM((2, 2, 2, 64, 128), f32),
            pltpu.VMEM((2, 2, 32, 128), f32),
            pltpu.VMEM((2, 2, 2, 32, 128), f32),
            pltpu.VMEM((2, 2, 224, 128), f32),
            dma((12,)),
            dma((12,)),
        ],
        compiler_params=remote_params(1),
        name="strips",
    )(positions, acc, cur, *shared)
    acc, cur, late = pl.pallas_call(
        second_kernel,
        out_shape=(tile, tile, shape(LATE, dtype=jnp.int32)),
        in_specs=[SM, SM] + [VM] * 9,
        out_specs=[VM, VM, SM],
        scratch_shapes=[pltpu.SMEM((PMAX,), jnp.int32)],
        input_output_aliases={2: 0, 3: 1},
        compiler_params=params(),
        name="second",
    )(counts, positions, sums, cur, rv, rs, grads, *shared)
    folds = ((2, 2, 4, 32, 128), (2, 2, 128, 128))
    grads, gv, gc = pl.pallas_call(
        fold_kernel,
        out_shape=(shape(LATE, 2, PROBE, PROBE),) + tuple(shape(*s) for s in folds),
        in_specs=[SM, SM] + [VM] * 6,
        out_specs=[VM] * 3,
        scratch_shapes=[
            pltpu.VMEM((2, 2, 2, 8, 128), f32),
            pltpu.VMEM((2, 2, 128, 128), f32),
            pltpu.VMEM((2, 2, 2, 8, 128), f32),
            pltpu.VMEM((2, 2, 2, 32, 128), f32),
            dma((10,)),
            dma((10,)),
        ],
        compiler_params=remote_params(2),
        name="folds",
    )(positions, late, acc, cur, *shared)
    return pl.pallas_call(
        last_kernel,
        out_shape=(shape(2, TILE, TILE), shape(2, TILE, TILE), tile),
        in_specs=[SM, SM] + [VM] * 6,
        out_specs=[HBM, HBM, VM],
        scratch_shapes=[pltpu.VMEM((2, 4, TILE, 128), f32), dma((8,))],
        input_output_aliases={3: 2},
        compiler_params=params(),
        name="last",
    )(positions, late, object_field, acc, gv, gc, grads, shared[1])[:2]


def solution(mesh):
    placed = (
        P(None, "row", "col"),
        P(),
        P("row", None, "col"),
        P("row", "col", None, None),
        P("row", "col"),
    )
    return jax.shard_map(
        on_device,
        mesh=mesh,
        in_specs=placed,
        out_specs=(P(None, "row", "col"), P(None, "row", "col")),
        check_vma=False,
    )
```

```python
import functools

import jax
import jax.numpy as jnp
import ml_dtypes
import numpy as np
from jax import lax
from jax.experimental import pallas as pl
from jax.experimental.pallas import tpu as pltpu
from jax.sharding import PartitionSpec as P

BORDER = 32
PROBE = 128
TILE = 512
PMAX = 24
ROWS = TILE + 2 * BORDER
BLOCKS = 6
GROUP = 8
smoothing = 0.5
step_gain = 0.5
f32 = jnp.float32
bf16 = jnp.bfloat16
MESH = pl.DeviceIdType.MESH

DIRS = ((-1, 0), (1, 0), (0, -1), (0, 1))
OPP = (1, 0, 3, 2)


def tables():
    n = np.arange(PROBE)
    angle = 2.0 * np.pi / PROBE * (n[:, None] * n[None, :] % PROBE)
    real, imag = np.cos(angle) / np.sqrt(PROBE), -np.sin(angle) / np.sqrt(PROBE)
    whole = np.block([[real, -imag], [imag, real]]).astype(np.float32)

    def halves(matrix):
        high = matrix.astype(ml_dtypes.bfloat16)
        return high, (matrix - high.astype(np.float32)).astype(ml_dtypes.bfloat16)

    return np.stack(halves(whole)), np.stack(halves(whole.T.copy()))


def split(value):
    high = value.astype(bf16)
    return high, (value - high.astype(f32)).astype(bf16)


def dot(a, b):
    return jnp.dot(a, b, preferred_element_type=f32)


def left(table, pairs):
    parts = [split(jnp.concatenate([a, b], 0)) for a, b in pairs]
    high = jnp.concatenate([p[0] for p in parts], 1)
    low = jnp.concatenate([p[1] for p in parts], 1)
    wide = jnp.concatenate([table[0], table[0], table[1]], 1)
    out = dot(wide, jnp.concatenate([high, low, high], 0))
    n = PROBE
    return [(out[:n, n * k : n * k + n], out[n:, n * k : n * k + n]) for k in range(len(pairs))]


def right(table, pairs):
    parts = [split(jnp.concatenate([a, b], 1)) for a, b in pairs]
    high = jnp.concatenate([p[0] for p in parts], 0)
    low = jnp.concatenate([p[1] for p in parts], 0)
    tall = jnp.concatenate([table[0], table[0], table[1]], 0)
    out = dot(jnp.concatenate([high, low, high], 1), tall)
    n = PROBE
    return [(out[n * k : n * k + n, :n], out[n * k : n * k + n, n:]) for k in range(len(pairs))]


def lanes(rows=PROBE):
    return lax.broadcasted_iota(jnp.int32, (rows, 128), 1)


def cut(cur, row, col):
    block, lane = col >> 7, col & 127
    out = []
    for p in range(2):
        a = cur[p, block, pl.ds(row, PROBE), :]
        b = cur[p, block + 1, pl.ds(row, PROBE), :]
        out.append(pltpu.roll(jnp.where(lanes() >= lane, a, b), (128 - lane) & 127, 1))
    return out


def turned(grad, pos, s):
    lane = corner_of(pos, s)[1] & 127
    return [pltpu.roll(g, lane, 1) for g in grad]


def place(acc, grad, pos, s):
    row, col = corner_of(pos, s)
    block, lane = col >> 7, col & 127
    rows = pl.ds(row, PROBE)
    first = lanes() >= lane
    for p in range(2):
        a, b = acc[p, block, rows, :], acc[p, block + 1, rows, :]
        acc[p, block, rows, :] = a + jnp.where(first, grad[p], 0.0)
        acc[p, block + 1, rows, :] = b + jnp.where(first, 0.0, grad[p])


def gradients(cur, amps, probe, tabs, pos, slots, scale=None):
    forward, backward = tabs
    pr, pi = probe[0], probe[1]
    pairs = []
    for s in slots:
        a, b = cut(cur, *corner_of(pos, s))
        pairs.append((pr * a - pi * b, pr * b + pi * a))
    waves = left(forward, right(backward, pairs))
    shrunk = []
    for k, ((a, b), s) in enumerate(zip(waves, slots)):
        gain = amps[s] * lax.rsqrt(a * a + b * b + smoothing) - 1.0
        if scale is not None:
            gain = gain * scale[k]
        shrunk.append((a * gain, b * gain))
    backs = right(forward, left(backward, shrunk))
    return [(pr * a + pi * b, pr * b - pi * a) for a, b in backs]


def corner_of(pos, s):
    return pos[0, 0, 0, s] + BORDER, pos[0, 0, 1, s] + 128


def within(start, margin):
    return jnp.logical_and(start >= margin, start <= TILE - PROBE - margin)


def rows_within(pos, s, margin):
    return within(pos[0, 0, 0, s], margin)


def columns_within(pos, s, margin):
    return within(pos[0, 0, 1, s], margin)


def listed_slots(amount, todo, pos, cur, acc, amps, probe, tabs):
    def some(start, size):
        at = [start + k for k in range(size)]
        slots = [jnp.where(j < amount, todo[j], 0) for j in at]
        scale = [jnp.where(j < amount, 1.0, 0.0) for j in at]
        grads = gradients(cur, amps, probe, tabs, pos, slots, scale)
        grads = [turned(grad, pos, s) for grad, s in zip(grads, slots)]
        for grad, s in zip(grads, slots):
            place(acc, grad, pos, s)

    def body(i, carry):
        some(i * GROUP, GROUP)
        return carry

    full = lax.div(amount + GROUP // 2 - 1, GROUP)
    lax.fori_loop(0, full, body, 0)

    @pl.when(amount > full * GROUP)
    def _():
        some(full * GROUP, GROUP // 2)


def step_of(probe):
    return step_gain / (jnp.max(probe[0] * probe[0] + probe[1] * probe[1]) + 1e-06)


def neighbours():
    rows, cols = lax.axis_size("row"), lax.axis_size("col")
    row, col = lax.axis_index("row"), lax.axis_index("col")
    out = []
    for dr, dc in DIRS:
        there = None
        for cond in (
            [row > 0] if dr < 0 else [row < rows - 1] if dr > 0 else []
        ) + ([col > 0] if dc < 0 else [col < cols - 1] if dc > 0 else []):
            there = cond if there is None else jnp.logical_and(there, cond)
        out.append((there, (row + dr, col + dc)))
    return out


def greet(near):
    barrier = pltpu.get_barrier_semaphore()
    for there, where in near:
        @pl.when(there)
        def _():
            pl.semaphore_signal(barrier, inc=1, device_id=where, device_id_type=MESH)


def greeted(near):
    total = 0
    for there, _ in near:
        total = total + there.astype(jnp.int32)
    pl.semaphore_wait(pltpu.get_barrier_semaphore(), total)


def remote(k, near, source, target, send, recv, n):
    return pltpu.make_async_remote_copy(
        src_ref=source,
        dst_ref=target,
        send_sem=send.at[n],
        recv_sem=recv.at[n],
        device_id=near[k][1],
        device_id_type=MESH,
    )


class Post:
    def __init__(self, near, send, recv):
        self.near, self.send, self.recv = near, send, recv
        self.count, self.waits = 0, []

    def pair(self, k, outs, intos):
        for i, way in enumerate((k, OPP[k])):
            n = self.count + i
            @pl.when(self.near[way][0])
            def _(i=i, way=way, n=n):
                remote(way, self.near, outs[i], intos[1 - i], self.send, self.recv, n).start()

        def wait(base=self.count):
            for i, way in enumerate((k, OPP[k])):
                @pl.when(self.near[way][0])
                def _(i=i, way=way):
                    remote(way, self.near, outs[i], intos[i], self.send, self.recv, base + i).wait_send()
                    remote(way, self.near, outs[i], intos[i], self.send, self.recv, base + 1 - i).wait_recv()

        self.count += 2
        return wait


def groups_before():
    cols, col = lax.axis_size("col"), lax.axis_index("col")
    late = jnp.logical_or(col == cols // 2 - 1, col == cols // 2).astype(jnp.int32)
    return 1 + late, late


def pack(pieces, start):
    lane = lanes(pieces[0].shape[0])
    out = None
    for q, piece in enumerate(pieces):
        turn = (32 * q - start) % 128
        turned = pltpu.roll(piece, turn, 1) if turn else piece
        out = turned if out is None else jnp.where(lane >= 32 * q, turned, out)
    return out


def unpack(value, start):
    turns = [(start - 32 * q) % 128 for q in range(4)]
    return [pltpu.roll(value, turn, 1) if turn else value for turn in turns]


def pack_two(value):
    half = value.shape[0] // 2
    lane = lanes(half)
    middle = jnp.logical_and(lane >= 32, lane < 96)
    return jnp.where(middle, pltpu.roll(value[half:], 64, 1), value[:half])


def unpack_two(value):
    return jnp.concatenate([value, pltpu.roll(value, 64, 1)], 0)


def seam(a, b):
    return jnp.where(lanes(a.shape[0]) >= 96, a, b)


def present(near, k, value):
    return jnp.where(near[k][0], value, 0.0)


LATE = 8


def second_rule(pos, s):
    early = GROUP * groups_before()[1]
    done = jnp.logical_and(
        rows_within(pos, s, BORDER), jnp.logical_or(s >= early, columns_within(pos, s, BORDER))
    )
    inner = jnp.logical_and(rows_within(pos, s, 0), columns_within(pos, s, 0))
    return done, jnp.logical_and(inner, jnp.logical_not(done))


def keep_gradients(grads, cur, amps, probe, tabs, pos):
    def body(i, carry):
        slots = [i * GROUP + k for k in range(GROUP)]
        for s, grad in zip(slots, gradients(cur, amps, probe, tabs, pos, slots)):
            grads[s, 0], grads[s, 1] = turned(grad, pos, s)
        return carry

    return body


def halo_kernel(
    pos_far, obj, amps_far, probe_far, t0_far, t1_far, cur, acc, grads, amps, probe, t0, t1, hv, hc, hd, sc, sd, pos, send, recv, sems
):
    near = neighbours()
    greet(near)
    tile_at = [
        pltpu.make_async_copy(
            obj.at[:, :, pl.ds(128 * j, 128)], cur.at[:, j + 1, pl.ds(BORDER, TILE), :], sems.at[j]
        )
        for j in range(4)
    ]
    others = [
        pltpu.make_async_copy(there, here, sems.at[4 + n])
        for n, (there, here) in enumerate(
            ((probe_far, probe), (t0_far, t0), (t1_far, t1), (amps_far, amps), (pos_far, pos))
        )
    ]
    for copy in [tile_at[j] for j in (0, 3, 1, 2)] + others:
        copy.start()
    zeros = jnp.zeros((2, BLOCKS, BORDER, 128), f32)
    cur[:, :, 0:BORDER, :] = zeros
    cur[:, :, BORDER + TILE :, :] = zeros
    cur[:, 0] = jnp.zeros((2, ROWS, 128), f32)
    cur[:, 5] = jnp.zeros((2, ROWS, 128), f32)
    acc[...] = jnp.zeros_like(acc)
    for side in range(2):
        tile_at[3 * side].wait()
        block, start = 1 + 3 * side, 96 * side
        for p in range(2):
            sc[side, p] = pack(
                [cur[p, block, BORDER + 128 * q : BORDER + 128 * q + 128, :] for q in range(4)], start
            )
    greeted(near)
    post = Post(near, send, recv)
    sideways = post.pair(2, [sc.at[0], sc.at[1]], [hc.at[0], hc.at[1]])
    waits = [post.pair(0, [obj.at[:, pl.ds(0, 32), :], obj.at[:, pl.ds(TILE - 32, 32), :]], [hv.at[0], hv.at[1]])]
    for copy in [tile_at[1], tile_at[2]] + others:
        copy.wait()
    body = keep_gradients(grads, cur, amps, probe, (t0, t1), pos)
    before, _ = groups_before()
    lax.fori_loop(0, before, body, 0)
    sideways()
    for p in range(2):
        for side in range(2):
            for q, piece in enumerate(unpack(hc[side, p], 96 - 96 * side)):
                at = BORDER + 128 * q
                cur[p, 5 * side, at : at + 128, :] = present(near, 2 + side, piece)
        for ud in range(2):
            rows = pl.ds(BORDER + (TILE - BORDER) * ud, BORDER)
            sd[ud, p] = pack_two(seam(cur[p, 0, rows, :], cur[p, 5, rows, :]))
    waits.append(post.pair(0, [sd.at[0], sd.at[1]], [hd.at[0], hd.at[1]]))
    lax.fori_loop(before, PMAX // GROUP, body, 0)
    for wait in waits:
        wait()
    for p in range(2):
        for k in range(2):
            base = (BORDER + TILE) * k
            for j in range(4):
                cur[p, j + 1, base : base + 32, :] = present(near, k, hv[k, p, :, 128 * j : 128 * j + 128])
            beside = present(near, k, unpack_two(hd[k, p]))
            for side in range(2):
                cur[p, 5 * side, base : base + 32, :] = beside


def first_kernel(count, pos, acc_in, cur, grads, amps, probe, t0, t1, acc, todo):
    del acc_in
    early = GROUP * groups_before()[0]

    def sort(s, amount):
        done = jnp.logical_and(
            rows_within(pos, s, 0), jnp.logical_or(s >= early, columns_within(pos, s, 0))
        )

        @pl.when(done)
        def _():
            place(acc, (grads[s, 0], grads[s, 1]), pos, s)

        @pl.when(jnp.logical_not(done))
        def _():
            todo[amount] = s

        return amount + jnp.where(done, 0, 1)

    amount = lax.fori_loop(0, count[0, 0], sort, jnp.int32(0))
    listed_slots(amount, todo, pos, cur, acc, amps, probe, (t0, t1))


def side_sums(near, rc, rm, side, p):
    for rows, value in (
        (pl.ds(0, 64), rc[side, 0, p]),
        (pl.ds(64, TILE - 64), rm[side, p]),
        (pl.ds(TILE, 64), rc[side, 1, p]),
    ):
        yield rows, present(near, 2 + side, unpack_two(value))


def strip_kernel(
    pos, acc, cur_in, amps, probe, t0, t1, rate, grads, cur, sums, rv, rs, rc, rm, sv, ss, sc, sm, send, recv
):
    near = neighbours()
    greet(near)
    for p in range(2):
        for side in range(2):
            for ud in range(2):
                rows = pl.ds(TILE * ud, 64)
                sc[side, ud, p] = pack_two(seam(acc[p, 4 * side, rows, :], acc[p, 4 * side + 1, rows, :]))
    greeted(near)
    post = Post(near, send, recv)
    corners = post.pair(2, [sc.at[0], sc.at[1]], [rc.at[0], rc.at[1]])
    for p in range(2):
        for side in range(2):
            sm[side, p] = pack_two(seam(acc[p, 4 * side, 64:TILE, :], acc[p, 4 * side + 1, 64:TILE, :]))
    middle = post.pair(2, [sm.at[0], sm.at[1]], [rm.at[0], rm.at[1]])
    waits = [
        post.pair(
            0,
            [acc.at[:, pl.ds(2, 2), pl.ds(TILE * ud, 64), :] for ud in range(2)],
            [rv.at[ud, :, pl.ds(1, 2)] for ud in range(2)],
        )
    ]
    step = step_of(probe)
    rate[...] = jnp.full(rate.shape, step, f32)
    cur[...] = cur_in[...] + step * acc[...]
    corners()
    lane = lanes(64)
    for p in range(2):
        for ud in range(2):
            rows = pl.ds(TILE * ud, 64)
            west = present(near, 2, unpack_two(rc[0, ud, p]))
            east = present(near, 3, unpack_two(rc[1, ud, p]))
            sv[ud, p, 0] = acc[p, 1, rows, :] + jnp.where(lane < 32, west, 0.0)
            sv[ud, p, 1] = acc[p, 4, rows, :] + jnp.where(lane >= 96, east, 0.0)
            ss[ud, p] = pack_two(seam(acc[p, 0, rows, :] + west, acc[p, 5, rows, :] + east))
    for n, block in ((0, 0), (1, 3)):
        waits.append(
            post.pair(0, [sv.at[ud, :, n] for ud in range(2)], [rv.at[ud, :, block] for ud in range(2)])
        )
    waits.append(post.pair(0, [ss.at[0], ss.at[1]], [rs.at[0], rs.at[1]]))
    for k in range(2):
        outside = pl.ds((BORDER + TILE) * k, BORDER)
        cur[:, :, outside, :] = present(near, k, cur[:, :, outside, :])
        cur[:, 5 * k] = present(near, 2 + k, cur[:, 5 * k])
    body = keep_gradients(grads, cur, amps, probe, (t0, t1), pos)
    _, before = groups_before()
    lax.fori_loop(0, before, body, 0)
    middle()
    for p in range(2):
        for side in range(2):
            for rows, value in side_sums(near, rc, rm, side, p):
                lane = lanes(value.shape[0])
                for block, mine in ((4 * side, lane >= 96), (4 * side + 1, lane < 32)):
                    cur[p, block, rows, :] += step * jnp.where(mine, value, 0.0)
        for k in range(2):
            outside = pl.ds((BORDER + TILE) * k, BORDER)
            for block in (1, 4):
                cur[p, block, outside, :] = present(near, k, cur[p, block, outside, :])
                cur[p, 5 * (block // 4), outside, :] = present(near, k, cur[p, 5 * (block // 4), outside, :])
    lax.fori_loop(before, PMAX // GROUP, body, 0)
    sums[:, 1:5] = acc[:, 1:5]
    for p in range(2):
        for side in range(2):
            for rows, value in side_sums(near, rc, rm, side, p):
                lane = lanes(value.shape[0])
                sums[p, 1 + 3 * side, rows, :] += jnp.where(lane >= 96 if side else lane < 32, value, 0.0)
    for k in range(2):
        sums[:, 1:5, pl.ds((BORDER + TILE) * k, BORDER), :] = jnp.zeros((2, 4, BORDER, 128), f32)
        sums[:, 5 * k] = jnp.zeros((2, ROWS, 128), f32)
    for wait in waits:
        wait()


def second_kernel(
    count, pos, acc_in, cur_in, rv, rs, rate, grads, amps, probe, t0, t1, acc, cur, todo
):
    near = neighbours()
    step = rate[0:1, :]
    del acc_in, cur_in
    lane = lanes(64)
    for p in range(2):
        for ud in range(2):
            rows = pl.ds(TILE * ud, 64)
            inner, at = pl.ds(BORDER + (TILE - 32) * ud, 32), slice(32 - 32 * ud, 64 - 32 * ud)
            for j in range(4):
                value = present(near, ud, rv[ud, p, j])
                cur[p, j + 1, rows, :] += step * value
                acc[p, j + 1, inner, :] += value[at]
            value = step * present(near, ud, unpack_two(rs[ud, p]))
            for side, mine in ((0, lane >= 96), (1, lane < 32)):
                mine = jnp.logical_and(mine, near[2 + side][0])
                cur[p, 5 * side, rows, :] += jnp.where(mine, value, 0.0)
    def sort(s, carry):
        amount, held = carry
        done, hold = second_rule(pos, s)
        hold = jnp.logical_and(hold, held < LATE)

        @pl.when(done)
        def _():
            place(acc, (grads[s, 0], grads[s, 1]), pos, s)

        now = jnp.logical_not(jnp.logical_or(done, hold))

        @pl.when(now)
        def _():
            todo[amount] = s

        return amount + jnp.where(now, 1, 0), held + jnp.where(hold, 1, 0)

    amount, _ = lax.fori_loop(0, count[0, 0], sort, (jnp.int32(0), jnp.int32(0)))
    listed_slots(amount, todo, pos, cur, acc, amps, probe, (t0, t1))


def fold_kernel(
    count, pos, acc, cur, amps, probe, t0, t1, grads, gv, gc, gd, sc, sd, sv, late, follow, send, recv
):
    near = neighbours()
    greet(near)
    for p in range(2):
        for side in range(2):
            for ud in range(2):
                base = (BORDER + TILE) * ud
                sd[side, ud, p] = pack(
                    [acc[p, 5 * side, base + 8 * q : base + 8 * q + 8, :] for q in range(4)], 96 - 96 * side
                )
    greeted(near)
    post = Post(near, send, recv)
    corners = post.pair(2, [sd.at[0], sd.at[1]], [gd.at[0], gd.at[1]])
    waits = [
        post.pair(
            0,
            [acc.at[:, pl.ds(2, 2), pl.ds((BORDER + TILE) * ud, BORDER), :] for ud in range(2)],
            [gv.at[ud, :, pl.ds(1, 2)] for ud in range(2)],
        )
    ]
    for p in range(2):
        for side in range(2):
            sc[side, p] = pack(
                [acc[p, 5 * side, BORDER + 128 * q : BORDER + 128 * q + 128, :] for q in range(4)], 96 - 96 * side
            )
    waits.append(post.pair(2, [sc.at[0], sc.at[1]], [gc.at[0], gc.at[1]]))
    corners()
    lane = lanes(BORDER)
    for p in range(2):
        for ud in range(2):
            rows = pl.ds((BORDER + TILE) * ud, BORDER)
            for side in range(2):
                beside = present(near, 2 + side, jnp.concatenate(unpack(gd[side, ud, p], 96 * side), 0))
                mine = lane >= 96 if side else lane < 32
                sv[ud, p, side] = acc[p, 1 + 3 * side, rows, :] + jnp.where(mine, beside, 0.0)
    for side in range(2):
        waits.append(
            post.pair(0, [sv.at[ud, :, side] for ud in range(2)], [gv.at[ud, :, 3 * side] for ud in range(2)])
        )

    coming = jnp.int32(PMAX)
    follow[PMAX] = coming
    for s in range(PMAX - 1, -1, -1):
        hold = jnp.logical_and(s < count[0, 0], second_rule(pos, s)[1])
        coming = jnp.where(hold, s, coming)
        follow[s] = coming
    for k in range(LATE):
        late[k] = coming
        coming = follow[jnp.minimum(coming + 1, PMAX)]

    def body(i, carry):
        slots = [jnp.minimum(late[i * GROUP + k], PMAX - 1) for k in range(GROUP)]
        for k, grad in enumerate(gradients(cur, amps, probe, (t0, t1), pos, slots)):
            grads[i * GROUP + k, 0], grads[i * GROUP + k, 1] = turned(grad, pos, slots[k])
        return carry

    lax.fori_loop(0, LATE // GROUP, body, 0)
    for wait in waits:
        wait()


def last_kernel(count, pos, obj, acc_in, gv, gc, grads, rate, est_out, corr_out, acc, est, sems):
    near = neighbours()
    del acc_in
    step = rate[0:1, :]

    def put(s, held):
        hold = jnp.logical_and(second_rule(pos, s)[1], held < LATE)

        @pl.when(hold)
        def _():
            place(acc, (grads[held, 0], grads[held, 1]), pos, s)

        return held + jnp.where(hold, 1, 0)

    lax.fori_loop(0, count[0, 0], put, jnp.int32(0))
    inner = pl.ds(BORDER, TILE)
    stores = []

    def leave(j):
        out = pl.ds(128 * j, 128)
        acc[:, j + 1, inner, :] = step * acc[:, j + 1, inner, :]
        stores.append(pltpu.make_async_copy(acc.at[:, j + 1, inner, :], corr_out.at[:, :, out], sems.at[j]))
        stores[-1].start()
        est[:, j] = obj[:, :, 128 * j : 128 * j + 128] + acc[:, j + 1, inner, :]
        stores.append(pltpu.make_async_copy(est.at[:, j], est_out.at[:, :, out], sems.at[4 + j]))
        stores[-1].start()

    for j in (1, 2, 0, 3):
        for p in range(2):
            for ud in range(2):
                base = BORDER + (TILE - 32) * ud
                acc[p, j + 1, base : base + 32, :] += present(near, ud, gv[ud, p, j])
        if j in (0, 3):
            side, block, start = j // 3, j + 1, 32 * j

            def mine(rows):
                return lanes(rows) >= 96 if side else lanes(rows) < 32

            for p in range(2):
                for q, piece in enumerate(unpack(gc[side, p], start)):
                    at = BORDER + 128 * q
                    acc[p, block, at : at + 128, :] += jnp.where(mine(128), present(near, 2 + side, piece), 0.0)
        leave(j)
    for store in stores:
        store.wait()


VM = pl.BlockSpec(memory_space=pltpu.VMEM)
SM = pl.BlockSpec(memory_space=pltpu.SMEM)
HBM = pl.BlockSpec(memory_space=pltpu.HBM)


def shape(*dims, dtype=f32):
    return jax.ShapeDtypeStruct(dims, dtype)


def params(limit_mib=14, **kw):
    return pltpu.CompilerParams(vmem_limit_bytes=limit_mib * 2**20, **kw)


def remote_params(which):
    return params(collective_id=which, has_side_effects=True)


def on_device(object_field, probe_field, amplitudes, positions, counts):
    tabs = [jnp.asarray(t) for t in tables()]
    dma = pltpu.SemaphoreType.DMA
    tile = shape(2, BLOCKS, ROWS, 128)
    kept = shape(PMAX, 2, PROBE, PROBE)
    far = [
        pltpu.with_memory_space_constraint(x, pltpu.HBM)
        for x in (positions, object_field, amplitudes, probe_field, *tabs)
    ]
    cur, acc, grads, *shared = pl.pallas_call(
        halo_kernel,
        out_shape=[tile, tile, kept]
        + [jax.ShapeDtypeStruct(x.shape, x.dtype) for x in (amplitudes, probe_field, *tabs)],
        in_specs=[HBM] * 6,
        out_specs=[VM] * 7,
        scratch_shapes=[
            pltpu.VMEM((2, 2, 32, TILE), f32),
            pltpu.VMEM((2, 2, 128, 128), f32),
            pltpu.VMEM((2, 2, 16, 128), f32),
            pltpu.VMEM((2, 2, 128, 128), f32),
            pltpu.VMEM((2, 2, 16, 128), f32),
            pltpu.SMEM((1, 1, 2, PMAX), jnp.int32),
            dma((8,)),
            dma((8,)),
            dma((9,)),
        ],
        compiler_params=remote_params(0),
        name="halo",
    )(*far)
    acc = pl.pallas_call(
        first_kernel,
        out_shape=tile,
        in_specs=[SM, SM] + [VM] * 7,
        out_specs=VM,
        scratch_shapes=[pltpu.SMEM((PMAX,), jnp.int32)],
        input_output_aliases={2: 0},
        compiler_params=params(),
        name="first",
    )(counts, positions, acc, cur, grads, *shared)
    strips = ((2, 2, 4, 64, 128), (2, 2, 32, 128), (2, 2, 2, 32, 128), (2, 2, 224, 128))
    rate, grads, cur, sums, rv, rs, *_ = pl.pallas_call(
        strip_kernel,
        out_shape=(shape(8, 128), kept, tile, tile) + tuple(shape(*s) for s in strips),
        in_specs=[SM] + [VM] * 6,
        out_specs=[VM] * 8,
        scratch_shapes=[
            pltpu.VMEM((2, 2, 2, 64, 128), f32),
            pltpu.VMEM((2, 2, 32, 128), f32),
            pltpu.VMEM((2, 2, 2, 32, 128), f32),
            pltpu.VMEM((2, 2, 224, 128), f32),
            dma((12,)),
            dma((12,)),
        ],
        compiler_params=remote_params(1),
        name="strips",
    )(positions, acc, cur, *shared)
    acc, cur = pl.pallas_call(
        second_kernel,
        out_shape=(tile, tile),
        in_specs=[SM, SM] + [VM] * 10,
        out_specs=[VM, VM],
        scratch_shapes=[pltpu.SMEM((PMAX,), jnp.int32)],
        input_output_aliases={2: 0, 3: 1},
        compiler_params=params(),
        name="second",
    )(counts, positions, sums, cur, rv, rs, rate, grads, *shared)
    folds = ((2, 2, 4, 32, 128), (2, 2, 128, 128))
    grads, gv, gc = pl.pallas_call(
        fold_kernel,
        out_shape=(shape(LATE, 2, PROBE, PROBE),) + tuple(shape(*s) for s in folds),
        in_specs=[SM, SM] + [VM] * 6,
        out_specs=[VM] * 3,
        scratch_shapes=[
            pltpu.VMEM((2, 2, 2, 8, 128), f32),
            pltpu.VMEM((2, 2, 128, 128), f32),
            pltpu.VMEM((2, 2, 2, 8, 128), f32),
            pltpu.VMEM((2, 2, 2, 32, 128), f32),
            pltpu.SMEM((LATE,), jnp.int32),
            pltpu.SMEM((PMAX + 1,), jnp.int32),
            dma((10,)),
            dma((10,)),
        ],
        compiler_params=remote_params(2),
        name="folds",
    )(counts, positions, acc, cur, *shared)
    return pl.pallas_call(
        last_kernel,
        out_shape=(shape(2, TILE, TILE), shape(2, TILE, TILE), tile),
        in_specs=[SM, SM] + [VM] * 6,
        out_specs=[HBM, HBM, VM],
        scratch_shapes=[pltpu.VMEM((2, 4, TILE, 128), f32), dma((8,))],
        input_output_aliases={3: 2},
        compiler_params=params(),
        name="last",
    )(counts, positions, object_field, acc, gv, gc, grads, rate)[:2]


def solution(mesh):
    placed = (
        P(None, "row", "col"),
        P(),
        P("row", None, "col"),
        P("row", "col", None, None),
        P("row", "col"),
    )
    return jax.shard_map(
        on_device,
        mesh=mesh,
        in_specs=placed,
        out_specs=(P(None, "row", "col"), P(None, "row", "col")),
        check_vma=False,
    )
```

```python
import functools

import jax
import jax.numpy as jnp
import ml_dtypes
import numpy as np
from jax import lax
from jax.experimental import pallas as pl
from jax.experimental.pallas import tpu as pltpu
from jax.sharding import PartitionSpec as P

BORDER = 32
PROBE = 128
TILE = 512
PMAX = 24
ROWS = TILE + 2 * BORDER
BLOCKS = 6
GROUP = 8
smoothing = 0.5
step_gain = 0.5
f32 = jnp.float32
bf16 = jnp.bfloat16
MESH = pl.DeviceIdType.MESH

DIRS = ((-1, 0), (1, 0), (0, -1), (0, 1))
OPP = (1, 0, 3, 2)


def tables():
    n = np.arange(PROBE)
    angle = 2.0 * np.pi / PROBE * (n[:, None] * n[None, :] % PROBE)
    real, imag = np.cos(angle) / np.sqrt(PROBE), -np.sin(angle) / np.sqrt(PROBE)
    whole = np.block([[real, -imag], [imag, real]]).astype(np.float32)

    def halves(matrix):
        high = matrix.astype(ml_dtypes.bfloat16)
        return high, (matrix - high.astype(np.float32)).astype(ml_dtypes.bfloat16)

    return np.stack(halves(whole)), np.stack(halves(whole.T.copy()))


def split(value):
    high = value.astype(bf16)
    return high, (value - high.astype(f32)).astype(bf16)


def dot(a, b):
    return jnp.dot(a, b, preferred_element_type=f32)


def left(table, pairs):
    parts = [split(jnp.concatenate([a, b], 0)) for a, b in pairs]
    high = jnp.concatenate([p[0] for p in parts], 1)
    low = jnp.concatenate([p[1] for p in parts], 1)
    wide = jnp.concatenate([table[0], table[0], table[1]], 1)
    out = dot(wide, jnp.concatenate([high, low, high], 0))
    n = PROBE
    return [(out[:n, n * k : n * k + n], out[n:, n * k : n * k + n]) for k in range(len(pairs))]


def right(table, pairs):
    parts = [split(jnp.concatenate([a, b], 1)) for a, b in pairs]
    high = jnp.concatenate([p[0] for p in parts], 0)
    low = jnp.concatenate([p[1] for p in parts], 0)
    tall = jnp.concatenate([table[0], table[0], table[1]], 0)
    out = dot(jnp.concatenate([high, low, high], 1), tall)
    n = PROBE
    return [(out[n * k : n * k + n, :n], out[n * k : n * k + n, n:]) for k in range(len(pairs))]


def lanes(rows=PROBE):
    return lax.broadcasted_iota(jnp.int32, (rows, 128), 1)


def cut(cur, row, col):
    block, lane = col >> 7, col & 127
    out = []
    for p in range(2):
        a = cur[p, block, pl.ds(row, PROBE), :]
        b = cur[p, block + 1, pl.ds(row, PROBE), :]
        out.append(pltpu.roll(jnp.where(lanes() >= lane, a, b), (128 - lane) & 127, 1))
    return out


def turned(grad, pos, s):
    lane = corner_of(pos, s)[1] & 127
    return [pltpu.roll(g, lane, 1) for g in grad]


def place(acc, grad, pos, s):
    row, col = corner_of(pos, s)
    block, lane = col >> 7, col & 127
    rows = pl.ds(row, PROBE)
    first = lanes() >= lane
    for p in range(2):
        a, b = acc[p, block, rows, :], acc[p, block + 1, rows, :]
        acc[p, block, rows, :] = a + jnp.where(first, grad[p], 0.0)
        acc[p, block + 1, rows, :] = b + jnp.where(first, 0.0, grad[p])


def gradients(cur, amps, probe, tabs, pos, slots, scale=None):
    forward, backward = tabs
    pr, pi = probe[0], probe[1]
    pairs = []
    for s in slots:
        a, b = cut(cur, *corner_of(pos, s))
        pairs.append((pr * a - pi * b, pr * b + pi * a))
    waves = left(forward, right(backward, pairs))
    shrunk = []
    for k, ((a, b), s) in enumerate(zip(waves, slots)):
        gain = amps[s] * lax.rsqrt(a * a + b * b + smoothing) - 1.0
        if scale is not None:
            gain = gain * scale[k]
        shrunk.append((a * gain, b * gain))
    backs = right(forward, left(backward, shrunk))
    return [(pr * a + pi * b, pr * b - pi * a) for a, b in backs]


def corner_of(pos, s):
    return pos[0, 0, 0, s] + BORDER, pos[0, 0, 1, s] + 128


def within(start, margin):
    return jnp.logical_and(start >= margin, start <= TILE - PROBE - margin)


def rows_within(pos, s, margin):
    return within(pos[0, 0, 0, s], margin)


def columns_within(pos, s, margin):
    return within(pos[0, 0, 1, s], margin)


def listed_slots(amount, todo, pos, cur, acc, amps, probe, tabs):
    def some(start, size):
        at = [start + k for k in range(size)]
        slots = [jnp.where(j < amount, todo[j], 0) for j in at]
        scale = [jnp.where(j < amount, 1.0, 0.0) for j in at]
        grads = gradients(cur, amps, probe, tabs, pos, slots, scale)
        grads = [turned(grad, pos, s) for grad, s in zip(grads, slots)]
        for grad, s in zip(grads, slots):
            place(acc, grad, pos, s)

    def body(i, carry):
        some(i * GROUP, GROUP)
        return carry

    full = lax.div(amount + 1, GROUP)
    lax.fori_loop(0, full, body, 0)
    rest = amount - full * GROUP
    for least, size in ((1, 4), (5, 6)):

        @pl.when(jnp.logical_and(rest >= least, rest <= size))
        def _():
            some(full * GROUP, size)


def step_of(probe):
    return step_gain / (jnp.max(probe[0] * probe[0] + probe[1] * probe[1]) + 1e-06)


def neighbours():
    rows, cols = lax.axis_size("row"), lax.axis_size("col")
    row, col = lax.axis_index("row"), lax.axis_index("col")
    out = []
    for dr, dc in DIRS:
        there = None
        for cond in (
            [row > 0] if dr < 0 else [row < rows - 1] if dr > 0 else []
        ) + ([col > 0] if dc < 0 else [col < cols - 1] if dc > 0 else []):
            there = cond if there is None else jnp.logical_and(there, cond)
        out.append((there, (row + dr, col + dc)))
    return out


def greet(near):
    barrier = pltpu.get_barrier_semaphore()
    for there, where in near:
        @pl.when(there)
        def _():
            pl.semaphore_signal(barrier, inc=1, device_id=where, device_id_type=MESH)


def greeted(near):
    total = 0
    for there, _ in near:
        total = total + there.astype(jnp.int32)
    pl.semaphore_wait(pltpu.get_barrier_semaphore(), total)


def remote(k, near, source, target, send, recv, n):
    return pltpu.make_async_remote_copy(
        src_ref=source,
        dst_ref=target,
        send_sem=send.at[n],
        recv_sem=recv.at[n],
        device_id=near[k][1],
        device_id_type=MESH,
    )


class Post:
    def __init__(self, near, send, recv):
        self.near, self.send, self.recv = near, send, recv
        self.count, self.waits = 0, []

    def pair(self, k, outs, intos):
        for i, way in enumerate((k, OPP[k])):
            n = self.count + i
            @pl.when(self.near[way][0])
            def _(i=i, way=way, n=n):
                remote(way, self.near, outs[i], intos[1 - i], self.send, self.recv, n).start()

        def wait(base=self.count):
            for i, way in enumerate((k, OPP[k])):
                @pl.when(self.near[way][0])
                def _(i=i, way=way):
                    remote(way, self.near, outs[i], intos[i], self.send, self.recv, base + i).wait_send()
                    remote(way, self.near, outs[i], intos[i], self.send, self.recv, base + 1 - i).wait_recv()

        self.count += 2
        return wait


def groups_before():
    cols, col = lax.axis_size("col"), lax.axis_index("col")
    late = jnp.logical_or(col == cols // 2 - 1, col == cols // 2).astype(jnp.int32)
    return 1 + late, late


def pack(pieces, start):
    lane = lanes(pieces[0].shape[0])
    out = None
    for q, piece in enumerate(pieces):
        turn = (32 * q - start) % 128
        turned = pltpu.roll(piece, turn, 1) if turn else piece
        out = turned if out is None else jnp.where(lane >= 32 * q, turned, out)
    return out


def unpack(value, start):
    turns = [(start - 32 * q) % 128 for q in range(4)]
    return [pltpu.roll(value, turn, 1) if turn else value for turn in turns]


def pack_two(value):
    half = value.shape[0] // 2
    lane = lanes(half)
    middle = jnp.logical_and(lane >= 32, lane < 96)
    return jnp.where(middle, pltpu.roll(value[half:], 64, 1), value[:half])


def unpack_two(value):
    return jnp.concatenate([value, pltpu.roll(value, 64, 1)], 0)


def seam(a, b):
    return jnp.where(lanes(a.shape[0]) >= 96, a, b)


def present(near, k, value):
    return jnp.where(near[k][0], value, 0.0)


LATE = 8


def second_rule(pos, s):
    early = GROUP * groups_before()[1]
    done = jnp.logical_and(
        rows_within(pos, s, BORDER), jnp.logical_or(s >= early, columns_within(pos, s, BORDER))
    )
    inner = jnp.logical_and(rows_within(pos, s, 0), columns_within(pos, s, 0))
    return done, jnp.logical_and(inner, jnp.logical_not(done))


def keep_gradients(grads, cur, amps, probe, tabs, pos):
    def body(i, carry):
        slots = [i * GROUP + k for k in range(GROUP)]
        for s, grad in zip(slots, gradients(cur, amps, probe, tabs, pos, slots)):
            grads[s, 0], grads[s, 1] = turned(grad, pos, s)
        return carry

    return body


def halo_kernel(
    pos_far, obj, amps_far, probe_far, t0_far, t1_far, cur, acc, grads, amps, probe, t0, t1, hv, hc, hd, sc, sd, pos, send, recv, sems
):
    near = neighbours()
    greet(near)
    tile_at = [
        pltpu.make_async_copy(
            obj.at[:, :, pl.ds(128 * j, 128)], cur.at[:, j + 1, pl.ds(BORDER, TILE), :], sems.at[j]
        )
        for j in range(4)
    ]
    others = [
        pltpu.make_async_copy(there, here, sems.at[4 + n])
        for n, (there, here) in enumerate(
            ((probe_far, probe), (t0_far, t0), (t1_far, t1), (amps_far, amps), (pos_far, pos))
        )
    ]
    for copy in [tile_at[j] for j in (0, 3, 1, 2)] + others:
        copy.start()
    zeros = jnp.zeros((2, BLOCKS, BORDER, 128), f32)
    cur[:, :, 0:BORDER, :] = zeros
    cur[:, :, BORDER + TILE :, :] = zeros
    cur[:, 0] = jnp.zeros((2, ROWS, 128), f32)
    cur[:, 5] = jnp.zeros((2, ROWS, 128), f32)
    acc[...] = jnp.zeros_like(acc)
    for side in range(2):
        tile_at[3 * side].wait()
        block, start = 1 + 3 * side, 96 * side
        for p in range(2):
            sc[side, p] = pack(
                [cur[p, block, BORDER + 128 * q : BORDER + 128 * q + 128, :] for q in range(4)], start
            )
    greeted(near)
    post = Post(near, send, recv)
    sideways = post.pair(2, [sc.at[0], sc.at[1]], [hc.at[0], hc.at[1]])
    waits = [post.pair(0, [obj.at[:, pl.ds(0, 32), :], obj.at[:, pl.ds(TILE - 32, 32), :]], [hv.at[0], hv.at[1]])]
    for copy in [tile_at[1], tile_at[2]] + others:
        copy.wait()
    body = keep_gradients(grads, cur, amps, probe, (t0, t1), pos)
    before, _ = groups_before()
    lax.fori_loop(0, before, body, 0)
    sideways()
    for p in range(2):
        for side in range(2):
            for q, piece in enumerate(unpack(hc[side, p], 96 - 96 * side)):
                at = BORDER + 128 * q
                cur[p, 5 * side, at : at + 128, :] = present(near, 2 + side, piece)
        for ud in range(2):
            rows = pl.ds(BORDER + (TILE - BORDER) * ud, BORDER)
            sd[ud, p] = pack_two(seam(cur[p, 0, rows, :], cur[p, 5, rows, :]))
    waits.append(post.pair(0, [sd.at[0], sd.at[1]], [hd.at[0], hd.at[1]]))
    lax.fori_loop(before, PMAX // GROUP, body, 0)
    for wait in waits:
        wait()
    for p in range(2):
        for k in range(2):
            base = (BORDER + TILE) * k
            for j in range(4):
                cur[p, j + 1, base : base + 32, :] = present(near, k, hv[k, p, :, 128 * j : 128 * j + 128])
            beside = present(near, k, unpack_two(hd[k, p]))
            for side in range(2):
                cur[p, 5 * side, base : base + 32, :] = beside


def first_kernel(count, pos, acc_in, cur, grads, amps, probe, t0, t1, acc, todo):
    del acc_in
    early = GROUP * groups_before()[0]

    def sort(s, amount):
        done = jnp.logical_and(
            rows_within(pos, s, 0), jnp.logical_or(s >= early, columns_within(pos, s, 0))
        )

        @pl.when(done)
        def _():
            place(acc, (grads[s, 0], grads[s, 1]), pos, s)

        @pl.when(jnp.logical_not(done))
        def _():
            todo[amount] = s

        return amount + jnp.where(done, 0, 1)

    amount = lax.fori_loop(0, count[0, 0], sort, jnp.int32(0))
    listed_slots(amount, todo, pos, cur, acc, amps, probe, (t0, t1))


def side_sums(near, rc, rm, side, p):
    for rows, value in (
        (pl.ds(0, 64), rc[side, 0, p]),
        (pl.ds(64, TILE - 64), rm[side, p]),
        (pl.ds(TILE, 64), rc[side, 1, p]),
    ):
        yield rows, present(near, 2 + side, unpack_two(value))


def strip_kernel(
    pos, acc, cur_in, amps, probe, t0, t1, rate, grads, cur, sums, rv, rs, rc, rm, sv, ss, sc, sm, send, recv
):
    near = neighbours()
    greet(near)
    for p in range(2):
        for side in range(2):
            for ud in range(2):
                rows = pl.ds(TILE * ud, 64)
                sc[side, ud, p] = pack_two(seam(acc[p, 4 * side, rows, :], acc[p, 4 * side + 1, rows, :]))
    greeted(near)
    post = Post(near, send, recv)
    corners = post.pair(2, [sc.at[0], sc.at[1]], [rc.at[0], rc.at[1]])
    for p in range(2):
        for side in range(2):
            sm[side, p] = pack_two(seam(acc[p, 4 * side, 64:TILE, :], acc[p, 4 * side + 1, 64:TILE, :]))
    middle = post.pair(2, [sm.at[0], sm.at[1]], [rm.at[0], rm.at[1]])
    waits = [
        post.pair(
            0,
            [acc.at[:, pl.ds(2, 2), pl.ds(TILE * ud, 64), :] for ud in range(2)],
            [rv.at[ud, :, pl.ds(1, 2)] for ud in range(2)],
        )
    ]
    step = step_of(probe)
    rate[...] = jnp.full(rate.shape, step, f32)
    cur[...] = cur_in[...] + step * acc[...]
    corners()
    lane = lanes(64)
    for p in range(2):
        for ud in range(2):
            rows = pl.ds(TILE * ud, 64)
            west = present(near, 2, unpack_two(rc[0, ud, p]))
            east = present(near, 3, unpack_two(rc[1, ud, p]))
            sv[ud, p, 0] = acc[p, 1, rows, :] + jnp.where(lane < 32, west, 0.0)
            sv[ud, p, 1] = acc[p, 4, rows, :] + jnp.where(lane >= 96, east, 0.0)
            ss[ud, p] = pack_two(seam(acc[p, 0, rows, :] + west, acc[p, 5, rows, :] + east))
    for n, block in ((0, 0), (1, 3)):
        waits.append(
            post.pair(0, [sv.at[ud, :, n] for ud in range(2)], [rv.at[ud, :, block] for ud in range(2)])
        )
    waits.append(post.pair(0, [ss.at[0], ss.at[1]], [rs.at[0], rs.at[1]]))
    for k in range(2):
        outside = pl.ds((BORDER + TILE) * k, BORDER)
        cur[:, :, outside, :] = present(near, k, cur[:, :, outside, :])
        cur[:, 5 * k] = present(near, 2 + k, cur[:, 5 * k])
    body = keep_gradients(grads, cur, amps, probe, (t0, t1), pos)
    _, before = groups_before()
    lax.fori_loop(0, before, body, 0)
    middle()
    for p in range(2):
        for side in range(2):
            for rows, value in side_sums(near, rc, rm, side, p):
                lane = lanes(value.shape[0])
                for block, mine in ((4 * side, lane >= 96), (4 * side + 1, lane < 32)):
                    cur[p, block, rows, :] += step * jnp.where(mine, value, 0.0)
        for k in range(2):
            outside = pl.ds((BORDER + TILE) * k, BORDER)
            for block in (1, 4):
                cur[p, block, outside, :] = present(near, k, cur[p, block, outside, :])
                cur[p, 5 * (block // 4), outside, :] = present(near, k, cur[p, 5 * (block // 4), outside, :])
    lax.fori_loop(before, PMAX // GROUP, body, 0)
    sums[:, 1:5] = acc[:, 1:5]
    for p in range(2):
        for side in range(2):
            for rows, value in side_sums(near, rc, rm, side, p):
                lane = lanes(value.shape[0])
                sums[p, 1 + 3 * side, rows, :] += jnp.where(lane >= 96 if side else lane < 32, value, 0.0)
    for k in range(2):
        sums[:, 1:5, pl.ds((BORDER + TILE) * k, BORDER), :] = jnp.zeros((2, 4, BORDER, 128), f32)
        sums[:, 5 * k] = jnp.zeros((2, ROWS, 128), f32)
    for wait in waits:
        wait()


def second_kernel(
    count, pos, acc_in, cur_in, rv, rs, rate, grads, amps, probe, t0, t1, acc, cur, todo
):
    near = neighbours()
    step = rate[0:1, :]
    del acc_in, cur_in
    lane = lanes(64)
    for p in range(2):
        for ud in range(2):
            rows = pl.ds(TILE * ud, 64)
            inner, at = pl.ds(BORDER + (TILE - 32) * ud, 32), slice(32 - 32 * ud, 64 - 32 * ud)
            for j in range(4):
                value = present(near, ud, rv[ud, p, j])
                cur[p, j + 1, rows, :] += step * value
                acc[p, j + 1, inner, :] += value[at]
            value = step * present(near, ud, unpack_two(rs[ud, p]))
            for side, mine in ((0, lane >= 96), (1, lane < 32)):
                mine = jnp.logical_and(mine, near[2 + side][0])
                cur[p, 5 * side, rows, :] += jnp.where(mine, value, 0.0)
    def sort(s, carry):
        amount, held = carry
        done, hold = second_rule(pos, s)
        hold = jnp.logical_and(hold, held < LATE)

        @pl.when(done)
        def _():
            place(acc, (grads[s, 0], grads[s, 1]), pos, s)

        now = jnp.logical_not(jnp.logical_or(done, hold))

        @pl.when(now)
        def _():
            todo[amount] = s

        return amount + jnp.where(now, 1, 0), held + jnp.where(hold, 1, 0)

    amount, _ = lax.fori_loop(0, count[0, 0], sort, (jnp.int32(0), jnp.int32(0)))
    listed_slots(amount, todo, pos, cur, acc, amps, probe, (t0, t1))


def fold_kernel(
    count, pos, acc, cur, amps, probe, t0, t1, grads, gv, gc, gd, sc, sd, sv, late, follow, send, recv
):
    near = neighbours()
    greet(near)
    for p in range(2):
        for side in range(2):
            for ud in range(2):
                base = (BORDER + TILE) * ud
                sd[side, ud, p] = pack(
                    [acc[p, 5 * side, base + 8 * q : base + 8 * q + 8, :] for q in range(4)], 96 - 96 * side
                )
    greeted(near)
    post = Post(near, send, recv)
    corners = post.pair(2, [sd.at[0], sd.at[1]], [gd.at[0], gd.at[1]])
    waits = [
        post.pair(
            0,
            [acc.at[:, pl.ds(2, 2), pl.ds((BORDER + TILE) * ud, BORDER), :] for ud in range(2)],
            [gv.at[ud, :, pl.ds(1, 2)] for ud in range(2)],
        )
    ]
    for p in range(2):
        for side in range(2):
            sc[side, p] = pack(
                [acc[p, 5 * side, BORDER + 128 * q : BORDER + 128 * q + 128, :] for q in range(4)], 96 - 96 * side
            )
    waits.append(post.pair(2, [sc.at[0], sc.at[1]], [gc.at[0], gc.at[1]]))
    corners()
    lane = lanes(BORDER)
    for p in range(2):
        for ud in range(2):
            rows = pl.ds((BORDER + TILE) * ud, BORDER)
            for side in range(2):
                beside = present(near, 2 + side, jnp.concatenate(unpack(gd[side, ud, p], 96 * side), 0))
                mine = lane >= 96 if side else lane < 32
                sv[ud, p, side] = acc[p, 1 + 3 * side, rows, :] + jnp.where(mine, beside, 0.0)
    for side in range(2):
        waits.append(
            post.pair(0, [sv.at[ud, :, side] for ud in range(2)], [gv.at[ud, :, 3 * side] for ud in range(2)])
        )

    coming = jnp.int32(PMAX)
    follow[PMAX] = coming
    for s in range(PMAX - 1, -1, -1):
        hold = jnp.logical_and(s < count[0, 0], second_rule(pos, s)[1])
        coming = jnp.where(hold, s, coming)
        follow[s] = coming
    for k in range(LATE):
        late[k] = coming
        coming = follow[jnp.minimum(coming + 1, PMAX)]

    def body(i, carry):
        slots = [jnp.minimum(late[i * GROUP + k], PMAX - 1) for k in range(GROUP)]
        for k, grad in enumerate(gradients(cur, amps, probe, (t0, t1), pos, slots)):
            grads[i * GROUP + k, 0], grads[i * GROUP + k, 1] = turned(grad, pos, slots[k])
        return carry

    lax.fori_loop(0, LATE // GROUP, body, 0)
    for wait in waits:
        wait()


def last_kernel(count, pos, obj, acc_in, gv, gc, grads, rate, est_out, corr_out, acc, est, sems):
    near = neighbours()
    del acc_in
    step = rate[0:1, :]

    def put(s, held):
        hold = jnp.logical_and(second_rule(pos, s)[1], held < LATE)

        @pl.when(hold)
        def _():
            place(acc, (grads[held, 0], grads[held, 1]), pos, s)

        return held + jnp.where(hold, 1, 0)

    lax.fori_loop(0, count[0, 0], put, jnp.int32(0))
    inner = pl.ds(BORDER, TILE)
    stores = []

    def leave(j):
        out = pl.ds(128 * j, 128)
        acc[:, j + 1, inner, :] = step * acc[:, j + 1, inner, :]
        stores.append(pltpu.make_async_copy(acc.at[:, j + 1, inner, :], corr_out.at[:, :, out], sems.at[j]))
        stores[-1].start()
        est[:, j] = obj[:, :, 128 * j : 128 * j + 128] + acc[:, j + 1, inner, :]
        stores.append(pltpu.make_async_copy(est.at[:, j], est_out.at[:, :, out], sems.at[4 + j]))
        stores[-1].start()

    for j in (1, 2, 0, 3):
        for p in range(2):
            for ud in range(2):
                base = BORDER + (TILE - 32) * ud
                acc[p, j + 1, base : base + 32, :] += present(near, ud, gv[ud, p, j])
        if j in (0, 3):
            side, block, start = j // 3, j + 1, 32 * j

            def mine(rows):
                return lanes(rows) >= 96 if side else lanes(rows) < 32

            for p in range(2):
                for q, piece in enumerate(unpack(gc[side, p], start)):
                    at = BORDER + 128 * q
                    acc[p, block, at : at + 128, :] += jnp.where(mine(128), present(near, 2 + side, piece), 0.0)
        leave(j)
    for store in stores:
        store.wait()


VM = pl.BlockSpec(memory_space=pltpu.VMEM)
SM = pl.BlockSpec(memory_space=pltpu.SMEM)
HBM = pl.BlockSpec(memory_space=pltpu.HBM)


def shape(*dims, dtype=f32):
    return jax.ShapeDtypeStruct(dims, dtype)


def params(limit_mib=14, **kw):
    return pltpu.CompilerParams(vmem_limit_bytes=limit_mib * 2**20, **kw)


def remote_params(which):
    return params(collective_id=which, has_side_effects=True)


def on_device(object_field, probe_field, amplitudes, positions, counts):
    tabs = [jnp.asarray(t) for t in tables()]
    dma = pltpu.SemaphoreType.DMA
    tile = shape(2, BLOCKS, ROWS, 128)
    kept = shape(PMAX, 2, PROBE, PROBE)
    far = [
        pltpu.with_memory_space_constraint(x, pltpu.HBM)
        for x in (positions, object_field, amplitudes, probe_field, *tabs)
    ]
    cur, acc, grads, *shared = pl.pallas_call(
        halo_kernel,
        out_shape=[tile, tile, kept]
        + [jax.ShapeDtypeStruct(x.shape, x.dtype) for x in (amplitudes, probe_field, *tabs)],
        in_specs=[HBM] * 6,
        out_specs=[VM] * 7,
        scratch_shapes=[
            pltpu.VMEM((2, 2, 32, TILE), f32),
            pltpu.VMEM((2, 2, 128, 128), f32),
            pltpu.VMEM((2, 2, 16, 128), f32),
            pltpu.VMEM((2, 2, 128, 128), f32),
            pltpu.VMEM((2, 2, 16, 128), f32),
            pltpu.SMEM((1, 1, 2, PMAX), jnp.int32),
            dma((8,)),
            dma((8,)),
            dma((9,)),
        ],
        compiler_params=remote_params(0),
        name="halo",
    )(*far)
    acc = pl.pallas_call(
        first_kernel,
        out_shape=tile,
        in_specs=[SM, SM] + [VM] * 7,
        out_specs=VM,
        scratch_shapes=[pltpu.SMEM((PMAX,), jnp.int32)],
        input_output_aliases={2: 0},
        compiler_params=params(),
        name="first",
    )(counts, positions, acc, cur, grads, *shared)
    strips = ((2, 2, 4, 64, 128), (2, 2, 32, 128), (2, 2, 2, 32, 128), (2, 2, 224, 128))
    rate, grads, cur, sums, rv, rs, *_ = pl.pallas_call(
        strip_kernel,
        out_shape=(shape(8, 128), kept, tile, tile) + tuple(shape(*s) for s in strips),
        in_specs=[SM] + [VM] * 6,
        out_specs=[VM] * 8,
        scratch_shapes=[
            pltpu.VMEM((2, 2, 2, 64, 128), f32),
            pltpu.VMEM((2, 2, 32, 128), f32),
            pltpu.VMEM((2, 2, 2, 32, 128), f32),
            pltpu.VMEM((2, 2, 224, 128), f32),
            dma((12,)),
            dma((12,)),
        ],
        compiler_params=remote_params(1),
        name="strips",
    )(positions, acc, cur, *shared)
    acc, cur = pl.pallas_call(
        second_kernel,
        out_shape=(tile, tile),
        in_specs=[SM, SM] + [VM] * 10,
        out_specs=[VM, VM],
        scratch_shapes=[pltpu.SMEM((PMAX,), jnp.int32)],
        input_output_aliases={2: 0, 3: 1},
        compiler_params=params(),
        name="second",
    )(counts, positions, sums, cur, rv, rs, rate, grads, *shared)
    folds = ((2, 2, 4, 32, 128), (2, 2, 128, 128))
    grads, gv, gc = pl.pallas_call(
        fold_kernel,
        out_shape=(shape(LATE, 2, PROBE, PROBE),) + tuple(shape(*s) for s in folds),
        in_specs=[SM, SM] + [VM] * 6,
        out_specs=[VM] * 3,
        scratch_shapes=[
            pltpu.VMEM((2, 2, 2, 8, 128), f32),
            pltpu.VMEM((2, 2, 128, 128), f32),
            pltpu.VMEM((2, 2, 2, 8, 128), f32),
            pltpu.VMEM((2, 2, 2, 32, 128), f32),
            pltpu.SMEM((LATE,), jnp.int32),
            pltpu.SMEM((PMAX + 1,), jnp.int32),
            dma((10,)),
            dma((10,)),
        ],
        compiler_params=remote_params(2),
        name="folds",
    )(counts, positions, acc, cur, *shared)
    return pl.pallas_call(
        last_kernel,
        out_shape=(shape(2, TILE, TILE), shape(2, TILE, TILE), tile),
        in_specs=[SM, SM] + [VM] * 6,
        out_specs=[HBM, HBM, VM],
        scratch_shapes=[pltpu.VMEM((2, 4, TILE, 128), f32), dma((8,))],
        input_output_aliases={3: 2},
        compiler_params=params(),
        name="last",
    )(counts, positions, object_field, acc, gv, gc, grads, rate)[:2]


def solution(mesh):
    placed = (
        P(None, "row", "col"),
        P(),
        P("row", None, "col"),
        P("row", "col", None, None),
        P("row", "col"),
    )
    return jax.shard_map(
        on_device,
        mesh=mesh,
        in_specs=placed,
        out_specs=(P(None, "row", "col"), P(None, "row", "col")),
        check_vma=False,
    )
```

```python
import functools

import jax
import jax.numpy as jnp
import ml_dtypes
import numpy as np
from jax import lax
from jax.experimental import pallas as pl
from jax.experimental.pallas import tpu as pltpu
from jax.sharding import PartitionSpec as P

BORDER = 32
PROBE = 128
TILE = 512
PMAX = 24
ROWS = TILE + 2 * BORDER
BLOCKS = 6
GROUP = 8
smoothing = 0.5
step_gain = 0.5
f32 = jnp.float32
bf16 = jnp.bfloat16
MESH = pl.DeviceIdType.MESH

DIRS = ((-1, 0), (1, 0), (0, -1), (0, 1))
OPP = (1, 0, 3, 2)


def tables():
    n = np.arange(PROBE)
    angle = 2.0 * np.pi / PROBE * (n[:, None] * n[None, :] % PROBE)
    real, imag = np.cos(angle) / np.sqrt(PROBE), -np.sin(angle) / np.sqrt(PROBE)
    whole = np.block([[real, -imag], [imag, real]]).astype(np.float32)

    def halves(matrix):
        high = matrix.astype(ml_dtypes.bfloat16)
        return high, (matrix - high.astype(np.float32)).astype(ml_dtypes.bfloat16)

    return np.stack(halves(whole)), np.stack(halves(whole.T.copy()))


def split(value):
    high = value.astype(bf16)
    return high, (value - high.astype(f32)).astype(bf16)


def dot(a, b):
    return jnp.dot(a, b, preferred_element_type=f32)


def left(table, pairs):
    parts = [split(jnp.concatenate([a, b], 0)) for a, b in pairs]
    high = jnp.concatenate([p[0] for p in parts], 1)
    low = jnp.concatenate([p[1] for p in parts], 1)
    wide = jnp.concatenate([table[0], table[0], table[1]], 1)
    out = dot(wide, jnp.concatenate([high, low, high], 0))
    n = PROBE
    return [(out[:n, n * k : n * k + n], out[n:, n * k : n * k + n]) for k in range(len(pairs))]


def right(table, pairs):
    parts = [split(jnp.concatenate([a, b], 1)) for a, b in pairs]
    high = jnp.concatenate([p[0] for p in parts], 0)
    low = jnp.concatenate([p[1] for p in parts], 0)
    tall = jnp.concatenate([table[0], table[0], table[1]], 0)
    out = dot(jnp.concatenate([high, low, high], 1), tall)
    n = PROBE
    return [(out[n * k : n * k + n, :n], out[n * k : n * k + n, n:]) for k in range(len(pairs))]


def lanes(rows=PROBE):
    return lax.broadcasted_iota(jnp.int32, (rows, 128), 1)


def cut(cur, row, col):
    block, lane = col >> 7, col & 127
    out = []
    for p in range(2):
        a = cur[p, block, pl.ds(row, PROBE), :]
        b = cur[p, block + 1, pl.ds(row, PROBE), :]
        out.append(pltpu.roll(jnp.where(lanes() >= lane, a, b), (128 - lane) & 127, 1))
    return out


def turned(grad, pos, s):
    lane = corner_of(pos, s)[1] & 127
    return [pltpu.roll(g, lane, 1) for g in grad]


def place(acc, grad, pos, s):
    row, col = corner_of(pos, s)
    block, lane = col >> 7, col & 127
    rows = pl.ds(row, PROBE)
    first = lanes() >= lane
    for p in range(2):
        a, b = acc[p, block, rows, :], acc[p, block + 1, rows, :]
        acc[p, block, rows, :] = a + jnp.where(first, grad[p], 0.0)
        acc[p, block + 1, rows, :] = b + jnp.where(first, 0.0, grad[p])


def gradients(cur, amps, probe, tabs, pos, slots, scale=None):
    forward, backward = tabs
    pr, pi = probe[0], probe[1]
    pairs = []
    for s in slots:
        a, b = cut(cur, *corner_of(pos, s))
        pairs.append((pr * a - pi * b, pr * b + pi * a))
    waves = left(forward, right(backward, pairs))
    shrunk = []
    for k, ((a, b), s) in enumerate(zip(waves, slots)):
        gain = amps[s] * lax.rsqrt(a * a + b * b + smoothing) - 1.0
        if scale is not None:
            gain = gain * scale[k]
        shrunk.append((a * gain, b * gain))
    backs = right(forward, left(backward, shrunk))
    return [(pr * a + pi * b, pr * b - pi * a) for a, b in backs]


def corner_of(pos, s):
    return pos[0, 0, 0, s] + BORDER, pos[0, 0, 1, s] + 128


def within(start, margin):
    return jnp.logical_and(start >= margin, start <= TILE - PROBE - margin)


def rows_within(pos, s, margin):
    return within(pos[0, 0, 0, s], margin)


def columns_within(pos, s, margin):
    return within(pos[0, 0, 1, s], margin)


def listed_slots(amount, todo, pos, cur, acc, amps, probe, tabs):
    def some(start, size):
        at = [start + k for k in range(size)]
        slots = [jnp.where(j < amount, todo[j], 0) for j in at]
        scale = [jnp.where(j < amount, 1.0, 0.0) for j in at]
        grads = gradients(cur, amps, probe, tabs, pos, slots, scale)
        grads = [turned(grad, pos, s) for grad, s in zip(grads, slots)]
        for grad, s in zip(grads, slots):
            place(acc, grad, pos, s)

    def body(i, carry):
        some(i * GROUP, GROUP)
        return carry

    full = lax.div(amount + 1, GROUP)
    lax.fori_loop(0, full, body, 0)
    rest = amount - full * GROUP
    for least, size in ((1, 4), (5, 6)):

        @pl.when(jnp.logical_and(rest >= least, rest <= size))
        def _():
            some(full * GROUP, size)


def step_of(probe):
    return step_gain / (jnp.max(probe[0] * probe[0] + probe[1] * probe[1]) + 1e-06)


def neighbours():
    rows, cols = lax.axis_size("row"), lax.axis_size("col")
    row, col = lax.axis_index("row"), lax.axis_index("col")
    out = []
    for dr, dc in DIRS:
        there = None
        for cond in (
            [row > 0] if dr < 0 else [row < rows - 1] if dr > 0 else []
        ) + ([col > 0] if dc < 0 else [col < cols - 1] if dc > 0 else []):
            there = cond if there is None else jnp.logical_and(there, cond)
        out.append((there, (row + dr, col + dc)))
    return out


def greet(near):
    barrier = pltpu.get_barrier_semaphore()
    for there, where in near:
        @pl.when(there)
        def _():
            pl.semaphore_signal(barrier, inc=1, device_id=where, device_id_type=MESH)


def greeted(near):
    total = 0
    for there, _ in near:
        total = total + there.astype(jnp.int32)
    pl.semaphore_wait(pltpu.get_barrier_semaphore(), total)


def remote(k, near, source, target, send, recv, n):
    return pltpu.make_async_remote_copy(
        src_ref=source,
        dst_ref=target,
        send_sem=send.at[n],
        recv_sem=recv.at[n],
        device_id=near[k][1],
        device_id_type=MESH,
    )


class Post:
    def __init__(self, near, send, recv):
        self.near, self.send, self.recv = near, send, recv
        self.count, self.waits = 0, []

    def pair(self, k, outs, intos):
        for i, way in enumerate((k, OPP[k])):
            n = self.count + i
            @pl.when(self.near[way][0])
            def _(i=i, way=way, n=n):
                remote(way, self.near, outs[i], intos[1 - i], self.send, self.recv, n).start()

        def wait(base=self.count):
            for i, way in enumerate((k, OPP[k])):
                @pl.when(self.near[way][0])
                def _(i=i, way=way):
                    remote(way, self.near, outs[i], intos[i], self.send, self.recv, base + i).wait_send()
                    remote(way, self.near, outs[i], intos[i], self.send, self.recv, base + 1 - i).wait_recv()

        self.count += 2
        return wait


def groups_before():
    cols, col = lax.axis_size("col"), lax.axis_index("col")
    late = jnp.logical_or(col == cols // 2 - 1, col == cols // 2).astype(jnp.int32)
    return 1 + late, late


def pack(pieces, start):
    lane = lanes(pieces[0].shape[0])
    out = None
    for q, piece in enumerate(pieces):
        turn = (32 * q - start) % 128
        turned = pltpu.roll(piece, turn, 1) if turn else piece
        out = turned if out is None else jnp.where(lane >= 32 * q, turned, out)
    return out


def unpack(value, start):
    turns = [(start - 32 * q) % 128 for q in range(4)]
    return [pltpu.roll(value, turn, 1) if turn else value for turn in turns]


def pack_two(value):
    half = value.shape[0] // 2
    lane = lanes(half)
    middle = jnp.logical_and(lane >= 32, lane < 96)
    return jnp.where(middle, pltpu.roll(value[half:], 64, 1), value[:half])


def unpack_two(value):
    return jnp.concatenate([value, pltpu.roll(value, 64, 1)], 0)


def seam(a, b):
    return jnp.where(lanes(a.shape[0]) >= 96, a, b)


def present(near, k, value):
    return jnp.where(near[k][0], value, 0.0)


LATE = 8


def second_rule(pos, s):
    early = GROUP * groups_before()[1]
    done = jnp.logical_and(
        rows_within(pos, s, BORDER), jnp.logical_or(s >= early, columns_within(pos, s, BORDER))
    )
    inner = jnp.logical_and(rows_within(pos, s, 0), columns_within(pos, s, 0))
    return done, jnp.logical_and(inner, jnp.logical_not(done))


def inside(pos, s):
    return jnp.logical_and(rows_within(pos, s, 0), columns_within(pos, s, 0))


def early_order(pos, early, ahead, behind, follow, follow_other):
    seen, taken = jnp.int32(0), []
    for s in range(PMAX):
        own = inside(pos, s)
        taken.append((own, jnp.logical_and(own, seen < early)))
        seen = seen + own.astype(jnp.int32)
    last = jnp.int32(PMAX)
    follow[PMAX], follow_other[PMAX] = last, last
    coming, other = last, last
    for s in range(PMAX - 1, -1, -1):
        coming, other = jnp.where(taken[s][0], s, coming), jnp.where(taken[s][1], other, s)
        follow[s], follow_other[s] = coming, other
    for k in range(PMAX):
        ahead[k], behind[k] = jnp.minimum(coming, PMAX - 1), jnp.minimum(other, PMAX - 1)
        coming = follow[jnp.minimum(coming + 1, PMAX)]
        other = follow_other[jnp.minimum(other + 1, PMAX)]

    def slot_at(k):
        return jnp.where(k < early, ahead[k], behind[jnp.maximum(k - early, 0)])

    return slot_at


def keep_gradients(grads, cur, amps, probe, tabs, pos, slot_at=lambda k: k):
    def body(i, carry):
        places = [i * GROUP + k for k in range(GROUP)]
        slots = [slot_at(k) for k in places]
        for k, s, grad in zip(places, slots, gradients(cur, amps, probe, tabs, pos, slots)):
            grads[k, 0], grads[k, 1] = turned(grad, pos, s)
        return carry

    return body


def halo_kernel(
    pos_far, obj, amps_far, probe_far, t0_far, t1_far, cur, acc, grads, amps, probe, t0, t1, hv, hc, hd, sc, sd, pos,
    ahead, behind, follow, follow_other, send, recv, sems
):
    near = neighbours()
    greet(near)
    tile_at = [
        pltpu.make_async_copy(
            obj.at[:, :, pl.ds(128 * j, 128)], cur.at[:, j + 1, pl.ds(BORDER, TILE), :], sems.at[j]
        )
        for j in range(4)
    ]
    others = [
        pltpu.make_async_copy(there, here, sems.at[4 + n])
        for n, (there, here) in enumerate(
            ((probe_far, probe), (t0_far, t0), (t1_far, t1), (amps_far, amps), (pos_far, pos))
        )
    ]
    for copy in [tile_at[j] for j in (0, 3, 1, 2)] + others:
        copy.start()
    zeros = jnp.zeros((2, BLOCKS, BORDER, 128), f32)
    cur[:, :, 0:BORDER, :] = zeros
    cur[:, :, BORDER + TILE :, :] = zeros
    cur[:, 0] = jnp.zeros((2, ROWS, 128), f32)
    cur[:, 5] = jnp.zeros((2, ROWS, 128), f32)
    acc[...] = jnp.zeros_like(acc)
    for side in range(2):
        tile_at[3 * side].wait()
        block, start = 1 + 3 * side, 96 * side
        for p in range(2):
            sc[side, p] = pack(
                [cur[p, block, BORDER + 128 * q : BORDER + 128 * q + 128, :] for q in range(4)], start
            )
    greeted(near)
    post = Post(near, send, recv)
    sideways = post.pair(2, [sc.at[0], sc.at[1]], [hc.at[0], hc.at[1]])
    waits = [post.pair(0, [obj.at[:, pl.ds(0, 32), :], obj.at[:, pl.ds(TILE - 32, 32), :]], [hv.at[0], hv.at[1]])]
    for copy in [tile_at[1], tile_at[2]] + others:
        copy.wait()
    before, _ = groups_before()
    slot_at = early_order(pos, GROUP * before, ahead, behind, follow, follow_other)
    body = keep_gradients(grads, cur, amps, probe, (t0, t1), pos, slot_at)
    lax.fori_loop(0, before, body, 0)
    sideways()
    for p in range(2):
        for side in range(2):
            for q, piece in enumerate(unpack(hc[side, p], 96 - 96 * side)):
                at = BORDER + 128 * q
                cur[p, 5 * side, at : at + 128, :] = present(near, 2 + side, piece)
        for ud in range(2):
            rows = pl.ds(BORDER + (TILE - BORDER) * ud, BORDER)
            sd[ud, p] = pack_two(seam(cur[p, 0, rows, :], cur[p, 5, rows, :]))
    waits.append(post.pair(0, [sd.at[0], sd.at[1]], [hd.at[0], hd.at[1]]))
    lax.fori_loop(before, PMAX // GROUP, body, 0)
    for wait in waits:
        wait()
    for p in range(2):
        for k in range(2):
            base = (BORDER + TILE) * k
            for j in range(4):
                cur[p, j + 1, base : base + 32, :] = present(near, k, hv[k, p, :, 128 * j : 128 * j + 128])
            beside = present(near, k, unpack_two(hd[k, p]))
            for side in range(2):
                cur[p, 5 * side, base : base + 32, :] = beside


def first_kernel(count, pos, acc_in, cur, grads, amps, probe, t0, t1, acc, todo):
    del acc_in
    early = GROUP * groups_before()[0]

    def sort(s, carry):
        amount, seen, others = carry
        own = inside(pos, s)
        taken = jnp.logical_and(own, seen < early)
        k = jnp.where(taken, seen, early + others)
        done = jnp.logical_or(taken, jnp.logical_and(rows_within(pos, s, 0), k < PMAX))

        @pl.when(done)
        def _():
            place(acc, (grads[k, 0], grads[k, 1]), pos, s)

        @pl.when(jnp.logical_not(done))
        def _():
            todo[amount] = s

        return (
            amount + jnp.where(done, 0, 1),
            seen + jnp.where(own, 1, 0),
            others + jnp.where(taken, 0, 1),
        )

    zero = jnp.int32(0)
    amount, _, _ = lax.fori_loop(0, count[0, 0], sort, (zero, zero, zero))
    listed_slots(amount, todo, pos, cur, acc, amps, probe, (t0, t1))


def side_sums(near, rc, rm, side, p):
    for rows, value in (
        (pl.ds(0, 64), rc[side, 0, p]),
        (pl.ds(64, TILE - 64), rm[side, p]),
        (pl.ds(TILE, 64), rc[side, 1, p]),
    ):
        yield rows, present(near, 2 + side, unpack_two(value))


def strip_kernel(
    pos, acc, cur_in, amps, probe, t0, t1, rate, grads, cur, sums, rv, rs, rc, rm, sv, ss, sc, sm, send, recv
):
    near = neighbours()
    greet(near)
    for p in range(2):
        for side in range(2):
            for ud in range(2):
                rows = pl.ds(TILE * ud, 64)
                sc[side, ud, p] = pack_two(seam(acc[p, 4 * side, rows, :], acc[p, 4 * side + 1, rows, :]))
    greeted(near)
    post = Post(near, send, recv)
    corners = post.pair(2, [sc.at[0], sc.at[1]], [rc.at[0], rc.at[1]])
    for p in range(2):
        for side in range(2):
            sm[side, p] = pack_two(seam(acc[p, 4 * side, 64:TILE, :], acc[p, 4 * side + 1, 64:TILE, :]))
    middle = post.pair(2, [sm.at[0], sm.at[1]], [rm.at[0], rm.at[1]])
    waits = [
        post.pair(
            0,
            [acc.at[:, pl.ds(2, 2), pl.ds(TILE * ud, 64), :] for ud in range(2)],
            [rv.at[ud, :, pl.ds(1, 2)] for ud in range(2)],
        )
    ]
    step = step_of(probe)
    rate[...] = jnp.full(rate.shape, step, f32)
    cur[...] = cur_in[...] + step * acc[...]
    corners()
    lane = lanes(64)
    for p in range(2):
        for ud in range(2):
            rows = pl.ds(TILE * ud, 64)
            west = present(near, 2, unpack_two(rc[0, ud, p]))
            east = present(near, 3, unpack_two(rc[1, ud, p]))
            sv[ud, p, 0] = acc[p, 1, rows, :] + jnp.where(lane < 32, west, 0.0)
            sv[ud, p, 1] = acc[p, 4, rows, :] + jnp.where(lane >= 96, east, 0.0)
            ss[ud, p] = pack_two(seam(acc[p, 0, rows, :] + west, acc[p, 5, rows, :] + east))
    for n, block in ((0, 0), (1, 3)):
        waits.append(
            post.pair(0, [sv.at[ud, :, n] for ud in range(2)], [rv.at[ud, :, block] for ud in range(2)])
        )
    waits.append(post.pair(0, [ss.at[0], ss.at[1]], [rs.at[0], rs.at[1]]))
    for k in range(2):
        outside = pl.ds((BORDER + TILE) * k, BORDER)
        cur[:, :, outside, :] = present(near, k, cur[:, :, outside, :])
        cur[:, 5 * k] = present(near, 2 + k, cur[:, 5 * k])
    body = keep_gradients(grads, cur, amps, probe, (t0, t1), pos)
    _, before = groups_before()
    lax.fori_loop(0, before, body, 0)
    middle()
    for p in range(2):
        for side in range(2):
            for rows, value in side_sums(near, rc, rm, side, p):
                lane = lanes(value.shape[0])
                for block, mine in ((4 * side, lane >= 96), (4 * side + 1, lane < 32)):
                    cur[p, block, rows, :] += step * jnp.where(mine, value, 0.0)
        for k in range(2):
            outside = pl.ds((BORDER + TILE) * k, BORDER)
            for block in (1, 4):
                cur[p, block, outside, :] = present(near, k, cur[p, block, outside, :])
                cur[p, 5 * (block // 4), outside, :] = present(near, k, cur[p, 5 * (block // 4), outside, :])
    lax.fori_loop(before, PMAX // GROUP, body, 0)
    sums[:, 1:5] = acc[:, 1:5]
    for p in range(2):
        for side in range(2):
            for rows, value in side_sums(near, rc, rm, side, p):
                lane = lanes(value.shape[0])
                sums[p, 1 + 3 * side, rows, :] += jnp.where(lane >= 96 if side else lane < 32, value, 0.0)
    for k in range(2):
        sums[:, 1:5, pl.ds((BORDER + TILE) * k, BORDER), :] = jnp.zeros((2, 4, BORDER, 128), f32)
        sums[:, 5 * k] = jnp.zeros((2, ROWS, 128), f32)
    for wait in waits:
        wait()


def second_kernel(
    count, pos, acc_in, cur_in, rv, rs, rate, grads, amps, probe, t0, t1, acc, cur, todo
):
    near = neighbours()
    step = rate[0:1, :]
    del acc_in, cur_in
    lane = lanes(64)
    for p in range(2):
        for ud in range(2):
            rows = pl.ds(TILE * ud, 64)
            inner, at = pl.ds(BORDER + (TILE - 32) * ud, 32), slice(32 - 32 * ud, 64 - 32 * ud)
            for j in range(4):
                value = present(near, ud, rv[ud, p, j])
                cur[p, j + 1, rows, :] += step * value
                acc[p, j + 1, inner, :] += value[at]
            value = step * present(near, ud, unpack_two(rs[ud, p]))
            for side, mine in ((0, lane >= 96), (1, lane < 32)):
                mine = jnp.logical_and(mine, near[2 + side][0])
                cur[p, 5 * side, rows, :] += jnp.where(mine, value, 0.0)
    def sort(s, carry):
        amount, held = carry
        done, hold = second_rule(pos, s)
        hold = jnp.logical_and(hold, held < LATE)

        @pl.when(done)
        def _():
            place(acc, (grads[s, 0], grads[s, 1]), pos, s)

        now = jnp.logical_not(jnp.logical_or(done, hold))

        @pl.when(now)
        def _():
            todo[amount] = s

        return amount + jnp.where(now, 1, 0), held + jnp.where(hold, 1, 0)

    amount, _ = lax.fori_loop(0, count[0, 0], sort, (jnp.int32(0), jnp.int32(0)))
    listed_slots(amount, todo, pos, cur, acc, amps, probe, (t0, t1))


def fold_kernel(
    count, pos, acc, cur, amps, probe, t0, t1, grads, gv, gc, gd, sc, sd, sv, late, follow, send, recv
):
    near = neighbours()
    greet(near)
    for p in range(2):
        for side in range(2):
            for ud in range(2):
                base = (BORDER + TILE) * ud
                sd[side, ud, p] = pack(
                    [acc[p, 5 * side, base + 8 * q : base + 8 * q + 8, :] for q in range(4)], 96 - 96 * side
                )
    greeted(near)
    post = Post(near, send, recv)
    corners = post.pair(2, [sd.at[0], sd.at[1]], [gd.at[0], gd.at[1]])
    waits = [
        post.pair(
            0,
            [acc.at[:, pl.ds(2, 2), pl.ds((BORDER + TILE) * ud, BORDER), :] for ud in range(2)],
            [gv.at[ud, :, pl.ds(1, 2)] for ud in range(2)],
        )
    ]
    for p in range(2):
        for side in range(2):
            sc[side, p] = pack(
                [acc[p, 5 * side, BORDER + 128 * q : BORDER + 128 * q + 128, :] for q in range(4)], 96 - 96 * side
            )
    waits.append(post.pair(2, [sc.at[0], sc.at[1]], [gc.at[0], gc.at[1]]))
    corners()
    lane = lanes(BORDER)
    for p in range(2):
        for ud in range(2):
            rows = pl.ds((BORDER + TILE) * ud, BORDER)
            for side in range(2):
                beside = present(near, 2 + side, jnp.concatenate(unpack(gd[side, ud, p], 96 * side), 0))
                mine = lane >= 96 if side else lane < 32
                sv[ud, p, side] = acc[p, 1 + 3 * side, rows, :] + jnp.where(mine, beside, 0.0)
    for side in range(2):
        waits.append(
            post.pair(0, [sv.at[ud, :, side] for ud in range(2)], [gv.at[ud, :, 3 * side] for ud in range(2)])
        )

    coming = jnp.int32(PMAX)
    follow[PMAX] = coming
    for s in range(PMAX - 1, -1, -1):
        hold = jnp.logical_and(s < count[0, 0], second_rule(pos, s)[1])
        coming = jnp.where(hold, s, coming)
        follow[s] = coming
    for k in range(LATE):
        late[k] = coming
        coming = follow[jnp.minimum(coming + 1, PMAX)]

    def body(i, carry):
        slots = [jnp.minimum(late[i * GROUP + k], PMAX - 1) for k in range(GROUP)]
        for k, grad in enumerate(gradients(cur, amps, probe, (t0, t1), pos, slots)):
            grads[i * GROUP + k, 0], grads[i * GROUP + k, 1] = turned(grad, pos, slots[k])
        return carry

    lax.fori_loop(0, LATE // GROUP, body, 0)
    for wait in waits:
        wait()


def last_kernel(count, pos, obj, acc_in, gv, gc, grads, rate, est_out, corr_out, acc, est, sems):
    near = neighbours()
    del acc_in
    step = rate[0:1, :]

    def put(s, held):
        hold = jnp.logical_and(second_rule(pos, s)[1], held < LATE)

        @pl.when(hold)
        def _():
            place(acc, (grads[held, 0], grads[held, 1]), pos, s)

        return held + jnp.where(hold, 1, 0)

    lax.fori_loop(0, count[0, 0], put, jnp.int32(0))
    inner = pl.ds(BORDER, TILE)
    stores = []

    def leave(j):
        out = pl.ds(128 * j, 128)
        acc[:, j + 1, inner, :] = step * acc[:, j + 1, inner, :]
        stores.append(pltpu.make_async_copy(acc.at[:, j + 1, inner, :], corr_out.at[:, :, out], sems.at[j]))
        stores[-1].start()
        est[:, j] = obj[:, :, 128 * j : 128 * j + 128] + acc[:, j + 1, inner, :]
        stores.append(pltpu.make_async_copy(est.at[:, j], est_out.at[:, :, out], sems.at[4 + j]))
        stores[-1].start()

    for j in (1, 2, 0, 3):
        for p in range(2):
            for ud in range(2):
                base = BORDER + (TILE - 32) * ud
                acc[p, j + 1, base : base + 32, :] += present(near, ud, gv[ud, p, j])
        if j in (0, 3):
            side, block, start = j // 3, j + 1, 32 * j

            def mine(rows):
                return lanes(rows) >= 96 if side else lanes(rows) < 32

            for p in range(2):
                for q, piece in enumerate(unpack(gc[side, p], start)):
                    at = BORDER + 128 * q
                    acc[p, block, at : at + 128, :] += jnp.where(mine(128), present(near, 2 + side, piece), 0.0)
        leave(j)
    for store in stores:
        store.wait()


VM = pl.BlockSpec(memory_space=pltpu.VMEM)
SM = pl.BlockSpec(memory_space=pltpu.SMEM)
HBM = pl.BlockSpec(memory_space=pltpu.HBM)


def shape(*dims, dtype=f32):
    return jax.ShapeDtypeStruct(dims, dtype)


def params(limit_mib=14, **kw):
    return pltpu.CompilerParams(vmem_limit_bytes=limit_mib * 2**20, **kw)


def remote_params(which):
    return params(collective_id=which, has_side_effects=True)


def on_device(object_field, probe_field, amplitudes, positions, counts):
    tabs = [jnp.asarray(t) for t in tables()]
    dma = pltpu.SemaphoreType.DMA
    tile = shape(2, BLOCKS, ROWS, 128)
    kept = shape(PMAX, 2, PROBE, PROBE)
    far = [
        pltpu.with_memory_space_constraint(x, pltpu.HBM)
        for x in (positions, object_field, amplitudes, probe_field, *tabs)
    ]
    cur, acc, grads, *shared = pl.pallas_call(
        halo_kernel,
        out_shape=[tile, tile, kept]
        + [jax.ShapeDtypeStruct(x.shape, x.dtype) for x in (amplitudes, probe_field, *tabs)],
        in_specs=[HBM] * 6,
        out_specs=[VM] * 7,
        scratch_shapes=[
            pltpu.VMEM((2, 2, 32, TILE), f32),
            pltpu.VMEM((2, 2, 128, 128), f32),
            pltpu.VMEM((2, 2, 16, 128), f32),
            pltpu.VMEM((2, 2, 128, 128), f32),
            pltpu.VMEM((2, 2, 16, 128), f32),
            pltpu.SMEM((1, 1, 2, PMAX), jnp.int32),
            *[pltpu.SMEM((n,), jnp.int32) for n in (PMAX, PMAX, PMAX + 1, PMAX + 1)],
            dma((8,)),
            dma((8,)),
            dma((9,)),
        ],
        compiler_params=remote_params(0),
        name="halo",
    )(*far)
    acc = pl.pallas_call(
        first_kernel,
        out_shape=tile,
        in_specs=[SM, SM] + [VM] * 7,
        out_specs=VM,
        scratch_shapes=[pltpu.SMEM((PMAX,), jnp.int32)],
        input_output_aliases={2: 0},
        compiler_params=params(),
        name="first",
    )(counts, positions, acc, cur, grads, *shared)
    strips = ((2, 2, 4, 64, 128), (2, 2, 32, 128), (2, 2, 2, 32, 128), (2, 2, 224, 128))
    rate, grads, cur, sums, rv, rs, *_ = pl.pallas_call(
        strip_kernel,
        out_shape=(shape(8, 128), kept, tile, tile) + tuple(shape(*s) for s in strips),
        in_specs=[SM] + [VM] * 6,
        out_specs=[VM] * 8,
        scratch_shapes=[
            pltpu.VMEM((2, 2, 2, 64, 128), f32),
            pltpu.VMEM((2, 2, 32, 128), f32),
            pltpu.VMEM((2, 2, 2, 32, 128), f32),
            pltpu.VMEM((2, 2, 224, 128), f32),
            dma((12,)),
            dma((12,)),
        ],
        compiler_params=remote_params(1),
        name="strips",
    )(positions, acc, cur, *shared)
    acc, cur = pl.pallas_call(
        second_kernel,
        out_shape=(tile, tile),
        in_specs=[SM, SM] + [VM] * 10,
        out_specs=[VM, VM],
        scratch_shapes=[pltpu.SMEM((PMAX,), jnp.int32)],
        input_output_aliases={2: 0, 3: 1},
        compiler_params=params(),
        name="second",
    )(counts, positions, sums, cur, rv, rs, rate, grads, *shared)
    folds = ((2, 2, 4, 32, 128), (2, 2, 128, 128))
    grads, gv, gc = pl.pallas_call(
        fold_kernel,
        out_shape=(shape(LATE, 2, PROBE, PROBE),) + tuple(shape(*s) for s in folds),
        in_specs=[SM, SM] + [VM] * 6,
        out_specs=[VM] * 3,
        scratch_shapes=[
            pltpu.VMEM((2, 2, 2, 8, 128), f32),
            pltpu.VMEM((2, 2, 128, 128), f32),
            pltpu.VMEM((2, 2, 2, 8, 128), f32),
            pltpu.VMEM((2, 2, 2, 32, 128), f32),
            pltpu.SMEM((LATE,), jnp.int32),
            pltpu.SMEM((PMAX + 1,), jnp.int32),
            dma((10,)),
            dma((10,)),
        ],
        compiler_params=remote_params(2),
        name="folds",
    )(counts, positions, acc, cur, *shared)
    return pl.pallas_call(
        last_kernel,
        out_shape=(shape(2, TILE, TILE), shape(2, TILE, TILE), tile),
        in_specs=[SM, SM] + [VM] * 6,
        out_specs=[HBM, HBM, VM],
        scratch_shapes=[pltpu.VMEM((2, 4, TILE, 128), f32), dma((8,))],
        input_output_aliases={3: 2},
        compiler_params=params(),
        name="last",
    )(counts, positions, object_field, acc, gv, gc, grads, rate)[:2]


def solution(mesh):
    placed = (
        P(None, "row", "col"),
        P(),
        P("row", None, "col"),
        P("row", "col", None, None),
        P("row", "col"),
    )
    return jax.shard_map(
        on_device,
        mesh=mesh,
        in_specs=placed,
        out_specs=(P(None, "row", "col"), P(None, "row", "col")),
        check_vma=False,
    )
```

```python
import functools

import jax
import jax.numpy as jnp
import ml_dtypes
import numpy as np
from jax import lax
from jax.experimental import pallas as pl
from jax.experimental.pallas import tpu as pltpu
from jax.sharding import PartitionSpec as P

BORDER = 32
PROBE = 128
TILE = 512
PMAX = 24
ROWS = TILE + 2 * BORDER
BLOCKS = 6
GROUP = 8
smoothing = 0.5
step_gain = 0.5
f32 = jnp.float32
bf16 = jnp.bfloat16
MESH = pl.DeviceIdType.MESH

DIRS = ((-1, 0), (1, 0), (0, -1), (0, 1))
OPP = (1, 0, 3, 2)


def tables():
    n = np.arange(PROBE)
    angle = 2.0 * np.pi / PROBE * (n[:, None] * n[None, :] % PROBE)
    real, imag = np.cos(angle) / np.sqrt(PROBE), -np.sin(angle) / np.sqrt(PROBE)
    whole = np.block([[real, -imag], [imag, real]]).astype(np.float32)

    def halves(matrix):
        high = matrix.astype(ml_dtypes.bfloat16)
        return high, (matrix - high.astype(np.float32)).astype(ml_dtypes.bfloat16)

    return np.stack(halves(whole)), np.stack(halves(whole.T.copy()))


def split(value):
    high = value.astype(bf16)
    return high, (value - high.astype(f32)).astype(bf16)


def dot(a, b):
    return jnp.dot(a, b, preferred_element_type=f32)


def left(table, pairs):
    parts = [split(jnp.concatenate([a, b], 0)) for a, b in pairs]
    high = jnp.concatenate([p[0] for p in parts], 1)
    low = jnp.concatenate([p[1] for p in parts], 1)
    wide = jnp.concatenate([table[0], table[0], table[1]], 1)
    out = dot(wide, jnp.concatenate([high, low, high], 0))
    n = PROBE
    return [(out[:n, n * k : n * k + n], out[n:, n * k : n * k + n]) for k in range(len(pairs))]


def right(table, pairs):
    parts = [split(jnp.concatenate([a, b], 1)) for a, b in pairs]
    high = jnp.concatenate([p[0] for p in parts], 0)
    low = jnp.concatenate([p[1] for p in parts], 0)
    tall = jnp.concatenate([table[0], table[0], table[1]], 0)
    out = dot(jnp.concatenate([high, low, high], 1), tall)
    n = PROBE
    return [(out[n * k : n * k + n, :n], out[n * k : n * k + n, n:]) for k in range(len(pairs))]


def lanes(rows=PROBE):
    return lax.broadcasted_iota(jnp.int32, (rows, 128), 1)


def cut(cur, row, col):
    block, lane = col >> 7, col & 127
    out = []
    for p in range(2):
        a = cur[p, block, pl.ds(row, PROBE), :]
        b = cur[p, block + 1, pl.ds(row, PROBE), :]
        out.append(pltpu.roll(jnp.where(lanes() >= lane, a, b), (128 - lane) & 127, 1))
    return out


def turned(grad, pos, s):
    lane = corner_of(pos, s)[1] & 127
    return [pltpu.roll(g, lane, 1) for g in grad]


def place(acc, grad, pos, s):
    row, col = corner_of(pos, s)
    block, lane = col >> 7, col & 127
    rows = pl.ds(row, PROBE)
    first = lanes() >= lane
    for p in range(2):
        a, b = acc[p, block, rows, :], acc[p, block + 1, rows, :]
        acc[p, block, rows, :] = a + jnp.where(first, grad[p], 0.0)
        acc[p, block + 1, rows, :] = b + jnp.where(first, 0.0, grad[p])


def gradients(cur, amps, probe, tabs, pos, slots, scale=None):
    forward, backward = tabs
    pr, pi = probe[0], probe[1]
    pairs = []
    for s in slots:
        a, b = cut(cur, *corner_of(pos, s))
        pairs.append((pr * a - pi * b, pr * b + pi * a))
    waves = left(forward, right(backward, pairs))
    shrunk = []
    for k, ((a, b), s) in enumerate(zip(waves, slots)):
        gain = amps[s] * lax.rsqrt(a * a + b * b + smoothing) - 1.0
        if scale is not None:
            gain = gain * scale[k]
        shrunk.append((a * gain, b * gain))
    backs = right(forward, left(backward, shrunk))
    return [(pr * a + pi * b, pr * b - pi * a) for a, b in backs]


def corner_of(pos, s):
    return pos[0, 0, 0, s] + BORDER, pos[0, 0, 1, s] + 128


def within(start, margin):
    return jnp.logical_and(start >= margin, start <= TILE - PROBE - margin)


def rows_within(pos, s, margin):
    return within(pos[0, 0, 0, s], margin)


def columns_within(pos, s, margin):
    return within(pos[0, 0, 1, s], margin)


def listed_slots(amount, todo, pos, cur, acc, amps, probe, tabs):
    def some(start, size):
        at = [start + k for k in range(size)]
        slots = [jnp.where(j < amount, todo[j], 0) for j in at]
        scale = [jnp.where(j < amount, 1.0, 0.0) for j in at]
        grads = gradients(cur, amps, probe, tabs, pos, slots, scale)
        grads = [turned(grad, pos, s) for grad, s in zip(grads, slots)]
        for grad, s in zip(grads, slots):
            place(acc, grad, pos, s)

    def body(i, carry):
        some(i * GROUP, GROUP)
        return carry

    full = lax.div(amount + 1, GROUP)
    lax.fori_loop(0, full, body, 0)
    rest = amount - full * GROUP
    for least, size in ((1, 2), (3, 4), (5, 6)):

        @pl.when(jnp.logical_and(rest >= least, rest <= size))
        def _():
            some(full * GROUP, size)


def step_of(probe):
    return step_gain / (jnp.max(probe[0] * probe[0] + probe[1] * probe[1]) + 1e-06)


def neighbours():
    rows, cols = lax.axis_size("row"), lax.axis_size("col")
    row, col = lax.axis_index("row"), lax.axis_index("col")
    out = []
    for dr, dc in DIRS:
        there = None
        for cond in (
            [row > 0] if dr < 0 else [row < rows - 1] if dr > 0 else []
        ) + ([col > 0] if dc < 0 else [col < cols - 1] if dc > 0 else []):
            there = cond if there is None else jnp.logical_and(there, cond)
        out.append((there, (row + dr, col + dc)))
    return out


def greet(near):
    barrier = pltpu.get_barrier_semaphore()
    for there, where in near:
        @pl.when(there)
        def _():
            pl.semaphore_signal(barrier, inc=1, device_id=where, device_id_type=MESH)


def greeted(near):
    total = 0
    for there, _ in near:
        total = total + there.astype(jnp.int32)
    pl.semaphore_wait(pltpu.get_barrier_semaphore(), total)


def remote(k, near, source, target, send, recv, n):
    return pltpu.make_async_remote_copy(
        src_ref=source,
        dst_ref=target,
        send_sem=send.at[n],
        recv_sem=recv.at[n],
        device_id=near[k][1],
        device_id_type=MESH,
    )


class Post:
    def __init__(self, near, send, recv):
        self.near, self.send, self.recv = near, send, recv
        self.count, self.waits = 0, []

    def pair(self, k, outs, intos):
        for i, way in enumerate((k, OPP[k])):
            n = self.count + i
            @pl.when(self.near[way][0])
            def _(i=i, way=way, n=n):
                remote(way, self.near, outs[i], intos[1 - i], self.send, self.recv, n).start()

        def wait(base=self.count):
            for i, way in enumerate((k, OPP[k])):
                @pl.when(self.near[way][0])
                def _(i=i, way=way):
                    remote(way, self.near, outs[i], intos[i], self.send, self.recv, base + i).wait_send()
                    remote(way, self.near, outs[i], intos[i], self.send, self.recv, base + 1 - i).wait_recv()

        self.count += 2
        return wait


def groups_before():
    cols, col = lax.axis_size("col"), lax.axis_index("col")
    late = jnp.logical_or(col == cols // 2 - 1, col == cols // 2).astype(jnp.int32)
    return 1 + late, late


def pack(pieces, start):
    lane = lanes(pieces[0].shape[0])
    out = None
    for q, piece in enumerate(pieces):
        turn = (32 * q - start) % 128
        turned = pltpu.roll(piece, turn, 1) if turn else piece
        out = turned if out is None else jnp.where(lane >= 32 * q, turned, out)
    return out


def unpack(value, start):
    turns = [(start - 32 * q) % 128 for q in range(4)]
    return [pltpu.roll(value, turn, 1) if turn else value for turn in turns]


def pack_two(value):
    half = value.shape[0] // 2
    lane = lanes(half)
    middle = jnp.logical_and(lane >= 32, lane < 96)
    return jnp.where(middle, pltpu.roll(value[half:], 64, 1), value[:half])


def unpack_two(value):
    return jnp.concatenate([value, pltpu.roll(value, 64, 1)], 0)


def seam(a, b):
    return jnp.where(lanes(a.shape[0]) >= 96, a, b)


def present(near, k, value):
    return jnp.where(near[k][0], value, 0.0)


LATE = 8


def second_rule(pos, s):
    early = GROUP * groups_before()[1]
    done = jnp.logical_and(
        rows_within(pos, s, BORDER), jnp.logical_or(s >= early, columns_within(pos, s, BORDER))
    )
    inner = jnp.logical_and(rows_within(pos, s, 0), columns_within(pos, s, 0))
    return done, jnp.logical_and(inner, jnp.logical_not(done))


def inside(pos, s):
    return jnp.logical_and(rows_within(pos, s, 0), columns_within(pos, s, 0))


def early_order(pos, early, ahead, behind, follow, follow_other):
    seen, taken = jnp.int32(0), []
    for s in range(PMAX):
        own = inside(pos, s)
        taken.append((own, jnp.logical_and(own, seen < early)))
        seen = seen + own.astype(jnp.int32)
    last = jnp.int32(PMAX)
    follow[PMAX], follow_other[PMAX] = last, last
    coming, other = last, last
    for s in range(PMAX - 1, -1, -1):
        coming, other = jnp.where(taken[s][0], s, coming), jnp.where(taken[s][1], other, s)
        follow[s], follow_other[s] = coming, other
    for k in range(PMAX):
        ahead[k], behind[k] = jnp.minimum(coming, PMAX - 1), jnp.minimum(other, PMAX - 1)
        coming = follow[jnp.minimum(coming + 1, PMAX)]
        other = follow_other[jnp.minimum(other + 1, PMAX)]

    def slot_at(k):
        return jnp.where(k < early, ahead[k], behind[jnp.maximum(k - early, 0)])

    return slot_at


def keep_gradients(grads, cur, amps, probe, tabs, pos, slot_at=lambda k: k):
    def body(i, carry):
        places = [i * GROUP + k for k in range(GROUP)]
        slots = [slot_at(k) for k in places]
        for k, s, grad in zip(places, slots, gradients(cur, amps, probe, tabs, pos, slots)):
            grads[k, 0], grads[k, 1] = turned(grad, pos, s)
        return carry

    return body


def halo_kernel(
    pos_far, obj, amps_far, probe_far, t0_far, t1_far, cur, acc, grads, amps, probe, t0, t1, hv, hc, hd, sc, sd, pos,
    ahead, behind, follow, follow_other, send, recv, sems
):
    near = neighbours()
    greet(near)
    tile_at = [
        pltpu.make_async_copy(
            obj.at[:, :, pl.ds(128 * j, 128)], cur.at[:, j + 1, pl.ds(BORDER, TILE), :], sems.at[j]
        )
        for j in range(4)
    ]
    others = [
        pltpu.make_async_copy(there, here, sems.at[4 + n])
        for n, (there, here) in enumerate(
            ((probe_far, probe), (t0_far, t0), (t1_far, t1), (amps_far, amps), (pos_far, pos))
        )
    ]
    for copy in [tile_at[j] for j in (0, 3, 1, 2)] + others:
        copy.start()
    zeros = jnp.zeros((2, BLOCKS, BORDER, 128), f32)
    cur[:, :, 0:BORDER, :] = zeros
    cur[:, :, BORDER + TILE :, :] = zeros
    cur[:, 0] = jnp.zeros((2, ROWS, 128), f32)
    cur[:, 5] = jnp.zeros((2, ROWS, 128), f32)
    acc[...] = jnp.zeros_like(acc)
    for side in range(2):
        tile_at[3 * side].wait()
        block, start = 1 + 3 * side, 96 * side
        for p in range(2):
            sc[side, p] = pack(
                [cur[p, block, BORDER + 128 * q : BORDER + 128 * q + 128, :] for q in range(4)], start
            )
    greeted(near)
    post = Post(near, send, recv)
    sideways = post.pair(2, [sc.at[0], sc.at[1]], [hc.at[0], hc.at[1]])
    waits = [post.pair(0, [obj.at[:, pl.ds(0, 32), :], obj.at[:, pl.ds(TILE - 32, 32), :]], [hv.at[0], hv.at[1]])]
    for copy in [tile_at[1], tile_at[2]] + others:
        copy.wait()
    before, _ = groups_before()
    slot_at = early_order(pos, GROUP * before, ahead, behind, follow, follow_other)
    body = keep_gradients(grads, cur, amps, probe, (t0, t1), pos, slot_at)
    lax.fori_loop(0, before, body, 0)
    sideways()
    for p in range(2):
        for side in range(2):
            for q, piece in enumerate(unpack(hc[side, p], 96 - 96 * side)):
                at = BORDER + 128 * q
                cur[p, 5 * side, at : at + 128, :] = present(near, 2 + side, piece)
        for ud in range(2):
            rows = pl.ds(BORDER + (TILE - BORDER) * ud, BORDER)
            sd[ud, p] = pack_two(seam(cur[p, 0, rows, :], cur[p, 5, rows, :]))
    waits.append(post.pair(0, [sd.at[0], sd.at[1]], [hd.at[0], hd.at[1]]))
    lax.fori_loop(before, PMAX // GROUP, body, 0)
    for wait in waits:
        wait()
    for p in range(2):
        for k in range(2):
            base = (BORDER + TILE) * k
            for j in range(4):
                cur[p, j + 1, base : base + 32, :] = present(near, k, hv[k, p, :, 128 * j : 128 * j + 128])
            beside = present(near, k, unpack_two(hd[k, p]))
            for side in range(2):
                cur[p, 5 * side, base : base + 32, :] = beside


def first_kernel(count, pos, acc_in, cur, grads, amps, probe, t0, t1, acc, todo):
    del acc_in
    early = GROUP * groups_before()[0]

    def sort(s, carry):
        amount, seen, others = carry
        own = inside(pos, s)
        taken = jnp.logical_and(own, seen < early)
        k = jnp.where(taken, seen, early + others)
        done = jnp.logical_or(taken, jnp.logical_and(rows_within(pos, s, 0), k < PMAX))

        @pl.when(done)
        def _():
            place(acc, (grads[k, 0], grads[k, 1]), pos, s)

        @pl.when(jnp.logical_not(done))
        def _():
            todo[amount] = s

        return (
            amount + jnp.where(done, 0, 1),
            seen + jnp.where(own, 1, 0),
            others + jnp.where(taken, 0, 1),
        )

    zero = jnp.int32(0)
    amount, _, _ = lax.fori_loop(0, count[0, 0], sort, (zero, zero, zero))
    listed_slots(amount, todo, pos, cur, acc, amps, probe, (t0, t1))


def side_sums(near, rc, rm, side, p):
    for rows, value in (
        (pl.ds(0, 64), rc[side, 0, p]),
        (pl.ds(64, TILE - 64), rm[side, p]),
        (pl.ds(TILE, 64), rc[side, 1, p]),
    ):
        yield rows, present(near, 2 + side, unpack_two(value))


def strip_kernel(
    pos, acc, cur_in, amps, probe, t0, t1, rate, grads, cur, sums, rv, rs, rc, rm, sv, ss, sc, sm, send, recv
):
    near = neighbours()
    greet(near)
    for p in range(2):
        for side in range(2):
            for ud in range(2):
                rows = pl.ds(TILE * ud, 64)
                sc[side, ud, p] = pack_two(seam(acc[p, 4 * side, rows, :], acc[p, 4 * side + 1, rows, :]))
    greeted(near)
    post = Post(near, send, recv)
    corners = post.pair(2, [sc.at[0], sc.at[1]], [rc.at[0], rc.at[1]])
    for p in range(2):
        for side in range(2):
            sm[side, p] = pack_two(seam(acc[p, 4 * side, 64:TILE, :], acc[p, 4 * side + 1, 64:TILE, :]))
    middle = post.pair(2, [sm.at[0], sm.at[1]], [rm.at[0], rm.at[1]])
    waits = [
        post.pair(
            0,
            [acc.at[:, pl.ds(2, 2), pl.ds(TILE * ud, 64), :] for ud in range(2)],
            [rv.at[ud, :, pl.ds(1, 2)] for ud in range(2)],
        )
    ]
    step = step_of(probe)
    rate[...] = jnp.full(rate.shape, step, f32)
    cur[...] = cur_in[...] + step * acc[...]
    corners()
    lane = lanes(64)
    for p in range(2):
        for ud in range(2):
            rows = pl.ds(TILE * ud, 64)
            west = present(near, 2, unpack_two(rc[0, ud, p]))
            east = present(near, 3, unpack_two(rc[1, ud, p]))
            sv[ud, p, 0] = acc[p, 1, rows, :] + jnp.where(lane < 32, west, 0.0)
            sv[ud, p, 1] = acc[p, 4, rows, :] + jnp.where(lane >= 96, east, 0.0)
            ss[ud, p] = pack_two(seam(acc[p, 0, rows, :] + west, acc[p, 5, rows, :] + east))
    for n, block in ((0, 0), (1, 3)):
        waits.append(
            post.pair(0, [sv.at[ud, :, n] for ud in range(2)], [rv.at[ud, :, block] for ud in range(2)])
        )
    waits.append(post.pair(0, [ss.at[0], ss.at[1]], [rs.at[0], rs.at[1]]))
    for k in range(2):
        outside = pl.ds((BORDER + TILE) * k, BORDER)
        cur[:, :, outside, :] = present(near, k, cur[:, :, outside, :])
        cur[:, 5 * k] = present(near, 2 + k, cur[:, 5 * k])
    body = keep_gradients(grads, cur, amps, probe, (t0, t1), pos)
    _, before = groups_before()
    lax.fori_loop(0, before, body, 0)
    middle()
    for p in range(2):
        for side in range(2):
            for rows, value in side_sums(near, rc, rm, side, p):
                lane = lanes(value.shape[0])
                for block, mine in ((4 * side, lane >= 96), (4 * side + 1, lane < 32)):
                    cur[p, block, rows, :] += step * jnp.where(mine, value, 0.0)
        for k in range(2):
            outside = pl.ds((BORDER + TILE) * k, BORDER)
            for block in (1, 4):
                cur[p, block, outside, :] = present(near, k, cur[p, block, outside, :])
                cur[p, 5 * (block // 4), outside, :] = present(near, k, cur[p, 5 * (block // 4), outside, :])
    lax.fori_loop(before, PMAX // GROUP, body, 0)
    sums[:, 1:5] = acc[:, 1:5]
    for p in range(2):
        for side in range(2):
            for rows, value in side_sums(near, rc, rm, side, p):
                lane = lanes(value.shape[0])
                sums[p, 1 + 3 * side, rows, :] += jnp.where(lane >= 96 if side else lane < 32, value, 0.0)
    for k in range(2):
        sums[:, 1:5, pl.ds((BORDER + TILE) * k, BORDER), :] = jnp.zeros((2, 4, BORDER, 128), f32)
        sums[:, 5 * k] = jnp.zeros((2, ROWS, 128), f32)
    for wait in waits:
        wait()


def second_kernel(
    count, pos, acc_in, cur_in, rv, rs, rate, grads, amps, probe, t0, t1, acc, cur, todo
):
    near = neighbours()
    step = rate[0:1, :]
    del acc_in, cur_in
    lane = lanes(64)
    for p in range(2):
        for ud in range(2):
            rows = pl.ds(TILE * ud, 64)
            inner, at = pl.ds(BORDER + (TILE - 32) * ud, 32), slice(32 - 32 * ud, 64 - 32 * ud)
            for j in range(4):
                value = present(near, ud, rv[ud, p, j])
                cur[p, j + 1, rows, :] += step * value
                acc[p, j + 1, inner, :] += value[at]
            value = step * present(near, ud, unpack_two(rs[ud, p]))
            for side, mine in ((0, lane >= 96), (1, lane < 32)):
                mine = jnp.logical_and(mine, near[2 + side][0])
                cur[p, 5 * side, rows, :] += jnp.where(mine, value, 0.0)
    def sort(s, carry):
        amount, held = carry
        done, hold = second_rule(pos, s)
        hold = jnp.logical_and(hold, held < LATE)

        @pl.when(done)
        def _():
            place(acc, (grads[s, 0], grads[s, 1]), pos, s)

        now = jnp.logical_not(jnp.logical_or(done, hold))

        @pl.when(now)
        def _():
            todo[amount] = s

        return amount + jnp.where(now, 1, 0), held + jnp.where(hold, 1, 0)

    amount, _ = lax.fori_loop(0, count[0, 0], sort, (jnp.int32(0), jnp.int32(0)))
    listed_slots(amount, todo, pos, cur, acc, amps, probe, (t0, t1))


def fold_kernel(
    count, pos, acc, cur, amps, probe, t0, t1, grads, gv, gc, gd, sc, sd, sv, late, follow, send, recv
):
    near = neighbours()
    greet(near)
    for p in range(2):
        for side in range(2):
            for ud in range(2):
                base = (BORDER + TILE) * ud
                sd[side, ud, p] = pack(
                    [acc[p, 5 * side, base + 8 * q : base + 8 * q + 8, :] for q in range(4)], 96 - 96 * side
                )
    greeted(near)
    post = Post(near, send, recv)
    corners = post.pair(2, [sd.at[0], sd.at[1]], [gd.at[0], gd.at[1]])
    waits = [
        post.pair(
            0,
            [acc.at[:, pl.ds(2, 2), pl.ds((BORDER + TILE) * ud, BORDER), :] for ud in range(2)],
            [gv.at[ud, :, pl.ds(1, 2)] for ud in range(2)],
        )
    ]
    for p in range(2):
        for side in range(2):
            sc[side, p] = pack(
                [acc[p, 5 * side, BORDER + 128 * q : BORDER + 128 * q + 128, :] for q in range(4)], 96 - 96 * side
            )
    waits.append(post.pair(2, [sc.at[0], sc.at[1]], [gc.at[0], gc.at[1]]))
    corners()
    lane = lanes(BORDER)
    for p in range(2):
        for ud in range(2):
            rows = pl.ds((BORDER + TILE) * ud, BORDER)
            for side in range(2):
                beside = present(near, 2 + side, jnp.concatenate(unpack(gd[side, ud, p], 96 * side), 0))
                mine = lane >= 96 if side else lane < 32
                sv[ud, p, side] = acc[p, 1 + 3 * side, rows, :] + jnp.where(mine, beside, 0.0)
    for side in range(2):
        waits.append(
            post.pair(0, [sv.at[ud, :, side] for ud in range(2)], [gv.at[ud, :, 3 * side] for ud in range(2)])
        )

    coming = jnp.int32(PMAX)
    follow[PMAX] = coming
    for s in range(PMAX - 1, -1, -1):
        hold = jnp.logical_and(s < count[0, 0], second_rule(pos, s)[1])
        coming = jnp.where(hold, s, coming)
        follow[s] = coming
    for k in range(LATE):
        late[k] = coming
        coming = follow[jnp.minimum(coming + 1, PMAX)]

    def body(i, carry):
        slots = [jnp.minimum(late[i * GROUP + k], PMAX - 1) for k in range(GROUP)]
        for k, grad in enumerate(gradients(cur, amps, probe, (t0, t1), pos, slots)):
            grads[i * GROUP + k, 0], grads[i * GROUP + k, 1] = turned(grad, pos, slots[k])
        return carry

    lax.fori_loop(0, LATE // GROUP, body, 0)
    for wait in waits:
        wait()


def last_kernel(count, pos, obj, acc_in, gv, gc, grads, rate, est_out, corr_out, acc, est, sems):
    near = neighbours()
    del acc_in
    step = rate[0:1, :]

    def put(s, held):
        hold = jnp.logical_and(second_rule(pos, s)[1], held < LATE)

        @pl.when(hold)
        def _():
            place(acc, (grads[held, 0], grads[held, 1]), pos, s)

        return held + jnp.where(hold, 1, 0)

    lax.fori_loop(0, count[0, 0], put, jnp.int32(0))
    inner = pl.ds(BORDER, TILE)
    stores = []

    def leave(j):
        out = pl.ds(128 * j, 128)
        acc[:, j + 1, inner, :] = step * acc[:, j + 1, inner, :]
        stores.append(pltpu.make_async_copy(acc.at[:, j + 1, inner, :], corr_out.at[:, :, out], sems.at[j]))
        stores[-1].start()
        est[:, j] = obj[:, :, 128 * j : 128 * j + 128] + acc[:, j + 1, inner, :]
        stores.append(pltpu.make_async_copy(est.at[:, j], est_out.at[:, :, out], sems.at[4 + j]))
        stores[-1].start()

    for j in (1, 2, 0, 3):
        for p in range(2):
            for ud in range(2):
                base = BORDER + (TILE - 32) * ud
                acc[p, j + 1, base : base + 32, :] += present(near, ud, gv[ud, p, j])
        if j in (0, 3):
            side, block, start = j // 3, j + 1, 32 * j

            def mine(rows):
                return lanes(rows) >= 96 if side else lanes(rows) < 32

            for p in range(2):
                for q, piece in enumerate(unpack(gc[side, p], start)):
                    at = BORDER + 128 * q
                    acc[p, block, at : at + 128, :] += jnp.where(mine(128), present(near, 2 + side, piece), 0.0)
        leave(j)
    for store in stores:
        store.wait()


VM = pl.BlockSpec(memory_space=pltpu.VMEM)
SM = pl.BlockSpec(memory_space=pltpu.SMEM)
HBM = pl.BlockSpec(memory_space=pltpu.HBM)


def shape(*dims, dtype=f32):
    return jax.ShapeDtypeStruct(dims, dtype)


def params(limit_mib=14, **kw):
    return pltpu.CompilerParams(vmem_limit_bytes=limit_mib * 2**20, **kw)


def remote_params(which):
    return params(collective_id=which, has_side_effects=True)


def on_device(object_field, probe_field, amplitudes, positions, counts):
    tabs = [jnp.asarray(t) for t in tables()]
    dma = pltpu.SemaphoreType.DMA
    tile = shape(2, BLOCKS, ROWS, 128)
    kept = shape(PMAX, 2, PROBE, PROBE)
    far = [
        pltpu.with_memory_space_constraint(x, pltpu.HBM)
        for x in (positions, object_field, amplitudes, probe_field, *tabs)
    ]
    cur, acc, grads, *shared = pl.pallas_call(
        halo_kernel,
        out_shape=[tile, tile, kept]
        + [jax.ShapeDtypeStruct(x.shape, x.dtype) for x in (amplitudes, probe_field, *tabs)],
        in_specs=[HBM] * 6,
        out_specs=[VM] * 7,
        scratch_shapes=[
            pltpu.VMEM((2, 2, 32, TILE), f32),
            pltpu.VMEM((2, 2, 128, 128), f32),
            pltpu.VMEM((2, 2, 16, 128), f32),
            pltpu.VMEM((2, 2, 128, 128), f32),
            pltpu.VMEM((2, 2, 16, 128), f32),
            pltpu.SMEM((1, 1, 2, PMAX), jnp.int32),
            *[pltpu.SMEM((n,), jnp.int32) for n in (PMAX, PMAX, PMAX + 1, PMAX + 1)],
            dma((8,)),
            dma((8,)),
            dma((9,)),
        ],
        compiler_params=remote_params(0),
        name="halo",
    )(*far)
    acc = pl.pallas_call(
        first_kernel,
        out_shape=tile,
        in_specs=[SM, SM] + [VM] * 7,
        out_specs=VM,
        scratch_shapes=[pltpu.SMEM((PMAX,), jnp.int32)],
        input_output_aliases={2: 0},
        compiler_params=params(),
        name="first",
    )(counts, positions, acc, cur, grads, *shared)
    strips = ((2, 2, 4, 64, 128), (2, 2, 32, 128), (2, 2, 2, 32, 128), (2, 2, 224, 128))
    rate, grads, cur, sums, rv, rs, *_ = pl.pallas_call(
        strip_kernel,
        out_shape=(shape(8, 128), kept, tile, tile) + tuple(shape(*s) for s in strips),
        in_specs=[SM] + [VM] * 6,
        out_specs=[VM] * 8,
        scratch_shapes=[
            pltpu.VMEM((2, 2, 2, 64, 128), f32),
            pltpu.VMEM((2, 2, 32, 128), f32),
            pltpu.VMEM((2, 2, 2, 32, 128), f32),
            pltpu.VMEM((2, 2, 224, 128), f32),
            dma((12,)),
            dma((12,)),
        ],
        compiler_params=remote_params(1),
        name="strips",
    )(positions, acc, cur, *shared)
    acc, cur = pl.pallas_call(
        second_kernel,
        out_shape=(tile, tile),
        in_specs=[SM, SM] + [VM] * 10,
        out_specs=[VM, VM],
        scratch_shapes=[pltpu.SMEM((PMAX,), jnp.int32)],
        input_output_aliases={2: 0, 3: 1},
        compiler_params=params(),
        name="second",
    )(counts, positions, sums, cur, rv, rs, rate, grads, *shared)
    folds = ((2, 2, 4, 32, 128), (2, 2, 128, 128))
    grads, gv, gc = pl.pallas_call(
        fold_kernel,
        out_shape=(shape(LATE, 2, PROBE, PROBE),) + tuple(shape(*s) for s in folds),
        in_specs=[SM, SM] + [VM] * 6,
        out_specs=[VM] * 3,
        scratch_shapes=[
            pltpu.VMEM((2, 2, 2, 8, 128), f32),
            pltpu.VMEM((2, 2, 128, 128), f32),
            pltpu.VMEM((2, 2, 2, 8, 128), f32),
            pltpu.VMEM((2, 2, 2, 32, 128), f32),
            pltpu.SMEM((LATE,), jnp.int32),
            pltpu.SMEM((PMAX + 1,), jnp.int32),
            dma((10,)),
            dma((10,)),
        ],
        compiler_params=remote_params(2),
        name="folds",
    )(counts, positions, acc, cur, *shared)
    return pl.pallas_call(
        last_kernel,
        out_shape=(shape(2, TILE, TILE), shape(2, TILE, TILE), tile),
        in_specs=[SM, SM] + [VM] * 6,
        out_specs=[HBM, HBM, VM],
        scratch_shapes=[pltpu.VMEM((2, 4, TILE, 128), f32), dma((8,))],
        input_output_aliases={3: 2},
        compiler_params=params(),
        name="last",
    )(counts, positions, object_field, acc, gv, gc, grads, rate)[:2]


def solution(mesh):
    placed = (
        P(None, "row", "col"),
        P(),
        P("row", None, "col"),
        P("row", "col", None, None),
        P("row", "col"),
    )
    return jax.shard_map(
        on_device,
        mesh=mesh,
        in_specs=placed,
        out_specs=(P(None, "row", "col"), P(None, "row", "col")),
        check_vma=False,
    )
```
